32 devices in a mesh: groups: 2 (over y), src: 4 (over z), tile: 2 (over x), pix: 2 (over core).
Axes of the slice: x: 2, y: 2, z: 4, core: 2. Of those that a mesh axis runs over, the one named last changes fastest.
Arguments:
- mask: float32 [4, 1024, 1024], P(('groups', 'tile'), ('src', 'pix')), parts along dimension 0, may hold values from -1 to 1
- target: float32 [4, 1024, 1024], P(('groups', 'tile'), ('src', 'pix')), parts along dimension 0, may hold values from 0 to 1
- tile_class: int32 [4], P(('groups', 'tile')), parts along dimension 0, may hold values from 0 to 3
- thresholds: float32 [4], replicated, may hold values from 0.3 to 1.2
- source_pupil: bfloat16 [512, 2048], P('src'), as said below
- source_weight: bfloat16 [512], P('src'), may hold values from 0.125 to 1.25
- source_cell: int32 [512], P('src'), may hold values from 0 to 288
- active_count: int32 [4], replicated, may hold values from 1 to 6, as said below
Outputs:
- intensity: float32 [4, 1024, 1024], P(('groups', 'tile'), ('src', 'pix')), parts along dimension 0
- mask_grad: float32 [4, 1024, 1024], P(('groups', 'tile'), ('src', 'pix')), parts along dimension 0
- source_grad: float32 [1024], P(('groups', 'src')), parts along dimension 0
The draws below stay inside these ranges and needn't reach their ends.
There are 2 independent parts, one for each index of `groups`. The reference program is written for one: setup_inputs(seed, part) draws one part's arguments, and reference() takes and returns one part's arrays. A program takes and returns all parts, laid end to end along the dimension named above; an argument that names none is the same for every part. Nothing has to cross between parts.
Inputs may be any that keep to these rules, and one draw needn't show every extreme that they name: Index d of src has active_count[d] live slots, its first ones; some index has exactly 6. `source_pupil`: each row holds a source point's 32 x 32 pupil samples, real parts then imaginary parts.
All inputs are finite; a program needn't handle non-finite values.
Results may differ from the reference program's by a relative error of at most 0.011.
Values may be sent and summed in bfloat16 or wider, within the bound.
No kernel may reach another device: no remote copies, remote signals or barrier semaphores. Data moves between devices by JAX's collectives and lax.ppermute only.
A program may use at most 64 MiB of HBM per device.

```python
import math
import jax
import jax.numpy as jnp
from jax import lax

N = 1024
K = 32
SG = 17
W = 48
SRC_DEV = 128
SOURCES = 512
MOST = 6
CLASSES = 4
CLIPS = 2
N_SRC = 4


def draw_source_pupil(key, part):
    key = jax.random.fold_in(key, 7)
    length_key, angle_key = jax.random.split(key)
    offsets = jnp.arange(K, dtype=jnp.int32) - K // 2
    inside = offsets[:, None] ** 2 + offsets[None, :] ** 2 <= (3 * K // 8) ** 2
    magnitude = jax.random.uniform(length_key, (SOURCES, K, K), jnp.float32, 0.5, 1.5)
    phase_angle = jax.random.uniform(angle_key, (SOURCES, K, K), jnp.float32, -jnp.pi, jnp.pi)
    magnitude = jnp.where(inside[None], magnitude, 0.0)
    stacked = jnp.stack([magnitude * jnp.cos(phase_angle), magnitude * jnp.sin(phase_angle)], 1)
    return stacked.reshape(SOURCES, 2 * K * K).astype(jnp.bfloat16)


def draw_active_count(key, part):
    key = jax.random.fold_in(key, 11)
    count_key, busy_key = jax.random.split(key)
    counts = jax.random.randint(count_key, (N_SRC,), 1, MOST // 2 + 1, dtype=jnp.int32)
    busiest = jax.random.randint(busy_key, (), 0, N_SRC, dtype=jnp.int32)
    return jnp.where(jnp.arange(N_SRC, dtype=jnp.int32) == busiest, MOST, counts).astype(jnp.int32)


def set_ends(result, rng, smallest, high):
    longest = result.shape.index(max(result.shape))
    spots = []
    for shift in (0, 1):
        where = [jax.random.randint(jax.random.fold_in(rng, axis), (), 0, length) for axis, length in enumerate(result.shape)]
        where[longest] = (where[longest] + shift) % result.shape[longest]
        spots.append(tuple(where))
    return result.at[spots[0]].set(smallest).at[spots[1]].set(high)


def block_scale(key, shape, cuts, low, largest):
    gain, own = 1.0, jax.random.fold_in(key, 6)
    for position, blocks in cuts:
        heights = jnp.exp(jax.random.uniform(jax.random.fold_in(own, position), (blocks,), jnp.float32, low / len(cuts), largest / len(cuts)))
        gain = gain * jnp.repeat(heights, shape[position] // blocks).reshape([-1 if axis == position else 1 for axis in range(len(shape))])
    return gain


def setup_inputs(seed: int = 0, part: int = 0) -> dict:
    arg_keys = jax.random.split(jax.random.key(seed), 9)
    part_keys = jax.random.split(jax.random.fold_in(arg_keys[8], part), 9)
    return {
        "mask": jnp.clip(jax.random.uniform(part_keys[0], (CLIPS, N, N), jnp.float32, -1.0, 1.0) * block_scale(part_keys[0], (CLIPS, N, N), ((0, 2), (1, 8)), -0.4, 0.0), -1.0, 1.0),
        "target": jnp.clip(1.0 * jax.random.uniform(part_keys[1], (CLIPS, N, N), jnp.float32) ** block_scale(part_keys[1], (CLIPS, N, N), ((0, 2), (1, 8)), -0.2, 0.2), 0.0, 1.0),
        "tile_class": jax.random.randint(part_keys[2], (CLIPS,), 0, CLASSES).astype(jnp.int32),
        "thresholds": jnp.clip(jax.random.uniform(arg_keys[3], (CLASSES,), jnp.float32, 0.3, 1.2), 0.3, 1.2),
        "source_pupil": draw_source_pupil(jax.random.fold_in(arg_keys[8], 71), part),
        "source_weight": jnp.clip(jnp.exp(math.log(1.25) - 2.3025851 * jax.random.uniform(arg_keys[5], (SOURCES,), jnp.float32) ** block_scale(arg_keys[5], (SOURCES,), ((0, 4),), -0.2, 0.2)), 0.125, 1.25).astype(jnp.bfloat16),
        "source_cell": set_ends(jax.random.randint(arg_keys[6], (SOURCES,), 0, SG * SG), jax.random.fold_in(arg_keys[6], 1), 0, (SG * SG) - 1).astype(jnp.int32),
        "active_count": draw_active_count(jax.random.fold_in(arg_keys[8], 71), part),
    }


steep = 4.0


def phase_pair(freqs, places, period):
    turns = (freqs[:, None] * places[None, :]) % period
    angle = (2.0 * jnp.pi / period) * turns.astype(jnp.float32)
    return jnp.cos(angle), jnp.sin(angle)


def mix_table(back_cos, back_sin):
    upper = jnp.concatenate([back_cos, back_sin], 1)
    lower = jnp.concatenate([-back_sin, back_cos], 1)
    return jnp.concatenate([upper, lower], 0).astype(jnp.bfloat16)


def left_of(row_ids, period):
    narrow = jnp.arange(K, dtype=jnp.int32) - K // 2
    cos_part, sin_part = phase_pair(row_ids, narrow, period)
    upper = jnp.concatenate([cos_part, -sin_part], 1)
    lower = jnp.concatenate([sin_part, cos_part], 1)
    return jnp.concatenate([upper, lower], 0).astype(jnp.bfloat16)


def make_stack(spectrum, pupil, row_shift, col_shift, back_mix, period):
    window = lax.dynamic_slice(spectrum, (jnp.int32(0), row_shift, col_shift), (2, K, K))
    wave_re = (pupil[0] * window[0] - pupil[1] * window[1]).astype(jnp.bfloat16)
    wave_im = (pupil[0] * window[1] + pupil[1] * window[0]).astype(jnp.bfloat16)
    joined = jnp.dot(jnp.concatenate([wave_re, wave_im], 1), back_mix, preferred_element_type=jnp.float32)
    return jnp.concatenate([joined[:, :period], joined[:, period:]], 0).astype(jnp.bfloat16)


def field_of(left_table, stacked):
    raw = jnp.dot(left_table, stacked, preferred_element_type=jnp.float32) * (1.0 / K)
    return lax.optimization_barrier(raw.astype(jnp.bfloat16)).astype(jnp.float32)


def spread_into(grad_spec, grad_stack, pupil, row_shift, col_shift, back_cos, back_sin):
    exact = lax.Precision.HIGHEST
    grad_re = grad_stack[:K]
    grad_im = grad_stack[K:]
    wave_re = jnp.dot(grad_re, back_cos.T, precision=exact) + jnp.dot(grad_im, back_sin.T, precision=exact)
    wave_im = jnp.dot(grad_im, back_cos.T, precision=exact) - jnp.dot(grad_re, back_sin.T, precision=exact)
    spot = (jnp.int32(0), row_shift, col_shift)
    before = lax.dynamic_slice(grad_spec, spot, (2, K, K))
    after = before + jnp.stack([pupil[0] * wave_re + pupil[1] * wave_im, pupil[0] * wave_im - pupil[1] * wave_re])
    return lax.dynamic_update_slice(grad_spec, after, spot)


def reference(mask, target, tile_class, thresholds, source_pupil, source_weight, source_cell, active_count):
    exact = lax.Precision.HIGHEST
    pixels = jnp.arange(N, dtype=jnp.int32)
    wide = jnp.arange(W, dtype=jnp.int32) - W // 2
    narrow = jnp.arange(K, dtype=jnp.int32) - K // 2
    spec_cos, spec_sin = phase_pair(wide, pixels, N)
    back_cos, back_sin = phase_pair(narrow, pixels, N)
    back_mix = mix_table(back_cos, back_sin)
    left_table = left_of(pixels, N)
    counts = active_count.astype(jnp.int32)
    ends = jnp.cumsum(counts).astype(jnp.int32)
    starts = (ends - counts).astype(jnp.int32)
    total = ends[-1]

    def source_data(number):
        owner = jnp.sum((ends <= number).astype(jnp.int32)).astype(jnp.int32)
        flat_index = (owner * SRC_DEV + number - starts[owner]).astype(jnp.int32)
        pupil = source_pupil[flat_index].reshape(2, K, K).astype(jnp.float32)
        weight = source_weight[flat_index].astype(jnp.float32)
        cell_id = source_cell[flat_index]
        return flat_index, pupil, weight, cell_id // SG, cell_id % SG

    def one_clip(inputs):
        tile_rows, aim_rows, tile_kind = inputs
        part_re = jnp.dot(tile_rows, spec_cos.T, precision=exact)
        part_im = -jnp.dot(tile_rows, spec_sin.T, precision=exact)
        spectrum = jnp.stack([
            jnp.dot(spec_cos, part_re, precision=exact) + jnp.dot(spec_sin, part_im, precision=exact),
            jnp.dot(spec_cos, part_im, precision=exact) - jnp.dot(spec_sin, part_re, precision=exact)]) / N

        def forward(number, total_power):
            flat_index, pupil, weight, row_shift, col_shift = source_data(number)
            stacked = make_stack(spectrum, pupil, row_shift, col_shift, back_mix, N)
            field_now = field_of(left_table, stacked)
            return total_power + weight * (field_now[:N] ** 2 + field_now[N:] ** 2)

        intensity = lax.fori_loop(0, total, forward, jnp.zeros((N, N), jnp.float32))
        threshold = jnp.sum(jnp.where(jnp.arange(CLASSES, dtype=jnp.int32) == tile_kind, thresholds, 0.0))
        resist = jax.nn.sigmoid(steep * (intensity - threshold))
        slope = (2.0 * (resist - aim_rows) * steep * resist * (1.0 - resist)).astype(jnp.bfloat16)
        slope_now = slope.astype(jnp.float32)

        def backward(number, state):
            grad_spec, grad_all = state
            flat_index, pupil, weight, row_shift, col_shift = source_data(number)
            stacked = make_stack(spectrum, pupil, row_shift, col_shift, back_mix, N)
            field_now = field_of(left_table, stacked)
            power_now = field_now[:N] ** 2 + field_now[N:] ** 2
            grad_all = grad_all.at[flat_index].add(jnp.sum(slope_now * power_now))
            scaled = (2.0 / K) * weight * slope_now
            pull = (jnp.concatenate([scaled, scaled], 0) * field_now).astype(jnp.bfloat16)
            grad_stack = lax.dot_general(left_table, pull, (((0,), (0,)), ((), ())), preferred_element_type=jnp.float32)
            grad_spec = spread_into(grad_spec, grad_stack, pupil, row_shift, col_shift, back_cos, back_sin)
            return grad_spec, grad_all

        grad_spec, grad_all = lax.fori_loop(0, total, backward, (jnp.zeros((2, W, W), jnp.float32), jnp.zeros((SOURCES,), jnp.float32)))
        z_one = jnp.dot(grad_spec[0], spec_cos, precision=exact) - jnp.dot(grad_spec[1], spec_sin, precision=exact)
        z_two = -jnp.dot(grad_spec[0], spec_sin, precision=exact) - jnp.dot(grad_spec[1], spec_cos, precision=exact)
        mask_grad = (jnp.dot(spec_cos.T, z_one, precision=exact) + jnp.dot(spec_sin.T, z_two, precision=exact)) / N
        return intensity, mask_grad, grad_all

    intensity, mask_grad, grads = lax.map(one_clip, (mask, target, tile_class))
    return intensity, mask_grad, jnp.sum(grads, 0) * (1.0 / (N * K))
```

```python
import functools
import math

import jax
import jax.numpy as jnp
import ml_dtypes
import numpy as np
from jax import lax
from jax.experimental import pallas as pl
from jax.experimental.pallas import tpu as pltpu
from jax.sharding import PartitionSpec as P

K = 32
SG = 17
W = 48
MOST = 6
CLASSES = 4
STEEP = 4.0

M = 64
LANES = 128
GROUP = 3
PUPIL_ROWS = MOST * W + 16

f32 = jnp.float32
bf16 = jnp.bfloat16


def split_np(table):
    table = np.asarray(table, np.float32)
    high = table.astype(ml_dtypes.bfloat16)
    low = (table - high.astype(np.float32)).astype(ml_dtypes.bfloat16)
    return high, low


def halves(left, right):
    out = np.zeros((left.shape[0], LANES))
    out[:, : left.shape[1]] = left
    out[:, M : M + right.shape[1]] = right
    return out


@functools.lru_cache(maxsize=None)
def tables(period, span):
    blocks = period // span
    freqs = np.arange(W) - W // 2
    pixels = np.arange(period)
    wide = 2.0 * np.pi / period * ((freqs[:, None] * pixels[None, :]) % period)
    wide_cos, wide_sin = np.cos(wide), np.sin(wide)
    coarse = 2.0 * np.pi / M * ((freqs[:, None] * np.arange(M)[None, :]) % M)
    coarse_cos, coarse_sin = np.cos(coarse), np.sin(coarse)
    high, low = split_np(halves(wide_cos.T, -wide_sin.T))
    spec_cols = np.concatenate([high, low], 1)
    rows = np.concatenate(
        [wide_cos.reshape(W, blocks, span), wide_sin.reshape(W, blocks, span)], 2
    ).transpose(1, 0, 2)
    high, low = split_np(rows / period)
    spec_rows = np.concatenate([high, low], 1)
    lift = np.concatenate(
        [
            np.pad(np.concatenate([coarse_cos, coarse_sin], 1), ((0, M - W), (0, 0))),
            np.pad(np.concatenate([-coarse_sin, coarse_cos], 1), ((0, M - W), (0, 0))),
        ],
        0,
    )
    high, low = split_np(lift)
    lift_cols = np.concatenate([high, low], 0)
    left = np.concatenate([coarse_cos.T, coarse_sin.T], 0) / K
    high, low = split_np(left)
    lift_rows = np.concatenate([high, low, high], 1)
    orders = np.arange(-(M // 2 - 1), M // 2)
    places = pixels[:, None] * (M / period) - np.arange(M)[None, :]
    inter = np.cos(2.0 * np.pi / M * places[:, :, None] * orders).sum(-1) / M
    high, low = split_np(inter)
    fine_cols = np.concatenate([high.T, low.T, high.T, low.T], 0)
    fold_cols = np.concatenate([high, low], 1)
    fine_rows = np.concatenate([high, low, high, low], 1).reshape(blocks, span, 4 * M)
    high_t = high.reshape(blocks, span, M).transpose(0, 2, 1)
    low_t = low.reshape(blocks, span, M).transpose(0, 2, 1)
    fold_rows = np.concatenate([high_t, low_t, high_t], 2)
    high, low = split_np(np.concatenate([coarse_cos, coarse_sin], 0))
    drop_rows = np.concatenate([high, low, high], 1)
    drop = np.concatenate(
        [halves(coarse_cos.T, -coarse_sin.T), halves(coarse_sin.T, coarse_cos.T)], 0
    )
    high, low = split_np(drop)
    drop_cols = np.concatenate([high, low, high], 0)
    rows = np.concatenate(
        [
            wide_cos.reshape(W, blocks, span).transpose(1, 2, 0),
            wide_sin.reshape(W, blocks, span).transpose(1, 2, 0),
        ],
        2,
    )
    high, low = split_np(rows / period)
    grad_rows = np.concatenate([high, low, high], 2)
    high, low = split_np(
        np.concatenate(
            [
                np.pad(wide_cos, ((0, M - W), (0, 0))),
                np.pad(wide_sin, ((0, M - W), (0, 0))),
            ],
            0,
        )
    )
    grad_cols = np.concatenate([high, low], 0)
    return dict(
        spec_cols=spec_cols,
        spec_rows=spec_rows,
        lift_cols=lift_cols,
        lift_rows=lift_rows,
        fine_cols=fine_cols,
        fold_cols=fold_cols,
        fine_rows=fine_rows,
        fold_rows=fold_rows,
        drop_rows=drop_rows,
        drop_cols=drop_cols,
        grad_rows=grad_rows,
        grad_cols=grad_cols,
    )


def dot(left, right):
    return jnp.dot(left, right, preferred_element_type=f32)


def split(value):
    high = value.astype(bf16)
    return high, (value - high.astype(f32)).astype(bf16)


def lane_of(shape):
    return lax.broadcasted_iota(jnp.int32, shape, len(shape) - 1)


def swap(value):
    return pltpu.roll(value, M, 1)


def signs(rows, low, high):
    return jnp.where(lane_of((rows, LANES)) < M, f32(low), f32(high))


def my_block():
    return lax.axis_index("src") * lax.axis_size("pix") + lax.axis_index("pix")


def spectrum_kernel(
    mask_ref, pupil_ref, weight_ref, cell_ref, active_ref, cols_ref, rows_ref,
    part_ref, placed_ref, lined, spread,
):
    src = lax.axis_index("src")
    active = active_ref[src]
    raw = pupil_ref[...].astype(f32)[:8]
    for piece in range(16):
        lined[pl.ds(piece, 8, stride=16), :] = raw[:, piece * LANES : (piece + 1) * LANES]
    spread[...] = jnp.zeros_like(spread)
    lane = lane_of((8, LANES))
    for slot in range(MOST):
        cell = cell_ref[slot]
        row, col = lax.div(cell, SG), lax.rem(cell, SG)
        live = slot < active
        real = lined[pl.ds(slot * 16, 8), :]
        imag = lined[pl.ds(slot * 16 + 8, 8), :]
        in_real = (lane >= col) & (lane < col + K) & live
        in_imag = (lane >= col + M) & (lane < col + M + K) & live
        for turn in range(4):
            shift = LANES - K * turn
            moved_real = pltpu.roll(real, lax.rem(col + shift, LANES), 1)
            moved_imag = pltpu.roll(imag, lax.rem(col + shift + M, LANES), 1)
            placed = jnp.where(in_real, moved_real, jnp.where(in_imag, moved_imag, 0.0))
            spread[pl.ds(slot * W + row + turn, 8, stride=4), :] = placed
    placed_ref[: MOST * W] = spread[...].astype(bf16)
    weights = jnp.broadcast_to(weight_ref[...].astype(f32).reshape(1, -1), (16, weight_ref.shape[-1]))
    diagonal = lax.broadcasted_iota(jnp.int32, weights.shape, 0) == lane_of(weights.shape)
    column = jnp.sum(jnp.where(diagonal, weights, 0.0), 1, keepdims=True)
    placed_ref[MOST * W :] = jnp.broadcast_to(column, (16, LANES)).astype(bf16)
    high, low = split(mask_ref[0])
    both = dot(high, cols_ref[...])
    part = both[:, :LANES] + both[:, LANES:] + dot(low, cols_ref[:, :LANES])
    turned = swap(part) * signs(part.shape[0], 1.0, -1.0)
    high, low = split(jnp.concatenate([part, turned], 0))
    table = rows_ref[my_block()]
    product = dot(table, jnp.concatenate([high, low], 1))
    part_ref[...] = product[:W, :LANES] + product[:W, LANES:] + product[W:, :LANES]


def spread_pupil(placed):
    other = swap(placed)
    low = lane_of(placed.shape) < M
    return jnp.where(low, placed, other), jnp.where(low, other, placed)


def source_index(part, item, count, src):
    return jnp.bitwise_xor(src, part) if count == 1 else item


def for_groups(pupil_refs, active_ref, body, state):
    src = lax.axis_index("src")
    for part, ref in enumerate(pupil_refs):
        count = ref.shape[0]

        def owners(item, state, part=part, ref=ref, count=count):
            owner = source_index(part, item, count, src)
            groups = lax.div(active_ref[owner] + (GROUP - 1), GROUP)
            return lax.fori_loop(
                0, groups, lambda group, inner: body(inner, ref, item, owner, group), state
            )

        state = owners(0, state) if count == 1 else lax.fori_loop(0, count, owners, state)
    return state


def weight_row(ref, item, slot):
    rows = ref[item, pl.ds(MOST * W, 16), :].astype(f32)
    pick = lax.broadcasted_iota(jnp.int32, rows.shape, 0) == slot
    return jnp.sum(jnp.where(pick, rows, 0.0), 0, keepdims=True)


def image_kernel(counts, *refs):
    n_spec, n_pupil, rows_out = counts
    spec_refs, refs = refs[:n_spec], refs[n_spec:]
    pupil_refs, refs = refs[:n_pupil], refs[n_pupil:]
    (
        target_ref, active_ref, class_ref, thresholds_ref,
        lift_cols, lift_rows, fine_rows, fine_cols, fold_cols, fold_rows,
        intensity_ref, fold_ref, fields_ref,
    ) = refs
    spectrum = sum(ref[...] for ref in spec_refs[1:]) + spec_refs[0][...] if n_spec > 1 else spec_refs[0][...]
    turned = swap(spectrum) * signs(W, -1.0, 1.0)
    many = jnp.concatenate([spectrum] * GROUP, 0)
    many_turned = jnp.concatenate([turned] * GROUP, 0)
    left = lift_rows[...]
    turn = signs(M, -1.0, 1.0)

    def forward(total, ref, item, owner, group):
        start = pl.multiple_of(group * (GROUP * W), 16)
        real, imag = spread_pupil(ref[item, pl.ds(start, GROUP * W), :].astype(f32))
        wave = (real * many + imag * many_turned).astype(bf16)
        high, low = split(dot(jnp.concatenate([wave, wave], 1), lift_cols[...]))
        for slot in range(GROUP):
            here = slice(slot * W, (slot + 1) * W)
            raw = dot(left, jnp.concatenate([high[here], high[here], low[here]], 0))
            field = raw[:M] + turn * swap(raw[M:])
            number = owner * MOST + group * GROUP + slot
            fields_ref[number] = field
            weight = weight_row(ref, item, group * GROUP + slot)
            total = total + weight * (field * field)
        return total

    power = for_groups(pupil_refs, active_ref, forward, jnp.zeros((M, LANES), f32))
    high, low = split(power + swap(power))
    block = my_block()
    half = dot(fine_rows[block], jnp.concatenate([high, high, low, low], 0))
    high, low = split(half)
    intensity = dot(jnp.concatenate([high, low], 1), fine_cols[...])
    intensity_ref[0] = intensity
    kind = class_ref[0]
    threshold = thresholds_ref[0]
    for number in range(1, CLASSES):
        threshold = jnp.where(kind == number, thresholds_ref[number], threshold)
    resist = 1.0 / (1.0 + jnp.exp(-STEEP * (intensity - threshold)))
    slope = (2.0 * STEEP * (resist - target_ref[0]) * resist * (1.0 - resist)).astype(bf16)
    folded = dot(slope, fold_cols[...])
    high, low = split(folded + swap(folded))
    grid = dot(fold_rows[block], jnp.concatenate([high, high, low], 0))
    lane = lane_of((M // 2, LANES))
    fold_ref[: M // 2] = jnp.where(lane < M, grid[: M // 2], grid[M // 2 :])
    fold_ref[M // 2 :] = jnp.zeros((rows_out - M // 2, LANES), f32)

    def weigh(none, ref, item, owner, group):
        for slot in range(GROUP):
            number = owner * MOST + group * GROUP + slot
            field = fields_ref[number]
            fold_ref[pl.ds(M // 2 + number, 1), :] = jnp.sum(grid * (field * field), 0, keepdims=True)
        return none

    for_groups(pupil_refs, active_ref, weigh, 0)


def gradient_kernel(counts, *refs):
    n_fold, n_pupil = counts
    fold_refs, refs = refs[:n_fold], refs[n_fold:]
    pupil_refs, refs = refs[:n_pupil], refs[n_pupil:]
    fields_ref, active_ref, drop_rows, drop_cols, grad_rows, grad_cols, mask_grad_ref = refs
    packed = fold_refs[0][: M // 2]
    for ref in fold_refs[1:]:
        packed = packed + ref[: M // 2]
    other = swap(packed)
    low_half = lane_of(packed.shape) < M
    grid = jnp.concatenate(
        [jnp.where(low_half, packed, other), jnp.where(low_half, other, packed)], 0
    )
    left = drop_rows[...]
    turn = signs(W, 1.0, -1.0)
    turn_many = signs(GROUP * W, 1.0, -1.0)

    def backward(total, ref, item, owner, group):
        waves = []
        for slot in range(GROUP):
            number = owner * MOST + group * GROUP + slot
            high, low = split(grid * fields_ref[number])
            raw = dot(left, jnp.concatenate([high, high, low], 0))
            waves.append(raw[:W] + turn * swap(raw[W:]))
        high, low = split(jnp.concatenate(waves, 0))
        back = dot(jnp.concatenate([high, high, low], 1), drop_cols[...])
        start = pl.multiple_of(group * (GROUP * W), 16)
        real, imag = spread_pupil(ref[item, pl.ds(start, GROUP * W), :].astype(f32))
        product = real * back + imag * (turn_many * swap(back))
        for slot in range(GROUP):
            weight = weight_row(ref, item, group * GROUP + slot) * (2.0 / K)
            total = total + weight * product[slot * W : (slot + 1) * W]
        return total

    grad = for_groups(pupil_refs, active_ref, backward, jnp.zeros((W, LANES), f32))
    high, low = split(jnp.concatenate([grad * turn, -swap(grad)], 0))
    half = dot(grad_rows[my_block()], jnp.concatenate([high, high, low], 0))
    high, low = split(half)
    mask_grad_ref[0] = dot(jnp.concatenate([high, high], 1), grad_cols[...]) + dot(
        low, grad_cols[:LANES]
    )


VMEM = pl.BlockSpec(memory_space=pltpu.VMEM)
SMEM = pl.BlockSpec(memory_space=pltpu.SMEM)
PARAMS = pltpu.CompilerParams(vmem_limit_bytes=48 * 1024 * 1024)


def others(value, axis):
    size = lax.axis_size(axis)
    return [
        lax.ppermute(value, axis, [(i, i ^ step) for i in range(size)]) for step in range(1, size)
    ]


def shards(
    mask, target, tile_class, thresholds, source_pupil, source_weight, source_cell, active_count
):
    span, period = mask.shape[1:]
    slots = source_pupil.shape[0]
    src_count = lax.axis_size("src")
    few = src_count in (2, 4)
    table = {name: jnp.asarray(value) for name, value in tables(period, span).items()}
    src = lax.axis_index("src")

    part, placed = pl.pallas_call(
        spectrum_kernel,
        grid=(1,),
        in_specs=[
            VMEM,
            pl.BlockSpec((16, source_pupil.shape[1]), lambda i: (0, 0)),
            VMEM, SMEM, SMEM, VMEM, VMEM,
        ],
        out_specs=[VMEM, VMEM],
        out_shape=[
            jax.ShapeDtypeStruct((W, LANES), f32),
            jax.ShapeDtypeStruct((PUPIL_ROWS, LANES), bf16),
        ],
        scratch_shapes=[pltpu.VMEM((LANES, LANES), f32), pltpu.VMEM((MOST * W, LANES), f32)],
        compiler_params=PARAMS,
        name="spectrum",
    )(
        mask, source_pupil, source_weight, source_cell, active_count,
        table["spec_cols"], table["spec_rows"],
    )

    def reduced(value):
        for other in others(value, "pix"):
            value = value + other
        if few:
            return [value] + others(value, "src")
        return [lax.psum(value, "src")]

    if few:
        pupils = [placed[None]] + [other[None] for other in others(placed, "src")]
    else:
        pupils = [lax.all_gather(placed, "src")]
    spectra = reduced(part)

    numbers = src_count * MOST
    fold_rows_out = M // 2 + -(-numbers // 8) * 8
    intensity, folded, fields = pl.pallas_call(
        functools.partial(image_kernel, (len(spectra), len(pupils), fold_rows_out)),
        in_specs=[VMEM] * (len(spectra) + len(pupils) + 1) + [SMEM] * 3 + [VMEM] * 6,
        out_specs=[VMEM] * 3,
        out_shape=[
            jax.ShapeDtypeStruct((1, span, period), f32),
            jax.ShapeDtypeStruct((fold_rows_out, LANES), f32),
            jax.ShapeDtypeStruct((numbers, M, LANES), f32),
        ],
        compiler_params=PARAMS,
        name="image",
    )(
        *spectra, *pupils, target, active_count, tile_class, thresholds,
        table["lift_cols"], table["lift_rows"], table["fine_rows"], table["fine_cols"],
        table["fold_cols"], table["fold_rows"],
    )

    folds = reduced(folded)
    first = M // 2 + src * MOST
    rows = sum(lax.dynamic_slice_in_dim(fold, first, MOST, 0) for fold in folds)
    for other in others(rows, "tile"):
        rows = rows + other
    mask_grad = pl.pallas_call(
        functools.partial(gradient_kernel, (len(folds), len(pupils))),
        in_specs=[VMEM] * (len(folds) + len(pupils) + 1) + [SMEM] + [VMEM] * 4,
        out_specs=VMEM,
        out_shape=jax.ShapeDtypeStruct((1, span, period), f32),
        compiler_params=PARAMS,
        name="gradient",
    )(
        *folds, *pupils, fields, active_count,
        table["drop_rows"], table["drop_cols"], table["grad_rows"], table["grad_cols"],
    )
    sums = jnp.sum(rows[:, :M] + rows[:, M:], 1) * (1.0 / (period * K))
    live = jnp.arange(MOST, dtype=jnp.int32) < active_count[src]
    source_grad = jnp.pad(jnp.where(live, sums, 0.0), (0, slots - MOST))
    return intensity, mask_grad, source_grad


def solution(mesh):
    in_specs = (
        P(("groups", "tile"), ("src", "pix"), None),
        P(("groups", "tile"), ("src", "pix"), None),
        P(("groups", "tile")),
        P(),
        P("src", None),
        P("src"),
        P("src"),
        P(),
    )
    out_specs = (
        P(("groups", "tile"), ("src", "pix"), None),
        P(("groups", "tile"), ("src", "pix"), None),
        P(("groups", "src")),
    )
    return jax.shard_map(shards, mesh=mesh, in_specs=in_specs, out_specs=out_specs, check_vma=False)
```

```python
import functools

import jax
import jax.numpy as jnp
import ml_dtypes
import numpy as np
from jax import lax
from jax.experimental import pallas as pl
from jax.experimental.pallas import tpu as pltpu
from jax.sharding import PartitionSpec as P

K = 32
SG = 17
W = 48
MOST = 6
CLASSES = 4
STEEP = 4.0

M = 64
LANES = 128
PAIRS = MOST // 2
AT_PUPILS = 2 * W
AT_TAIL = AT_PUPILS + PAIRS * K
ROWS = AT_TAIL + 16
TAIL_PAIR, TAIL_CELL = 8, 12

f32 = jnp.float32
bf16 = jnp.bfloat16


def split_np(table):
    table = np.asarray(table, np.float32)
    high = table.astype(ml_dtypes.bfloat16)
    low = (table - high.astype(np.float32)).astype(ml_dtypes.bfloat16)
    return high, low


def halves(left, right):
    out = np.zeros((left.shape[0], LANES))
    out[:, : left.shape[1]] = left
    out[:, M : M + right.shape[1]] = right
    return out


@functools.lru_cache(maxsize=None)
def tables(period, span):
    blocks = period // span
    freqs = np.arange(W) - W // 2
    pixels = np.arange(period)
    wide = 2.0 * np.pi / period * ((freqs[:, None] * pixels[None, :]) % period)
    wide_cos, wide_sin = np.cos(wide), np.sin(wide)
    narrow = np.arange(K) - K // 2
    coarse = 2.0 * np.pi / M * ((narrow[:, None] * np.arange(M)[None, :]) % M)
    coarse_cos, coarse_sin = np.cos(coarse), np.sin(coarse)
    near = 2.0 * np.pi / period * ((narrow[:, None] * pixels[None, :]) % period)
    gain = sum(
        (wave * wave.astype(np.float32).astype(ml_dtypes.bfloat16).astype(np.float64)).mean(1)
        for wave in (np.cos(near), np.sin(near))
    )
    rounded_cos, rounded_sin = gain[:, None] * coarse_cos, gain[:, None] * coarse_sin
    high, low = split_np(halves(wide_cos.T, -wide_sin.T))
    spec_cols = np.concatenate([high, low], 1)
    rows = np.concatenate(
        [wide_cos.reshape(W, blocks, span), wide_sin.reshape(W, blocks, span)], 2
    ).transpose(1, 0, 2)
    high, low = split_np(rows / period)
    spec_rows = np.concatenate([high, low], 1)
    def pair_table(cos, sin):
        out = np.zeros((4 * K, 4 * M))
        for slot in range(2):
            real, imag, at = slot * K, (2 + slot) * K, slot * 2 * M
            out[real : real + K, at : at + 2 * M] = np.concatenate([cos, sin], 1)
            out[imag : imag + K, at : at + 2 * M] = np.concatenate([-sin, cos], 1)
        return out

    high, low = split_np(pair_table(rounded_cos, rounded_sin))
    lift_cols = np.concatenate([high, low], 0)
    high, low = split_np(np.concatenate([rounded_cos.T, rounded_sin.T], 0) / K)
    lift_rows = np.concatenate([high, low, high], 1)
    orders = np.arange(-(M // 2 - 1), M // 2)
    places = pixels[:, None] * (M / period) - np.arange(M)[None, :]
    inter = np.cos(2.0 * np.pi / M * places[:, :, None] * orders).sum(-1) / M
    high, low = split_np(inter)
    fine_cols = np.concatenate([high.T, low.T, high.T, low.T], 0)
    fold_cols = np.concatenate([high, low], 1)
    fine_rows = np.concatenate([high, low, high, low], 1).reshape(blocks, span, 4 * M)
    high_t = high.reshape(blocks, span, M).transpose(0, 2, 1)
    low_t = low.reshape(blocks, span, M).transpose(0, 2, 1)
    fold_rows = np.concatenate([high_t, low_t, high_t], 2)
    high, low = split_np(np.concatenate([rounded_cos, rounded_sin], 0))
    drop_rows = np.concatenate([high, low, high], 1)
    high, low = split_np(pair_table(coarse_cos, coarse_sin).T)
    drop_cols = np.concatenate([high, low, high], 0)
    rows = np.concatenate(
        [
            wide_cos.reshape(W, blocks, span).transpose(1, 2, 0),
            wide_sin.reshape(W, blocks, span).transpose(1, 2, 0),
        ],
        2,
    )
    high, low = split_np(rows / period)
    grad_rows = np.concatenate([high, low, high], 2)
    padded = [np.pad(part, ((0, M - W), (0, 0))) for part in (wide_cos, wide_sin)]
    high, low = split_np(np.concatenate(padded, 0))
    grad_cols = np.concatenate([high, low], 0)
    return dict(
        spec_cols=spec_cols,
        spec_rows=spec_rows,
        lift_cols=lift_cols,
        lift_rows=lift_rows,
        fine_cols=fine_cols,
        fold_cols=fold_cols,
        fine_rows=fine_rows,
        fold_rows=fold_rows,
        drop_rows=drop_rows,
        drop_cols=drop_cols,
        grad_rows=grad_rows,
        grad_cols=grad_cols,
    )


def dot(left, right):
    return jnp.dot(left, right, preferred_element_type=f32)


def split(value):
    high = value.astype(bf16)
    return high, (value - high.astype(f32)).astype(bf16)


def lane_of(shape):
    return lax.broadcasted_iota(jnp.int32, shape, len(shape) - 1)


def row_of(shape):
    return lax.broadcasted_iota(jnp.int32, shape, 0)


def swap(value):
    return pltpu.roll(value, M, 1)


def signs(rows, low, high):
    return jnp.where(lane_of((rows, LANES)) < M, f32(low), f32(high))


def my_block():
    return lax.axis_index("src") * lax.axis_size("pix") + lax.axis_index("pix")


def copies(sems, *pairs):
    out = [
        pltpu.make_async_copy(source, place, sems.at[number])
        for number, (source, place) in enumerate(pairs)
    ]
    for copy in out:
        copy.start()
    return out


def spectrum_kernel(
    mask_ref, pupil_ref, weight_ref, cell_ref, active_ref, cols_ref, rows_ref,
    part_ref, sent_ref,
    mask_in, pupil_in, weight_in, cell_in, active_in, cols, rows, sems, lined, paired,
):
    get_active, get_cell, get_pupil, get_weight, get_mask, get_cols, get_rows = copies(
        sems,
        (active_ref, active_in),
        (cell_ref, cell_in),
        (pupil_ref.at[pl.ds(0, 16)], pupil_in),
        (weight_ref, weight_in),
        (mask_ref.at[0], mask_in),
        (cols_ref, cols),
        (rows_ref.at[my_block()], rows),
    )
    get_active.wait()
    get_cell.wait()
    get_pupil.wait()
    get_weight.wait()
    active = active_in[lax.axis_index("src")]
    raw = pupil_in[...].astype(f32)[:8]
    raw = jnp.where(row_of(raw.shape) < active, raw, 0.0)
    for piece in range(16):
        lined[pl.ds(piece, 8, stride=16), :] = raw[:, piece * LANES : (piece + 1) * LANES]
    quarter = lane_of((8, LANES)) // K
    for pair in range(PAIRS):
        first, second = pair * 32, pair * 32 + 16
        quarters = [lined[pl.ds(start, 8), :] for start in (first, second, first + 8, second + 8)]
        for turn in range(4):
            moved = [
                value if number == turn else pltpu.roll(value, K * (number - turn) % LANES, 1)
                for number, value in enumerate(quarters)
            ]
            out = moved[3]
            for number in range(3):
                out = jnp.where(quarter == number, moved[number], out)
            paired[pl.ds(pair * K + turn, 8, stride=4), :] = out
    sent_ref[: PAIRS * K] = paired[...].astype(bf16)
    shape = (8, LANES)
    weights = jnp.broadcast_to(weight_in[...].astype(f32).reshape(1, -1)[:, :LANES], shape)
    column = jnp.sum(jnp.where(row_of(shape) == lane_of(shape), weights, 0.0), 1, keepdims=True)
    column = jnp.broadcast_to(column, shape)
    tail = [column]
    for pair in range(PAIRS):
        even = lane_of((1, LANES)) // K % 2 == 0
        tail.append(jnp.where(even, column[2 * pair : 2 * pair + 1], column[2 * pair + 1 : 2 * pair + 2]))
    tail.append(jnp.zeros((1, LANES), f32))
    place = lane_of((1, LANES))
    row_code, col_code = jnp.zeros((1, LANES), f32), jnp.zeros((1, LANES), f32)
    for slot in range(MOST):
        cell = cell_in[slot]
        row_code = jnp.where(place == slot, lax.div(cell, SG).astype(f32), row_code)
        col_code = jnp.where(place == slot, lax.rem(cell, SG).astype(f32), col_code)
    tail += [row_code, col_code, jnp.zeros((2, LANES), f32)]
    sent_ref[PAIRS * K :] = jnp.concatenate(tail, 0).astype(bf16)
    get_mask.wait()
    get_cols.wait()
    get_rows.wait()
    high, low = split(mask_in[...])
    both = dot(high, cols[...])
    part = both[:, :LANES] + both[:, LANES:] + dot(low, cols[:, :LANES])
    turned = swap(part) * signs(part.shape[0], 1.0, -1.0)
    high, low = split(jnp.concatenate([part, turned], 0))
    product = dot(rows[...], jnp.concatenate([high, low], 1))
    part_ref[...] = product[:W, :LANES] + product[:W, LANES:] + product[W:, :LANES]


def pack_kernel(part_ref, *refs):
    *other_refs, sent_ref, out_ref = refs
    part = part_ref[...]
    for ref in other_refs:
        part = part + ref[...]
    high, low = split(part)
    out_ref[:W] = high
    out_ref[W : 2 * W] = low
    out_ref[AT_PUPILS:] = sent_ref[...]


def owners_of(refs):
    src = lax.axis_index("src")
    if len(refs) > 1:
        return [(ref, jnp.bitwise_xor(src, step)) for step, ref in enumerate(refs)]
    return None


def over_owners(refs, body, carry):
    together = owners_of(refs)
    if together is not None:
        return body(carry, together)
    (ref,) = refs
    return lax.fori_loop(
        0, ref.shape[0], lambda owner, carry: body(carry, [(ref.at[owner], owner)]), carry
    )


def codes_of(refs, codes_v):
    def body(none, items):
        for ref, owner in items:
            tail = ref[pl.ds(AT_TAIL, 16), :].astype(f32)
            code = tail[TAIL_CELL : TAIL_CELL + 1] * 32.0 + tail[TAIL_CELL + 1 : TAIL_CELL + 2]
            codes_v[pl.ds(owner, 1), :] = code.astype(jnp.int32)
        return none

    over_owners(refs, body, 0)


def window_of(codes, owner, slot):
    code = codes[owner, slot]
    return lax.div(code, 32), lax.rem(code, 32)


def pair_parts(ref, pair):
    value = ref[pl.ds(AT_PUPILS + pair * K, K), :].astype(f32)
    other = swap(value)
    low = lane_of(value.shape) < M
    return jnp.where(low, value, other), jnp.where(low, other, value)


def slot_lanes(rows):
    return lane_of((rows, LANES)) // K % 2 == 0


def image_kernel(n_sent, *refs):
    sent_refs, refs = refs[:n_sent], refs[n_sent:]
    (
        target_ref, class_ref, thresholds_ref,
        lift_cols_ref, lift_rows_ref, fine_rows_ref, fine_cols_ref, fold_cols_ref, fold_rows_ref,
        intensity_ref, fold_ref, fields_ref,
        target, kinds, thresholds,
        lift_cols, lift_rows, fine_rows, fine_cols, fold_cols, fold_rows,
        sems, codes_v, codes, spectrum, intensity_out,
    ) = refs
    block = my_block()
    codes_of(sent_refs, codes_v)
    gets = copies(
        sems,
        (codes_v, codes),
        (lift_cols_ref, lift_cols),
        (lift_rows_ref, lift_rows),
        (class_ref, kinds),
        (thresholds_ref, thresholds),
        (fine_rows_ref.at[block], fine_rows),
        (fine_cols_ref, fine_cols),
        (target_ref.at[0], target),
        (fold_cols_ref, fold_cols),
        (fold_rows_ref.at[block], fold_rows),
    )

    def gather(total, items):
        for ref, owner in items:
            total = total + (ref[:W].astype(f32) + ref[W : 2 * W].astype(f32))
        return total

    spectrum[...] = over_owners(sent_refs, gather, jnp.zeros((W, LANES), f32))
    for get in gets[:3]:
        get.wait()
    even = slot_lanes(K)
    turn_low = signs(K, -1.0, 1.0)
    turn = signs(M, -1.0, 1.0)

    def forward(total, items):
        waves = []
        for ref, owner in items:
            for pair in range(PAIRS):
                real, imag = pair_parts(ref, pair)
                row, col = window_of(codes, owner, 2 * pair)
                left = pltpu.roll(spectrum[pl.ds(row, K), :], lax.rem(LANES - col, LANES), 1)
                row, col = window_of(codes, owner, 2 * pair + 1)
                right = pltpu.roll(spectrum[pl.ds(row, K), :], lax.rem(LANES + K - col, LANES), 1)
                window = jnp.where(even, left, right)
                waves.append((real * window + imag * (turn_low * swap(window))).astype(bf16))
        wave = jnp.concatenate(waves, 0)
        high, low = split(dot(jnp.concatenate([wave, wave], 1), lift_cols[...]))
        number = 0
        for ref, owner in items:
            weights = ref[pl.ds(AT_TAIL, 16), :].astype(f32)
            for pair in range(PAIRS):
                here = slice(number * K, (number + 1) * K)
                number += 1
                raw = dot(lift_rows[...], jnp.concatenate([high[here], high[here], low[here]], 0))
                for slot in range(2):
                    mine = raw[:, slot * LANES : (slot + 1) * LANES]
                    field = mine[:M] + turn * swap(mine[M:])
                    fields_ref[owner * MOST + 2 * pair + slot] = field
                    at = 2 * pair + slot
                    total = total + weights[at : at + 1] * (field * field)
        return total

    power = over_owners(sent_refs, forward, jnp.zeros((M, LANES), f32))
    for get in gets[3:]:
        get.wait()
    high, low = split(power + swap(power))
    half = dot(fine_rows[...], jnp.concatenate([high, high, low, low], 0))
    high, low = split(half)
    intensity = dot(jnp.concatenate([high, low], 1), fine_cols[...])
    intensity_out[...] = intensity
    put = pltpu.make_async_copy(intensity_out, intensity_ref.at[0], sems.at[len(gets)])
    put.start()
    kind = kinds[0]
    threshold = thresholds[0]
    for number in range(1, CLASSES):
        threshold = jnp.where(kind == number, thresholds[number], threshold)
    resist = 1.0 / (1.0 + jnp.exp(-STEEP * (intensity - threshold)))
    slope = (2.0 * STEEP * (resist - target[...]) * resist * (1.0 - resist)).astype(bf16)
    folded = dot(slope, fold_cols[...])
    high, low = split(folded + swap(folded))
    grid = dot(fold_rows[...], jnp.concatenate([high, high, low], 0))
    lane = lane_of((M // 2, LANES))
    fold_ref[: M // 2] = jnp.where(lane < M, grid[: M // 2], grid[M // 2 :])

    def weigh(none, items):
        for ref, owner in items:
            for slot in range(MOST):
                number = owner * MOST + slot
                field = fields_ref[number]
                total = jnp.sum(grid * (field * field), 0, keepdims=True)
                fold_ref[pl.ds(M // 2 + number, 1), :] = total
        return none

    over_owners(sent_refs, weigh, 0)
    put.wait()


def gradient_kernel(n_fold, n_sent, *refs):
    fold_refs, refs = refs[:n_fold], refs[n_fold:]
    sent_refs, refs = refs[:n_sent], refs[n_sent:]
    (
        fields_ref, drop_rows_ref, drop_cols_ref, grad_rows_ref, grad_cols_ref,
        mask_grad_ref,
        drop_rows, drop_cols, grad_rows, grad_cols, sems, codes_v, codes, sums, mask_grad_out,
    ) = refs
    codes_of(sent_refs, codes_v)
    gets = copies(
        sems,
        (drop_rows_ref, drop_rows),
        (codes_v, codes),
        (drop_cols_ref, drop_cols),
        (grad_rows_ref.at[my_block()], grad_rows),
        (grad_cols_ref, grad_cols),
    )
    packed = fold_refs[0][: M // 2]
    for ref in fold_refs[1:]:
        packed = packed + ref[: M // 2]
    other = swap(packed)
    low_half = lane_of(packed.shape) < M
    grid = jnp.concatenate(
        [jnp.where(low_half, packed, other), jnp.where(low_half, other, packed)], 0
    )
    for number in range(2):
        sums[number] = jnp.zeros((W, LANES), f32)
    turn = signs(K, 1.0, -1.0)
    even = slot_lanes(K)
    real_or_imag = lane_of((K, LANES)) % M < K
    for get in gets[:3]:
        get.wait()

    def backward(none, items):
        waves = []
        for ref, owner in items:
            for pair in range(PAIRS):
                fields = [grid * fields_ref[owner * MOST + 2 * pair + slot] for slot in range(2)]
                high, low = split(jnp.concatenate(fields, 1))
                raw = dot(drop_rows[...], jnp.concatenate([high, high, low], 0))
                wave = []
                for slot in range(2):
                    mine = raw[:, slot * LANES : (slot + 1) * LANES]
                    wave.append(mine[:K] + turn * swap(mine[K:]))
                waves.append(jnp.concatenate(wave, 1))
        high, low = split(jnp.concatenate(waves, 0))
        back = dot(jnp.concatenate([high, high, low], 1), drop_cols[...])
        number = 0
        for ref, owner in items:
            weights = ref[pl.ds(AT_TAIL, 16), :].astype(f32) * (2.0 / K)
            for pair in range(PAIRS):
                mine = back[number * K : (number + 1) * K]
                number += 1
                real, imag = pair_parts(ref, pair)
                product = real * mine + imag * (turn * swap(mine))
                product = weights[TAIL_PAIR + pair : TAIL_PAIR + pair + 1] * product
                for slot in range(2):
                    row, col = window_of(codes, owner, 2 * pair + slot)
                    keep = even if slot == 0 else jnp.logical_not(even)
                    shift = lax.rem(col + LANES - slot * K, LANES)
                    moved = pltpu.roll(jnp.where(keep, product, 0.0), shift, 1)
                    sums[slot, pl.ds(row, K), :] += moved
        return none

    over_owners(sent_refs, backward, 0)
    for get in gets[3:]:
        get.wait()
    grad = sums[0] + sums[1]
    turn = signs(W, 1.0, -1.0)
    high, low = split(jnp.concatenate([grad * turn, -swap(grad)], 0))
    half = dot(grad_rows[...], jnp.concatenate([high, high, low], 0))
    high, low = split(half)
    mask_grad_out[...] = dot(jnp.concatenate([high, high], 1), grad_cols[...]) + dot(
        low, grad_cols[:LANES]
    )
    put = pltpu.make_async_copy(mask_grad_out, mask_grad_ref.at[0], sems.at[len(gets)])
    put.start()
    put.wait()


VMEM = pl.BlockSpec(memory_space=pltpu.VMEM)
HBM = pl.BlockSpec(memory_space=pltpu.HBM)
PARAMS = pltpu.CompilerParams(vmem_limit_bytes=48 * 1024 * 1024)


def others(value, axis):
    size = lax.axis_size(axis)
    return [
        lax.ppermute(value, axis, [(i, i ^ step) for i in range(size)]) for step in range(1, size)
    ]


def like(value):
    return pltpu.VMEM(value.shape, value.dtype)


def shards(
    mask, target, tile_class, thresholds, source_pupil, source_weight, source_cell, active_count
):
    span, period = mask.shape[1:]
    slots = source_pupil.shape[0]
    src_count = lax.axis_size("src")
    few = src_count in (2, 4)
    table = {name: jnp.asarray(value) for name, value in tables(period, span).items()}
    src = lax.axis_index("src")
    sems = pltpu.SemaphoreType.DMA
    smem = pltpu.SMEM

    part, sent = pl.pallas_call(
        spectrum_kernel,
        in_specs=[HBM] * 7,
        out_specs=[VMEM, VMEM],
        out_shape=[
            jax.ShapeDtypeStruct((W, LANES), f32),
            jax.ShapeDtypeStruct((ROWS - AT_PUPILS, LANES), bf16),
        ],
        scratch_shapes=[
            like(mask[0]),
            like(source_pupil[:16]),
            like(source_weight),
            smem(source_cell.shape, jnp.int32),
            smem(active_count.shape, jnp.int32),
            like(table["spec_cols"]),
            like(table["spec_rows"][0]),
            sems((7,)),
            pltpu.VMEM((LANES, LANES), f32),
            pltpu.VMEM((PAIRS * K, LANES), f32),
        ],
        compiler_params=PARAMS,
        name="spectrum",
    )(
        mask, source_pupil, source_weight, source_cell, active_count,
        table["spec_cols"], table["spec_rows"],
    )
    from_pix = others(part, "pix")
    sent = pl.pallas_call(
        pack_kernel,
        in_specs=[VMEM] * (2 + len(from_pix)),
        out_specs=VMEM,
        out_shape=jax.ShapeDtypeStruct((ROWS, LANES), bf16),
        compiler_params=PARAMS,
        name="pack",
    )(part, *from_pix, sent)
    if few:
        parcels = [sent] + others(sent, "src")
    else:
        parcels = [lax.all_gather(sent, "src")]

    numbers = src_count * MOST
    owners_up = -(-src_count // 8) * 8
    fold_out = M // 2 + -(-numbers // 8) * 8
    codes = [pltpu.VMEM((owners_up, LANES), jnp.int32), smem((owners_up, LANES), jnp.int32)]
    intensity, folded, fields = pl.pallas_call(
        functools.partial(image_kernel, len(parcels)),
        in_specs=[VMEM] * len(parcels) + [HBM] * 9,
        out_specs=[HBM, VMEM, VMEM],
        out_shape=[
            jax.ShapeDtypeStruct((1, span, period), f32),
            jax.ShapeDtypeStruct((fold_out, LANES), f32),
            jax.ShapeDtypeStruct((numbers, M, LANES), f32),
        ],
        scratch_shapes=[
            like(target[0]),
            smem(tile_class.shape, jnp.int32),
            smem(thresholds.shape, f32),
            like(table["lift_cols"]),
            like(table["lift_rows"]),
            like(table["fine_rows"][0]),
            like(table["fine_cols"]),
            like(table["fold_cols"]),
            like(table["fold_rows"][0]),
            sems((11,)),
            *codes,
            pltpu.VMEM((W, LANES), f32),
            like(target[0]),
        ],
        compiler_params=PARAMS,
        name="image",
    )(
        *parcels, target, tile_class, thresholds,
        table["lift_cols"], table["lift_rows"], table["fine_rows"], table["fine_cols"],
        table["fold_cols"], table["fold_rows"],
    )

    for other in others(folded, "pix"):
        folded = folded + other
    folds = [folded] + others(folded, "src") if few else [lax.psum(folded, "src")]
    first = M // 2 + src * MOST
    rows = sum(lax.dynamic_slice_in_dim(fold, first, MOST, 0) for fold in folds)
    for other in others(rows, "tile"):
        rows = rows + other
    mask_grad = pl.pallas_call(
        functools.partial(gradient_kernel, len(folds), len(parcels)),
        in_specs=[VMEM] * (len(folds) + len(parcels) + 1) + [HBM] * 4,
        out_specs=HBM,
        out_shape=jax.ShapeDtypeStruct((1, span, period), f32),
        scratch_shapes=[
            like(table["drop_rows"]),
            like(table["drop_cols"]),
            like(table["grad_rows"][0]),
            like(table["grad_cols"]),
            sems((6,)),
            *codes,
            pltpu.VMEM((2, W, LANES), f32),
            like(mask[0]),
        ],
        compiler_params=PARAMS,
        name="gradient",
    )(
        *folds, *parcels, fields,
        table["drop_rows"], table["drop_cols"], table["grad_rows"], table["grad_cols"],
    )
    sums = jnp.sum(rows, 1) * (1.0 / (period * K))
    source_grad = jnp.zeros((slots,), f32).at[:MOST].set(sums)
    return intensity, mask_grad, source_grad


def solution(mesh):
    in_specs = (
        P(("groups", "tile"), ("src", "pix"), None),
        P(("groups", "tile"), ("src", "pix"), None),
        P(("groups", "tile")),
        P(),
        P("src", None),
        P("src"),
        P("src"),
        P(),
    )
    out_specs = (
        P(("groups", "tile"), ("src", "pix"), None),
        P(("groups", "tile"), ("src", "pix"), None),
        P(("groups", "src")),
    )
    return jax.shard_map(shards, mesh=mesh, in_specs=in_specs, out_specs=out_specs, check_vma=False)
```

```python
import functools

import jax
import jax.numpy as jnp
import ml_dtypes
import numpy as np
from jax import lax
from jax.experimental import pallas as pl
from jax.experimental.pallas import tpu as pltpu
from jax.sharding import PartitionSpec as P

K = 32
SG = 17
W = 48
MOST = 6
CLASSES = 4
STEEP = 4.0

M = 64
LANES = 128
PAIRS = MOST // 2
AT_PUPILS = 2 * W
AT_TAIL = AT_PUPILS + PAIRS * K
ROWS = AT_TAIL + 16
TAIL_PAIR, TAIL_CELL = 8, 12

f32 = jnp.float32
bf16 = jnp.bfloat16


def split_np(table):
    table = np.asarray(table, np.float32)
    high = table.astype(ml_dtypes.bfloat16)
    low = (table - high.astype(np.float32)).astype(ml_dtypes.bfloat16)
    return high, low


def halves(left, right):
    out = np.zeros((left.shape[0], LANES))
    out[:, : left.shape[1]] = left
    out[:, M : M + right.shape[1]] = right
    return out


@functools.lru_cache(maxsize=None)
def tables(period, span):
    blocks = period // span
    freqs = np.arange(W) - W // 2
    pixels = np.arange(period)
    wide = 2.0 * np.pi / period * ((freqs[:, None] * pixels[None, :]) % period)
    wide_cos, wide_sin = np.cos(wide), np.sin(wide)
    narrow = np.arange(K) - K // 2
    coarse = 2.0 * np.pi / M * ((narrow[:, None] * np.arange(M)[None, :]) % M)
    coarse_cos, coarse_sin = np.cos(coarse), np.sin(coarse)
    near = 2.0 * np.pi / period * ((narrow[:, None] * pixels[None, :]) % period)
    gain = sum(
        (wave * wave.astype(np.float32).astype(ml_dtypes.bfloat16).astype(np.float64)).mean(1)
        for wave in (np.cos(near), np.sin(near))
    )
    rounded_cos, rounded_sin = gain[:, None] * coarse_cos, gain[:, None] * coarse_sin
    high, low = split_np(halves(wide_cos.T, -wide_sin.T))
    spec_cols = np.concatenate([high, low], 1)
    rows = np.concatenate(
        [wide_cos.reshape(W, blocks, span), wide_sin.reshape(W, blocks, span)], 2
    ).transpose(1, 0, 2)
    high, low = split_np(rows / period)
    spec_rows = np.concatenate([high, low], 1)
    def pair_table(cos, sin):
        out = np.zeros((4 * K, 4 * M))
        for slot in range(2):
            real, imag, at = slot * K, (2 + slot) * K, slot * 2 * M
            out[real : real + K, at : at + 2 * M] = np.concatenate([cos, sin], 1)
            out[imag : imag + K, at : at + 2 * M] = np.concatenate([-sin, cos], 1)
        return out

    high, low = split_np(pair_table(rounded_cos, rounded_sin))
    lift_cols = np.concatenate([high, low], 0)
    high, low = split_np(np.concatenate([rounded_cos.T, rounded_sin.T], 0) / K)
    lift_rows = np.concatenate([high, low, high], 1)
    orders = np.arange(-(M // 2 - 1), M // 2)
    places = pixels[:, None] * (M / period) - np.arange(M)[None, :]
    inter = np.cos(2.0 * np.pi / M * places[:, :, None] * orders).sum(-1) / M
    high, low = split_np(inter)
    fine_cols = np.concatenate([high.T, low.T, high.T, low.T], 0)
    fold_cols = np.concatenate([high, low], 1)
    fine_rows = np.concatenate([high, low, high, low], 1).reshape(blocks, span, 4 * M)
    high_t = high.reshape(blocks, span, M).transpose(0, 2, 1)
    low_t = low.reshape(blocks, span, M).transpose(0, 2, 1)
    fold_rows = np.concatenate([high_t, low_t, high_t], 2)
    high, low = split_np(np.concatenate([rounded_cos, rounded_sin], 0))
    drop_rows = np.concatenate([high, low, high], 1)
    high, low = split_np(pair_table(coarse_cos, coarse_sin).T)
    drop_cols = np.concatenate([high, low, high], 0)
    rows = np.concatenate(
        [
            wide_cos.reshape(W, blocks, span).transpose(1, 2, 0),
            wide_sin.reshape(W, blocks, span).transpose(1, 2, 0),
        ],
        2,
    )
    high, low = split_np(rows / period)
    grad_rows = np.concatenate([high, low, high], 2)
    padded = [np.pad(part, ((0, M - W), (0, 0))) for part in (wide_cos, wide_sin)]
    high, low = split_np(np.concatenate(padded, 0))
    grad_cols = np.concatenate([high, low], 0)
    chapters = [
        dict(lift_cols=lift_cols, lift_rows=lift_rows),
        dict(fine_cols=fine_cols, fold_cols=fold_cols),
        dict(drop_rows=drop_rows, drop_cols=drop_cols),
        dict(grad_cols=grad_cols),
    ]
    for block in range(blocks):
        chapters.append(dict(fine_rows=fine_rows[block], fold_rows=fold_rows[block]))
    for block in range(blocks):
        chapters.append(dict(grad_rows=grad_rows[block]))
    pages, starts, places, at = [], [], {}, 0
    for chapter in chapters:
        starts.append(at)
        for name, value in chapter.items():
            places[name] = (at - starts[-1], value.shape)
            for lane in range(0, value.shape[1], LANES):
                page = value[:, lane : lane + LANES]
                pages.append(np.pad(page, ((0, 0), (0, LANES - page.shape[1]))))
                at += page.shape[0]
    starts.append(at)
    return spec_cols, spec_rows, Book(np.concatenate(pages, 0), starts, places, blocks)


class Book:
    def __init__(self, pages, starts, places, blocks):
        self.pages, self.starts, self.places, self.blocks = pages, starts, places, blocks

    def rows(self, chapter):
        return self.starts[chapter + 1] - self.starts[chapter]

    def shapes(self, *chapters):
        return [jax.ShapeDtypeStruct((self.rows(chapter), LANES), bf16) for chapter in chapters]

    def where(self, ref, chapter, block=0):
        return ref.at[pl.ds(self.starts[chapter] + block * self.rows(chapter), self.rows(chapter))]

    def read(self, ref, name):
        at, (rows, lanes) = self.places[name]
        pages = [
            ref[at + number * rows : at + (number + 1) * rows, : min(LANES, lanes - lane)]
            for number, lane in enumerate(range(0, lanes, LANES))
        ]
        return pages[0] if len(pages) == 1 else jnp.concatenate(pages, 1)


LIFT, FINE, DROP, GRAD, IMAGE_ROWS = range(5)


def dot(left, right):
    return jnp.dot(left, right, preferred_element_type=f32)


def split(value):
    high = value.astype(bf16)
    return high, (value - high.astype(f32)).astype(bf16)


def lane_of(shape):
    return lax.broadcasted_iota(jnp.int32, shape, len(shape) - 1)


def row_of(shape):
    return lax.broadcasted_iota(jnp.int32, shape, 0)


def swap(value):
    return pltpu.roll(value, M, 1)


def signs(rows, low, high):
    return jnp.where(lane_of((rows, LANES)) < M, f32(low), f32(high))


def my_block():
    return lax.axis_index("src") * lax.axis_size("pix") + lax.axis_index("pix")


def copies(sems, *pairs):
    out = [
        pltpu.make_async_copy(source, place, sems.at[number])
        for number, (source, place) in enumerate(pairs)
    ]
    for copy in out:
        copy.start()
    return out


def spectrum_kernel(
    mask_ref, pupil_ref, weight_ref, cell_ref, active_ref, class_ref, thresholds_ref,
    cols_ref, rows_ref,
    part_ref, sent_ref, threshold_ref,
    mask_in, pupil_in, weight_in, cell_in, active_in, thresholds, cols, rows,
    sems, lined, paired,
):
    (
        get_active, get_cell, get_pupil, get_weight, get_mask, get_cols, get_rows,
        get_thresholds,
    ) = copies(
        sems,
        (active_ref, active_in),
        (cell_ref, cell_in),
        (pupil_ref.at[pl.ds(0, 16)], pupil_in),
        (weight_ref, weight_in),
        (mask_ref.at[0], mask_in),
        (cols_ref, cols),
        (rows_ref.at[my_block()], rows),
        (thresholds_ref, thresholds),
    )
    get_active.wait()
    get_cell.wait()
    get_pupil.wait()
    get_weight.wait()
    active = active_in[lax.axis_index("src")]
    raw = pupil_in[...].astype(f32)[:8]
    raw = jnp.where(row_of(raw.shape) < active, raw, 0.0)
    for piece in range(16):
        lined[pl.ds(piece, 8, stride=16), :] = raw[:, piece * LANES : (piece + 1) * LANES]
    quarter = lane_of((8, LANES)) // K
    for pair in range(PAIRS):
        first, second = pair * 32, pair * 32 + 16
        quarters = [lined[pl.ds(start, 8), :] for start in (first, second, first + 8, second + 8)]
        for turn in range(4):
            moved = [
                value if number == turn else pltpu.roll(value, K * (number - turn) % LANES, 1)
                for number, value in enumerate(quarters)
            ]
            out = moved[3]
            for number in range(3):
                out = jnp.where(quarter == number, moved[number], out)
            paired[pl.ds(pair * K + turn, 8, stride=4), :] = out
    sent_ref[: PAIRS * K] = paired[...].astype(bf16)
    shape = (8, LANES)
    weights = jnp.broadcast_to(weight_in[...].astype(f32).reshape(1, -1)[:, :LANES], shape)
    column = jnp.sum(jnp.where(row_of(shape) == lane_of(shape), weights, 0.0), 1, keepdims=True)
    column = jnp.broadcast_to(column, shape)
    tail = [column]
    for pair in range(PAIRS):
        even = lane_of((1, LANES)) // K % 2 == 0
        tail.append(jnp.where(even, column[2 * pair : 2 * pair + 1], column[2 * pair + 1 : 2 * pair + 2]))
    tail.append(jnp.zeros((1, LANES), f32))
    place = lane_of((1, LANES))
    row_code, col_code = jnp.zeros((1, LANES), f32), jnp.zeros((1, LANES), f32)
    for slot in range(MOST):
        cell = cell_in[slot]
        row_code = jnp.where(place == slot, lax.div(cell, SG).astype(f32), row_code)
        col_code = jnp.where(place == slot, lax.rem(cell, SG).astype(f32), col_code)
    tail += [row_code, col_code, jnp.zeros((2, LANES), f32)]
    sent_ref[PAIRS * K :] = jnp.concatenate(tail, 0).astype(bf16)
    get_mask.wait()
    get_cols.wait()
    get_rows.wait()
    high, low = split(mask_in[...])
    both = dot(high, cols[...])
    part = both[:, :LANES] + both[:, LANES:] + dot(low, cols[:, :LANES])
    turned = swap(part) * signs(part.shape[0], 1.0, -1.0)
    high, low = split(jnp.concatenate([part, turned], 0))
    product = dot(rows[...], jnp.concatenate([high, low], 1))
    part_ref[...] = product[:W, :LANES] + product[:W, LANES:] + product[W:, :LANES]
    get_thresholds.wait()
    kind = class_ref[0]
    threshold = thresholds[0]
    for number in range(1, CLASSES):
        threshold = jnp.where(kind == number, thresholds[number], threshold)
    threshold_ref[...] = jnp.full(threshold_ref.shape, threshold, f32)


def pack_kernel(part_ref, *refs):
    *other_refs, sent_ref, out_ref = refs
    part = part_ref[...]
    for ref in other_refs:
        part = part + ref[...]
    high, low = split(part)
    out_ref[:W] = high
    out_ref[W : 2 * W] = low
    out_ref[AT_PUPILS:] = sent_ref[...]


def stage_kernel(book, target_ref, book_ref, *refs):
    *out_refs, sems = refs
    target_out, lift_out, fine_out, rows_out, drop_out, grad_out, grad_rows_out = out_refs
    gets = copies(
        sems,
        (book.where(book_ref, LIFT), lift_out),
        (book.where(book_ref, IMAGE_ROWS, my_block()), rows_out),
        (book.where(book_ref, FINE), fine_out),
        (target_ref.at[0], target_out),
        (book.where(book_ref, DROP), drop_out),
        (book.where(book_ref, GRAD), grad_out),
        (book.where(book_ref, IMAGE_ROWS + book.blocks, my_block()), grad_rows_out),
    )
    for get in gets:
        get.wait()


def owners_of(refs):
    src = lax.axis_index("src")
    if len(refs) > 1:
        return [(ref, jnp.bitwise_xor(src, step)) for step, ref in enumerate(refs)]
    return None


def over_owners(refs, body, carry):
    together = owners_of(refs)
    if together is not None:
        return body(carry, together)
    (ref,) = refs
    return lax.fori_loop(
        0, ref.shape[0], lambda owner, carry: body(carry, [(ref.at[owner], owner)]), carry
    )


def codes_of(refs, codes_v):
    def body(none, items):
        for ref, owner in items:
            tail = ref[pl.ds(AT_TAIL, 16), :].astype(f32)
            code = tail[TAIL_CELL : TAIL_CELL + 1] * 32.0 + tail[TAIL_CELL + 1 : TAIL_CELL + 2]
            codes_v[pl.ds(owner, 1), :] = code.astype(jnp.int32)
        return none

    over_owners(refs, body, 0)


def window_of(codes, owner, slot):
    code = codes[owner, slot]
    return lax.div(code, 32), lax.rem(code, 32)


def pair_parts(ref, pair):
    value = ref[pl.ds(AT_PUPILS + pair * K, K), :].astype(f32)
    other = swap(value)
    low = lane_of(value.shape) < M
    return jnp.where(low, value, other), jnp.where(low, other, value)


def slot_lanes(rows):
    return lane_of((rows, LANES)) // K % 2 == 0


def image_kernel(book, n_sent, *refs):
    sent_refs, refs = refs[:n_sent], refs[n_sent:]
    (
        threshold_ref, target, lift, fine, image_rows,
        intensity_ref, fold_ref, fields,
        sems, codes_v, codes, spectrum, intensity_out,
    ) = refs
    codes_of(sent_refs, codes_v)
    (get_codes,) = copies(sems, (codes_v, codes))

    def gather(total, items):
        for ref, owner in items:
            total = total + (ref[:W].astype(f32) + ref[W : 2 * W].astype(f32))
        return total

    spectrum[...] = over_owners(sent_refs, gather, jnp.zeros((W, LANES), f32))
    get_codes.wait()
    lift_cols, lift_rows = book.read(lift, "lift_cols"), book.read(lift, "lift_rows")
    even = slot_lanes(K)
    turn_low = signs(K, -1.0, 1.0)
    turn = signs(M, -1.0, 1.0)

    def forward(total, items):
        waves = []
        for ref, owner in items:
            for pair in range(PAIRS):
                real, imag = pair_parts(ref, pair)
                row, col = window_of(codes, owner, 2 * pair)
                left = pltpu.roll(spectrum[pl.ds(row, K), :], lax.rem(LANES - col, LANES), 1)
                row, col = window_of(codes, owner, 2 * pair + 1)
                right = pltpu.roll(spectrum[pl.ds(row, K), :], lax.rem(LANES + K - col, LANES), 1)
                window = jnp.where(even, left, right)
                waves.append((real * window + imag * (turn_low * swap(window))).astype(bf16))
        wave = jnp.concatenate(waves, 0)
        high, low = split(dot(jnp.concatenate([wave, wave], 1), lift_cols))
        number = 0
        for ref, owner in items:
            weights = ref[pl.ds(AT_TAIL, 16), :].astype(f32)
            for pair in range(PAIRS):
                here = slice(number * K, (number + 1) * K)
                number += 1
                raw = dot(lift_rows, jnp.concatenate([high[here], high[here], low[here]], 0))
                for slot in range(2):
                    mine = raw[:, slot * LANES : (slot + 1) * LANES]
                    field = mine[:M] + turn * swap(mine[M:])
                    fields[owner * MOST + 2 * pair + slot] = field
                    at = 2 * pair + slot
                    total = total + weights[at : at + 1] * (field * field)
        return total

    power = over_owners(sent_refs, forward, jnp.zeros((M, LANES), f32))
    high, low = split(power + swap(power))
    half = dot(book.read(image_rows, "fine_rows"), jnp.concatenate([high, high, low, low], 0))
    high, low = split(half)
    intensity = dot(jnp.concatenate([high, low], 1), book.read(fine, "fine_cols"))
    intensity_out[...] = intensity
    put = pltpu.make_async_copy(intensity_out, intensity_ref.at[0], sems.at[1])
    put.start()
    threshold = threshold_ref[:1, :1]
    resist = 1.0 / (1.0 + jnp.exp(-STEEP * (intensity - threshold)))
    slope = (2.0 * STEEP * (resist - target[...]) * resist * (1.0 - resist)).astype(bf16)
    folded = dot(slope, book.read(fine, "fold_cols"))
    high, low = split(folded + swap(folded))
    grid = dot(book.read(image_rows, "fold_rows"), jnp.concatenate([high, high, low], 0))
    lane = lane_of((M // 2, LANES))
    fold_ref[: M // 2] = jnp.where(lane < M, grid[: M // 2], grid[M // 2 :])

    def weigh(none, items):
        for ref, owner in items:
            for slot in range(MOST):
                number = owner * MOST + slot
                field = fields[number]
                total = jnp.sum(grid * (field * field), 0, keepdims=True)
                fold_ref[pl.ds(M // 2 + number, 1), :] = total
        return none

    over_owners(sent_refs, weigh, 0)
    put.wait()


def gradient_kernel(book, n_fold, n_sent, *refs):
    fold_refs, refs = refs[:n_fold], refs[n_fold:]
    sent_refs, refs = refs[:n_sent], refs[n_sent:]
    (
        fields, drop, grad_table, rows_table,
        mask_grad_ref,
        sems, codes_v, codes, sums, mask_grad_out,
    ) = refs
    codes_of(sent_refs, codes_v)
    (get_codes,) = copies(sems, (codes_v, codes))
    packed = fold_refs[0][: M // 2]
    for ref in fold_refs[1:]:
        packed = packed + ref[: M // 2]
    other = swap(packed)
    low_half = lane_of(packed.shape) < M
    grid = jnp.concatenate(
        [jnp.where(low_half, packed, other), jnp.where(low_half, other, packed)], 0
    )
    for number in range(2):
        sums[number] = jnp.zeros((W, LANES), f32)
    turn = signs(K, 1.0, -1.0)
    even = slot_lanes(K)
    real_or_imag = lane_of((K, LANES)) % M < K
    get_codes.wait()
    drop_rows, drop_cols = book.read(drop, "drop_rows"), book.read(drop, "drop_cols")

    def backward(none, items):
        waves = []
        for ref, owner in items:
            for pair in range(PAIRS):
                scaled = [grid * fields[owner * MOST + 2 * pair + slot] for slot in range(2)]
                high, low = split(jnp.concatenate(scaled, 1))
                raw = dot(drop_rows, jnp.concatenate([high, high, low], 0))
                wave = []
                for slot in range(2):
                    mine = raw[:, slot * LANES : (slot + 1) * LANES]
                    wave.append(mine[:K] + turn * swap(mine[K:]))
                waves.append(jnp.concatenate(wave, 1))
        high, low = split(jnp.concatenate(waves, 0))
        back = dot(jnp.concatenate([high, high, low], 1), drop_cols)
        number = 0
        for ref, owner in items:
            weights = ref[pl.ds(AT_TAIL, 16), :].astype(f32) * (2.0 / K)
            for pair in range(PAIRS):
                mine = back[number * K : (number + 1) * K]
                number += 1
                real, imag = pair_parts(ref, pair)
                product = real * mine + imag * (turn * swap(mine))
                product = weights[TAIL_PAIR + pair : TAIL_PAIR + pair + 1] * product
                for slot in range(2):
                    row, col = window_of(codes, owner, 2 * pair + slot)
                    keep = even if slot == 0 else jnp.logical_not(even)
                    shift = lax.rem(col + LANES - slot * K, LANES)
                    moved = pltpu.roll(jnp.where(keep, product, 0.0), shift, 1)
                    sums[slot, pl.ds(row, K), :] += moved
        return none

    over_owners(sent_refs, backward, 0)
    grad_cols = book.read(grad_table, "grad_cols")
    grad = sums[0] + sums[1]
    turn = signs(W, 1.0, -1.0)
    high, low = split(jnp.concatenate([grad * turn, -swap(grad)], 0))
    half = dot(book.read(rows_table, "grad_rows"), jnp.concatenate([high, high, low], 0))
    high, low = split(half)
    mask_grad_out[...] = dot(jnp.concatenate([high, high], 1), grad_cols) + dot(
        low, grad_cols[:LANES]
    )
    put = pltpu.make_async_copy(mask_grad_out, mask_grad_ref.at[0], sems.at[1])
    put.start()
    put.wait()


VMEM = pl.BlockSpec(memory_space=pltpu.VMEM)
SMEM = pl.BlockSpec(memory_space=pltpu.SMEM)
HBM = pl.BlockSpec(memory_space=pltpu.HBM)


def room(kib):
    return pltpu.CompilerParams(vmem_limit_bytes=(64 * 1024 - kib) * 1024)


def in_hbm(value):
    return pltpu.with_memory_space_constraint(value, pltpu.HBM)


def others(value, axis):
    size = lax.axis_size(axis)
    return [
        lax.ppermute(value, axis, [(i, i ^ step) for i in range(size)]) for step in range(1, size)
    ]


def like(value):
    return pltpu.VMEM(value.shape, value.dtype)


def shards(
    mask, target, tile_class, thresholds, source_pupil, source_weight, source_cell, active_count
):
    span, period = mask.shape[1:]
    slots = source_pupil.shape[0]
    src_count = lax.axis_size("src")
    few = src_count in (2, 4)
    spec_cols, spec_rows, book = tables(period, span)
    pages = jnp.asarray(book.pages)
    src = lax.axis_index("src")
    sems = pltpu.SemaphoreType.DMA
    smem = pltpu.SMEM

    part, sent, threshold = pl.pallas_call(
        spectrum_kernel,
        in_specs=[HBM] * 5 + [SMEM] + [HBM] * 3,
        out_specs=[VMEM] * 3,
        out_shape=[
            jax.ShapeDtypeStruct((W, LANES), f32),
            jax.ShapeDtypeStruct((ROWS - AT_PUPILS, LANES), bf16),
            jax.ShapeDtypeStruct((8, LANES), f32),
        ],
        scratch_shapes=[
            like(mask[0]),
            like(source_pupil[:16]),
            like(source_weight),
            smem(source_cell.shape, jnp.int32),
            smem(active_count.shape, jnp.int32),
            smem(thresholds.shape, f32),
            like(spec_cols),
            like(spec_rows[0]),
            sems((8,)),
            pltpu.VMEM((LANES, LANES), f32),
            pltpu.VMEM((PAIRS * K, LANES), f32),
        ],
        compiler_params=room(24576),
        name="spectrum",
    )(
        *map(in_hbm, (mask, source_pupil, source_weight, source_cell, active_count)),
        tile_class,
        *map(in_hbm, (thresholds, jnp.asarray(spec_cols), jnp.asarray(spec_rows))),
    )
    from_pix = others(part, "pix")
    sent = pl.pallas_call(
        pack_kernel,
        in_specs=[VMEM] * (2 + len(from_pix)),
        out_specs=VMEM,
        out_shape=jax.ShapeDtypeStruct((ROWS, LANES), bf16),
        compiler_params=room(32768),
        name="pack",
    )(part, *from_pix, sent)
    if few:
        parcels = [sent] + others(sent, "src")
    else:
        parcels = [lax.all_gather(sent, "src")]

    late_target, late_pages, _ = lax.optimization_barrier((target, pages, sent))
    staged_shapes = [
        jax.ShapeDtypeStruct((span, period), f32),
        *book.shapes(LIFT, FINE, IMAGE_ROWS, DROP, GRAD, IMAGE_ROWS + book.blocks),
    ]
    staged = pl.pallas_call(
        functools.partial(stage_kernel, book),
        in_specs=[HBM] * 2,
        out_specs=[VMEM] * len(staged_shapes),
        out_shape=staged_shapes,
        scratch_shapes=[sems((len(staged_shapes),))],
        compiler_params=room(24576),
        name="stage",
    )(in_hbm(late_target), in_hbm(late_pages))
    for_image, for_gradient = staged[:4], staged[4:]

    numbers = src_count * MOST
    owners_up = -(-src_count // 8) * 8
    fold_out = M // 2 + -(-numbers // 8) * 8
    codes = [pltpu.VMEM((owners_up, LANES), jnp.int32), smem((owners_up, LANES), jnp.int32)]
    intensity, folded, fields = pl.pallas_call(
        functools.partial(image_kernel, book, len(parcels)),
        in_specs=[VMEM] * (len(parcels) + 1 + len(for_image)),
        out_specs=[HBM, VMEM, VMEM],
        out_shape=[
            jax.ShapeDtypeStruct((1, span, period), f32),
            jax.ShapeDtypeStruct((fold_out, LANES), f32),
            jax.ShapeDtypeStruct((numbers, M, LANES), f32),
        ],
        scratch_shapes=[
            sems((2,)),
            *codes,
            pltpu.VMEM((W, LANES), f32),
            like(target[0]),
        ],
        compiler_params=room(24576),
        name="image",
    )(*parcels, threshold, *for_image)

    for other in others(folded, "pix"):
        folded = folded + other
    folds = [folded] + others(folded, "src") if few else [lax.psum(folded, "src")]
    first = M // 2 + src * MOST
    rows = sum(lax.dynamic_slice_in_dim(fold, first, MOST, 0) for fold in folds)
    for other in others(rows, "tile"):
        rows = rows + other
    mask_grad = pl.pallas_call(
        functools.partial(gradient_kernel, book, len(folds), len(parcels)),
        in_specs=[VMEM] * (len(folds) + len(parcels) + 1 + len(for_gradient)),
        out_specs=HBM,
        out_shape=jax.ShapeDtypeStruct((1, span, period), f32),
        scratch_shapes=[
            sems((2,)),
            *codes,
            pltpu.VMEM((2, W, LANES), f32),
            like(mask[0]),
        ],
        compiler_params=room(24576),
        name="gradient",
    )(*folds, *parcels, fields, *for_gradient)
    sums = jnp.sum(rows, 1) * (1.0 / (period * K))
    source_grad = jnp.zeros((slots,), f32).at[:MOST].set(sums)
    return intensity, mask_grad, source_grad


def solution(mesh):
    in_specs = (
        P(("groups", "tile"), ("src", "pix"), None),
        P(("groups", "tile"), ("src", "pix"), None),
        P(("groups", "tile")),
        P(),
        P("src", None),
        P("src"),
        P("src"),
        P(),
    )
    out_specs = (
        P(("groups", "tile"), ("src", "pix"), None),
        P(("groups", "tile"), ("src", "pix"), None),
        P(("groups", "src")),
    )
    return jax.shard_map(shards, mesh=mesh, in_specs=in_specs, out_specs=out_specs, check_vma=False)
```

```python
import functools

import jax
import jax.numpy as jnp
import ml_dtypes
import numpy as np
from jax import lax
from jax.experimental import pallas as pl
from jax.experimental.pallas import tpu as pltpu
from jax.sharding import PartitionSpec as P

K = 32
SG = 17
W = 48
MOST = 6
CLASSES = 4
STEEP = 4.0

M = 64
LANES = 128
PAIRS = MOST // 2
AT_PUPILS = 2 * W
AT_TAIL = AT_PUPILS + PAIRS * K
ROWS = AT_TAIL + 16
TAIL_PAIR, TAIL_CELL = 8, 12
PIECES = 4
SUMS = 8

f32 = jnp.float32
bf16 = jnp.bfloat16


def split_np(table):
    table = np.asarray(table, np.float32)
    high = table.astype(ml_dtypes.bfloat16)
    low = (table - high.astype(np.float32)).astype(ml_dtypes.bfloat16)
    return high, low


def halves(left, right):
    out = np.zeros((left.shape[0], LANES))
    out[:, : left.shape[1]] = left
    out[:, M : M + right.shape[1]] = right
    return out


@functools.lru_cache(maxsize=None)
def tables(period, span):
    blocks = period // span
    freqs = np.arange(W) - W // 2
    pixels = np.arange(period)
    wide = 2.0 * np.pi / period * ((freqs[:, None] * pixels[None, :]) % period)
    wide_cos, wide_sin = np.cos(wide), np.sin(wide)
    narrow = np.arange(K) - K // 2
    coarse = 2.0 * np.pi / M * ((narrow[:, None] * np.arange(M)[None, :]) % M)
    coarse_cos, coarse_sin = np.cos(coarse), np.sin(coarse)
    near = 2.0 * np.pi / period * ((narrow[:, None] * pixels[None, :]) % period)
    gain = sum(
        (wave * wave.astype(np.float32).astype(ml_dtypes.bfloat16).astype(np.float64)).mean(1)
        for wave in (np.cos(near), np.sin(near))
    )
    rounded_cos, rounded_sin = gain[:, None] * coarse_cos, gain[:, None] * coarse_sin
    high, low = split_np(halves(wide_cos.T, -wide_sin.T))
    spec_cols = np.concatenate([high, low], 1)
    rows = np.concatenate(
        [wide_cos.reshape(W, blocks, span), wide_sin.reshape(W, blocks, span)], 2
    ).transpose(1, 0, 2)
    high, low = split_np(rows / period)
    spec_rows = np.concatenate([high, low], 1)
    def pair_table(cos, sin):
        out = np.zeros((4 * K, 4 * M))
        for slot in range(2):
            real, imag, at = slot * K, (2 + slot) * K, slot * 2 * M
            out[real : real + K, at : at + 2 * M] = np.concatenate([cos, sin], 1)
            out[imag : imag + K, at : at + 2 * M] = np.concatenate([-sin, cos], 1)
        return out

    high, low = split_np(pair_table(rounded_cos, rounded_sin))
    lift_cols = np.concatenate([high, low], 0)
    high, low = split_np(np.concatenate([rounded_cos.T, rounded_sin.T], 0) / K)
    lift_rows = np.concatenate([high, low, high], 1)
    orders = np.arange(-(M // 2 - 1), M // 2)
    places = pixels[:, None] * (M / period) - np.arange(M)[None, :]
    inter = np.cos(2.0 * np.pi / M * places[:, :, None] * orders).sum(-1) / M
    high, low = split_np(inter)
    fine_cols = np.concatenate([high.T, low.T, high.T, low.T], 0)
    fold_cols = np.concatenate([high, low], 1)
    fine_rows = np.concatenate([high, low, high, low], 1).reshape(blocks, span, 4 * M)
    high_t = high.reshape(blocks, span, M).transpose(0, 2, 1)
    low_t = low.reshape(blocks, span, M).transpose(0, 2, 1)
    fold_rows = np.concatenate([high_t, low_t, high_t], 2)
    high, low = split_np(np.concatenate([rounded_cos, rounded_sin], 0))
    drop_rows = np.concatenate([high, low, high], 1)
    high, low = split_np(pair_table(coarse_cos, coarse_sin).T)
    drop_cols = np.concatenate([high, low, high], 0)
    rows = np.concatenate(
        [
            wide_cos.reshape(W, blocks, span).transpose(1, 2, 0),
            wide_sin.reshape(W, blocks, span).transpose(1, 2, 0),
        ],
        2,
    )
    high, low = split_np(rows / period)
    grad_rows = np.concatenate([high, low, high], 2)
    padded = [np.pad(part, ((0, M - W), (0, 0))) for part in (wide_cos, wide_sin)]
    high, low = split_np(np.concatenate(padded, 0))
    grad_cols = np.concatenate([high, low], 0)
    chapters = [
        dict(lift_cols=lift_cols, lift_rows=lift_rows),
        dict(fine_cols=fine_cols, fold_cols=fold_cols),
        dict(drop_rows=drop_rows, drop_cols=drop_cols),
        dict(grad_cols=grad_cols),
    ]
    for block in range(blocks):
        chapters.append(dict(fine_rows=fine_rows[block], fold_rows=fold_rows[block]))
    for block in range(blocks):
        chapters.append(dict(grad_rows=grad_rows[block]))
    pages, starts, places, at = [], [], {}, 0
    for chapter in chapters:
        starts.append(at)
        for name, value in chapter.items():
            places[name] = (at - starts[-1], value.shape)
            for lane in range(0, value.shape[1], LANES):
                page = value[:, lane : lane + LANES]
                pages.append(np.pad(page, ((0, 0), (0, LANES - page.shape[1]))))
                at += page.shape[0]
    starts.append(at)
    return spec_cols, spec_rows, Book(np.concatenate(pages, 0), starts, places, blocks)


class Book:
    def __init__(self, pages, starts, places, blocks):
        self.pages, self.starts, self.places, self.blocks = pages, starts, places, blocks

    def rows(self, chapter):
        return self.starts[chapter + 1] - self.starts[chapter]

    def shapes(self, *chapters):
        return [jax.ShapeDtypeStruct((self.rows(chapter), LANES), bf16) for chapter in chapters]

    def where(self, ref, chapter, block=0):
        return ref.at[pl.ds(self.starts[chapter] + block * self.rows(chapter), self.rows(chapter))]

    def read(self, ref, name):
        at, (rows, lanes) = self.places[name]
        pages = [
            ref[at + number * rows : at + (number + 1) * rows, : min(LANES, lanes - lane)]
            for number, lane in enumerate(range(0, lanes, LANES))
        ]
        return pages[0] if len(pages) == 1 else jnp.concatenate(pages, 1)


LIFT, FINE, DROP, GRAD, IMAGE_ROWS = range(5)


def dot(left, right):
    return jnp.dot(left, right, preferred_element_type=f32)


def split(value):
    high = value.astype(bf16)
    return high, (value - high.astype(f32)).astype(bf16)


def lane_of(shape):
    return lax.broadcasted_iota(jnp.int32, shape, len(shape) - 1)


def row_of(shape):
    return lax.broadcasted_iota(jnp.int32, shape, 0)


def swap(value):
    return pltpu.roll(value, M, 1)


def signs(rows, low, high):
    return jnp.where(lane_of((rows, LANES)) < M, f32(low), f32(high))


def my_block():
    return lax.axis_index("src") * lax.axis_size("pix") + lax.axis_index("pix")


def chip_blocks():
    pix, count = lax.axis_index("pix"), lax.axis_size("pix")
    base = lax.axis_index("src") * count
    return [base + jnp.bitwise_xor(pix, step) for step in range(count)]


def copies(sems, *pairs):
    out = [
        pltpu.make_async_copy(source, place, sems.at[number])
        for number, (source, place) in enumerate(pairs)
    ]
    for copy in out:
        copy.start()
    return out


def spectrum_kernel(
    mask_ref, pupil_ref, weight_ref, cell_ref, active_ref, class_ref, thresholds_ref,
    cols_ref, rows_ref,
    part_ref, sent_ref, threshold_ref,
    mask_in, pupil_in, weight_in, cell_in, active_in, thresholds, cols, rows,
    sems, lined, paired,
):
    (
        get_active, get_cell, get_pupil, get_weight, get_mask, get_cols, get_rows,
        get_thresholds,
    ) = copies(
        sems,
        (active_ref, active_in),
        (cell_ref, cell_in),
        (pupil_ref.at[pl.ds(0, 16)], pupil_in),
        (weight_ref, weight_in),
        (mask_ref.at[0], mask_in),
        (cols_ref, cols),
        (rows_ref.at[my_block()], rows),
        (thresholds_ref, thresholds),
    )
    get_active.wait()
    get_cell.wait()
    get_pupil.wait()
    get_weight.wait()
    active = active_in[lax.axis_index("src")]
    raw = pupil_in[...].astype(f32)[:8]
    raw = jnp.where(row_of(raw.shape) < active, raw, 0.0)
    for piece in range(16):
        lined[pl.ds(piece, 8, stride=16), :] = raw[:, piece * LANES : (piece + 1) * LANES]
    quarter = lane_of((8, LANES)) // K
    for pair in range(PAIRS):
        first, second = pair * 32, pair * 32 + 16
        quarters = [lined[pl.ds(start, 8), :] for start in (first, second, first + 8, second + 8)]
        for turn in range(4):
            moved = [
                value if number == turn else pltpu.roll(value, K * (number - turn) % LANES, 1)
                for number, value in enumerate(quarters)
            ]
            out = moved[3]
            for number in range(3):
                out = jnp.where(quarter == number, moved[number], out)
            paired[pl.ds(pair * K + turn, 8, stride=4), :] = out
    sent_ref[: PAIRS * K] = paired[...].astype(bf16)
    shape = (8, LANES)
    weights = jnp.broadcast_to(weight_in[...].astype(f32).reshape(1, -1)[:, :LANES], shape)
    column = jnp.sum(jnp.where(row_of(shape) == lane_of(shape), weights, 0.0), 1, keepdims=True)
    column = jnp.broadcast_to(column, shape)
    tail = [column]
    for pair in range(PAIRS):
        even = lane_of((1, LANES)) // K % 2 == 0
        tail.append(jnp.where(even, column[2 * pair : 2 * pair + 1], column[2 * pair + 1 : 2 * pair + 2]))
    tail.append(jnp.zeros((1, LANES), f32))
    place = lane_of((1, LANES))
    row_code, col_code = jnp.zeros((1, LANES), f32), jnp.zeros((1, LANES), f32)
    for slot in range(MOST):
        cell = cell_in[slot]
        row_code = jnp.where(place == slot, lax.div(cell, SG).astype(f32), row_code)
        col_code = jnp.where(place == slot, lax.rem(cell, SG).astype(f32), col_code)
    tail += [row_code, col_code, jnp.zeros((2, LANES), f32)]
    sent_ref[PAIRS * K :] = jnp.concatenate(tail, 0).astype(bf16)
    get_mask.wait()
    get_cols.wait()
    get_rows.wait()
    high, low = split(mask_in[...])
    both = dot(high, cols[...])
    part = both[:, :LANES] + both[:, LANES:] + dot(low, cols[:, :LANES])
    turned = swap(part) * signs(part.shape[0], 1.0, -1.0)
    high, low = split(jnp.concatenate([part, turned], 0))
    product = dot(rows[...], jnp.concatenate([high, low], 1))
    part_ref[...] = product[:W, :LANES] + product[:W, LANES:] + product[W:, :LANES]
    get_thresholds.wait()
    kind = class_ref[0]
    threshold = thresholds[0]
    for number in range(1, CLASSES):
        threshold = jnp.where(kind == number, thresholds[number], threshold)
    threshold_ref[...] = jnp.full(threshold_ref.shape, threshold, f32)


def pack_kernel(part_ref, *refs):
    *other_refs, sent_ref, out_ref = refs
    part = part_ref[...]
    for ref in other_refs:
        part = part + ref[...]
    high, low = split(part)
    out_ref[:W] = high
    out_ref[W : 2 * W] = low
    out_ref[AT_PUPILS:] = sent_ref[...]


def stage_kernel(book, target_ref, book_ref, *refs):
    *out_refs, sems = refs
    target_out, lift_out, fine_out, drop_out, grad_out, grad_rows_out, *rows_out = out_refs
    gets = copies(
        sems,
        (book.where(book_ref, LIFT), lift_out),
        (book.where(book_ref, FINE), fine_out),
        (target_ref.at[0], target_out),
        *(
            (book.where(book_ref, IMAGE_ROWS, block), out)
            for block, out in zip(chip_blocks(), rows_out)
        ),
        (book.where(book_ref, DROP), drop_out),
        (book.where(book_ref, GRAD), grad_out),
        (book.where(book_ref, IMAGE_ROWS + book.blocks, my_block()), grad_rows_out),
    )
    for get in gets:
        get.wait()


def over_owners(refs, body, carry):
    if len(refs) > 1:
        return body(carry, [(ref, place) for place, ref in enumerate(refs)])
    (ref,) = refs
    return lax.fori_loop(
        0, ref.shape[0], lambda owner, carry: body(carry, [(ref.at[owner], owner)]), carry
    )


def codes_of(refs, codes_v):
    def body(none, items):
        for ref, place in items:
            tail = ref[pl.ds(AT_TAIL, 16), :].astype(f32)
            code = tail[TAIL_CELL : TAIL_CELL + 1] * 32.0 + tail[TAIL_CELL + 1 : TAIL_CELL + 2]
            codes_v[pl.ds(place, 1), :] = code.astype(jnp.int32)
        return none

    over_owners(refs, body, 0)


def window_of(codes, place, slot):
    code = codes[place, slot]
    return lax.div(code, 32), lax.rem(code, 32)


def pair_parts(ref, pair):
    value = ref[pl.ds(AT_PUPILS + pair * K, K), :].astype(f32)
    other = swap(value)
    low = lane_of(value.shape) < M
    return jnp.where(low, value, other), jnp.where(low, other, value)


def slot_lanes(rows):
    return lane_of((rows, LANES)) // K % 2 == 0


def image_kernel(book, n_sent, n_pix, *refs):
    sent_refs, refs = refs[:n_sent], refs[n_sent:]
    targets, refs = refs[:n_pix], refs[n_pix:]
    rows_refs, refs = refs[:n_pix], refs[n_pix:]
    (
        threshold_ref, lift, fine,
        intensity_ref, fields, *fold_refs,
        sems, codes_v, codes, spectrum, intensity_out,
    ) = refs
    codes_of(sent_refs, codes_v)
    (get_codes,) = copies(sems, (codes_v, codes))

    def gather(total, items):
        for ref, place in items:
            total = total + (ref[:W].astype(f32) + ref[W : 2 * W].astype(f32))
        return total

    spectrum[...] = over_owners(sent_refs, gather, jnp.zeros((W, LANES), f32))
    get_codes.wait()
    lift_cols, lift_rows = book.read(lift, "lift_cols"), book.read(lift, "lift_rows")
    even = slot_lanes(K)
    turn_low = signs(K, -1.0, 1.0)
    turn = signs(M, -1.0, 1.0)

    def forward(total, items):
        waves = []
        for ref, place in items:
            for pair in range(PAIRS):
                real, imag = pair_parts(ref, pair)
                row, col = window_of(codes, place, 2 * pair)
                left = pltpu.roll(spectrum[pl.ds(row, K), :], lax.rem(LANES - col, LANES), 1)
                row, col = window_of(codes, place, 2 * pair + 1)
                right = pltpu.roll(spectrum[pl.ds(row, K), :], lax.rem(LANES + K - col, LANES), 1)
                window = jnp.where(even, left, right)
                waves.append((real * window + imag * (turn_low * swap(window))).astype(bf16))
        wave = jnp.concatenate(waves, 0)
        high, low = split(dot(jnp.concatenate([wave, wave], 1), lift_cols))
        number = 0
        for ref, place in items:
            weights = ref[pl.ds(AT_TAIL, 16), :].astype(f32)
            for pair in range(PAIRS):
                here = slice(number * K, (number + 1) * K)
                number += 1
                raw = dot(lift_rows, jnp.concatenate([high[here], high[here], low[here]], 0))
                for slot in range(2):
                    mine = raw[:, slot * LANES : (slot + 1) * LANES]
                    field = mine[:M] + turn * swap(mine[M:])
                    fields[place * MOST + 2 * pair + slot] = field
                    at = 2 * pair + slot
                    total = total + weights[at : at + 1] * (field * field)
        return total

    power = over_owners(sent_refs, forward, jnp.zeros((M, LANES), f32))
    high, low = split(power + swap(power))
    coarse = jnp.concatenate([high, high, low, low], 0)
    fine_cols, fold_cols = book.read(fine, "fine_cols"), book.read(fine, "fold_cols")
    threshold = threshold_ref[:1, :1]
    grid = jnp.zeros((M, LANES), f32)
    for number, (target, rows_ref) in enumerate(zip(targets, rows_refs)):
        high, low = split(dot(book.read(rows_ref, "fine_rows"), coarse))
        intensity = dot(jnp.concatenate([high, low], 1), fine_cols)
        if number == 0:
            intensity_out[...] = intensity
            put = pltpu.make_async_copy(intensity_out, intensity_ref.at[0], sems.at[1])
            put.start()
        resist = 1.0 / (1.0 + jnp.exp(-STEEP * (intensity - threshold)))
        slope = (2.0 * STEEP * (resist - target[...]) * resist * (1.0 - resist)).astype(bf16)
        folded = dot(slope, fold_cols)
        high, low = split(folded + swap(folded))
        grid = grid + dot(
            book.read(rows_ref, "fold_rows"), jnp.concatenate([high, high, low], 0)
        )
    lane = lane_of((M // 2, LANES))
    packed = jnp.where(lane < M, grid[: M // 2], grid[M // 2 :])
    for fold_ref in fold_refs:
        fold_ref[: M // 2] = packed

    def weigh(none, items):
        for ref, place in items:
            sums = []
            for slot in range(MOST):
                field = fields[place * MOST + slot]
                sums.append(jnp.sum(grid * (field * field), 0, keepdims=True))
            sums = jnp.concatenate(sums + [jnp.zeros((SUMS - MOST, LANES), f32)], 0)
            if len(fold_refs) > 1:
                fold_refs[place][M // 2 :] = sums
            else:
                start = pl.multiple_of(M // 2 + place * SUMS, SUMS)
                fold_refs[0][pl.ds(start, SUMS), :] = sums
        return none

    over_owners(sent_refs, weigh, 0)
    put.wait()


def gradient_kernel(book, n_fold, n_sent, *refs):
    fold_refs, refs = refs[:n_fold], refs[n_fold:]
    sent_refs, refs = refs[:n_sent], refs[n_sent:]
    (
        fields, drop, grad_table, rows_table,
        mask_grad_ref,
        sems, codes_v, codes, sums, mask_grad_out,
    ) = refs
    codes_of(sent_refs, codes_v)
    (get_codes,) = copies(sems, (codes_v, codes))
    packed = fold_refs[0][: M // 2]
    for ref in fold_refs[1:]:
        packed = packed + ref[: M // 2]
    other = swap(packed)
    low_half = lane_of(packed.shape) < M
    grid = jnp.concatenate(
        [jnp.where(low_half, packed, other), jnp.where(low_half, other, packed)], 0
    )
    for number in range(2):
        sums[number] = jnp.zeros((W, LANES), f32)
    turn = signs(K, 1.0, -1.0)
    even = slot_lanes(K)
    real_or_imag = lane_of((K, LANES)) % M < K
    get_codes.wait()
    drop_rows, drop_cols = book.read(drop, "drop_rows"), book.read(drop, "drop_cols")

    def backward(none, items):
        waves = []
        for ref, place in items:
            for pair in range(PAIRS):
                scaled = [grid * fields[place * MOST + 2 * pair + slot] for slot in range(2)]
                high, low = split(jnp.concatenate(scaled, 1))
                raw = dot(drop_rows, jnp.concatenate([high, high, low], 0))
                wave = []
                for slot in range(2):
                    mine = raw[:, slot * LANES : (slot + 1) * LANES]
                    wave.append(mine[:K] + turn * swap(mine[K:]))
                waves.append(jnp.concatenate(wave, 1))
        high, low = split(jnp.concatenate(waves, 0))
        back = dot(jnp.concatenate([high, high, low], 1), drop_cols)
        number = 0
        for ref, place in items:
            weights = ref[pl.ds(AT_TAIL, 16), :].astype(f32) * (2.0 / K)
            for pair in range(PAIRS):
                mine = back[number * K : (number + 1) * K]
                number += 1
                real, imag = pair_parts(ref, pair)
                product = real * mine + imag * (turn * swap(mine))
                product = weights[TAIL_PAIR + pair : TAIL_PAIR + pair + 1] * product
                for slot in range(2):
                    row, col = window_of(codes, place, 2 * pair + slot)
                    keep = even if slot == 0 else jnp.logical_not(even)
                    shift = lax.rem(col + LANES - slot * K, LANES)
                    moved = pltpu.roll(jnp.where(keep, product, 0.0), shift, 1)
                    sums[slot, pl.ds(row, K), :] += moved
        return none

    over_owners(sent_refs, backward, 0)
    grad_cols = book.read(grad_table, "grad_cols")
    grad = sums[0] + sums[1]
    turn = signs(W, 1.0, -1.0)
    high, low = split(jnp.concatenate([grad * turn, -swap(grad)], 0))
    half = dot(book.read(rows_table, "grad_rows"), jnp.concatenate([high, high, low], 0))
    high, low = split(half)
    both = jnp.concatenate([high, high], 1)
    chunk = grad_cols.shape[1] // PIECES
    puts = []
    for piece in range(PIECES):
        here = slice(piece * chunk, (piece + 1) * chunk)
        mask_grad_out[:, here] = dot(both, grad_cols[:, here]) + dot(low, grad_cols[:LANES, here])
        place = mask_grad_ref.at[0, :, pl.ds(piece * chunk, chunk)]
        puts.append(
            pltpu.make_async_copy(mask_grad_out.at[:, pl.ds(piece * chunk, chunk)], place, sems.at[1 + piece])
        )
        puts[-1].start()
    for put in puts:
        put.wait()


VMEM = pl.BlockSpec(memory_space=pltpu.VMEM)
SMEM = pl.BlockSpec(memory_space=pltpu.SMEM)
HBM = pl.BlockSpec(memory_space=pltpu.HBM)


def room(kib):
    return pltpu.CompilerParams(vmem_limit_bytes=(64 * 1024 - kib) * 1024)


def in_hbm(value):
    return pltpu.with_memory_space_constraint(value, pltpu.HBM)


def exchange(value, axis, step):
    return lax.ppermute(value, axis, [(i, i ^ step) for i in range(lax.axis_size(axis))])


def others(value, axis):
    return [exchange(value, axis, step) for step in range(1, lax.axis_size(axis))]


def like(value):
    return pltpu.VMEM(value.shape, value.dtype)


def shards(
    mask, target, tile_class, thresholds, source_pupil, source_weight, source_cell, active_count
):
    span, period = mask.shape[1:]
    slots = source_pupil.shape[0]
    src_count = lax.axis_size("src")
    few = src_count in (2, 4)
    spec_cols, spec_rows, book = tables(period, span)
    pages = jnp.asarray(book.pages)
    src = lax.axis_index("src")
    sems = pltpu.SemaphoreType.DMA
    smem = pltpu.SMEM

    part, sent, threshold = pl.pallas_call(
        spectrum_kernel,
        in_specs=[HBM] * 5 + [SMEM] + [HBM] * 3,
        out_specs=[VMEM] * 3,
        out_shape=[
            jax.ShapeDtypeStruct((W, LANES), f32),
            jax.ShapeDtypeStruct((ROWS - AT_PUPILS, LANES), bf16),
            jax.ShapeDtypeStruct((8, LANES), f32),
        ],
        scratch_shapes=[
            like(mask[0]),
            like(source_pupil[:16]),
            like(source_weight),
            smem(source_cell.shape, jnp.int32),
            smem(active_count.shape, jnp.int32),
            smem(thresholds.shape, f32),
            like(spec_cols),
            like(spec_rows[0]),
            sems((8,)),
            pltpu.VMEM((LANES, LANES), f32),
            pltpu.VMEM((PAIRS * K, LANES), f32),
        ],
        compiler_params=room(24576),
        name="spectrum",
    )(
        *map(in_hbm, (mask, source_pupil, source_weight, source_cell, active_count)),
        tile_class,
        *map(in_hbm, (thresholds, jnp.asarray(spec_cols), jnp.asarray(spec_rows))),
    )
    from_pix = others(part, "pix")
    sent = pl.pallas_call(
        pack_kernel,
        in_specs=[VMEM] * (2 + len(from_pix)),
        out_specs=VMEM,
        out_shape=jax.ShapeDtypeStruct((ROWS, LANES), bf16),
        compiler_params=room(32768),
        name="pack",
    )(part, *from_pix, sent)
    if few:
        parcels = [sent] + others(sent, "src")
    else:
        parcels = [lax.all_gather(sent, "src")]

    late_target, late_pages, _ = lax.optimization_barrier((target, pages, sent))
    staged_shapes = [
        jax.ShapeDtypeStruct((span, period), f32),
        *book.shapes(LIFT, FINE, DROP, GRAD, IMAGE_ROWS + book.blocks),
        *book.shapes(IMAGE_ROWS) * lax.axis_size("pix"),
    ]
    staged = pl.pallas_call(
        functools.partial(stage_kernel, book),
        in_specs=[HBM] * 2,
        out_specs=[VMEM] * len(staged_shapes),
        out_shape=staged_shapes,
        scratch_shapes=[sems((len(staged_shapes),))],
        compiler_params=room(24576),
        name="stage",
    )(in_hbm(late_target), in_hbm(late_pages))
    near_target, lift, fine, *for_gradient = staged[:6]
    early_target, _ = lax.optimization_barrier((target, from_pix[0]))
    targets = [near_target] + others(early_target[0], "pix")
    image_rows = staged[6:]

    numbers = src_count * MOST
    owners_up = -(-src_count // 8) * 8
    fold_rows = M // 2 + (1 if few else src_count) * SUMS
    fold_count = src_count if few else 1
    codes = [pltpu.VMEM((owners_up, LANES), jnp.int32), smem((owners_up, LANES), jnp.int32)]
    intensity, fields, *folded = pl.pallas_call(
        functools.partial(image_kernel, book, len(parcels), len(targets)),
        in_specs=[VMEM] * (len(parcels) + 2 * len(targets) + 3),
        out_specs=[HBM, VMEM] + [VMEM] * fold_count,
        out_shape=[
            jax.ShapeDtypeStruct((1, span, period), f32),
            jax.ShapeDtypeStruct((numbers, M, LANES), f32),
            *[jax.ShapeDtypeStruct((fold_rows, LANES), f32)] * fold_count,
        ],
        scratch_shapes=[
            sems((2,)),
            *codes,
            pltpu.VMEM((W, LANES), f32),
            like(target[0]),
        ],
        compiler_params=room(24576),
        name="image",
    )(*parcels, *targets, *image_rows, threshold, lift, fine)

    if few:
        folds = [
            value if step == 0 else exchange(value, "src", step)
            for step, value in enumerate(folded)
        ]
        rows = sum(fold[M // 2 :] for fold in folds)
    else:
        folds = [lax.psum(folded[0], "src")]
        rows = lax.dynamic_slice_in_dim(folds[0], M // 2 + src * SUMS, SUMS, 0)
    for other in others(rows, "tile"):
        rows = rows + other
    mask_grad = pl.pallas_call(
        functools.partial(gradient_kernel, book, len(folds), len(parcels)),
        in_specs=[VMEM] * (len(folds) + len(parcels) + 1 + len(for_gradient)),
        out_specs=HBM,
        out_shape=jax.ShapeDtypeStruct((1, span, period), f32),
        scratch_shapes=[
            sems((1 + PIECES,)),
            *codes,
            pltpu.VMEM((2, W, LANES), f32),
            like(mask[0]),
        ],
        compiler_params=room(24576),
        name="gradient",
    )(*folds, *parcels, fields, *for_gradient)
    sums = jnp.sum(rows, 1) * (1.0 / (period * K))
    source_grad = jnp.zeros((slots,), f32).at[:SUMS].set(sums)
    return intensity, mask_grad, source_grad


def solution(mesh):
    in_specs = (
        P(("groups", "tile"), ("src", "pix"), None),
        P(("groups", "tile"), ("src", "pix"), None),
        P(("groups", "tile")),
        P(),
        P("src", None),
        P("src"),
        P("src"),
        P(),
    )
    out_specs = (
        P(("groups", "tile"), ("src", "pix"), None),
        P(("groups", "tile"), ("src", "pix"), None),
        P(("groups", "src")),
    )
    return jax.shard_map(shards, mesh=mesh, in_specs=in_specs, out_specs=out_specs, check_vma=False)
```

```python
import functools

import jax
import jax.numpy as jnp
import ml_dtypes
import numpy as np
from jax import lax
from jax.experimental import pallas as pl
from jax.experimental.pallas import tpu as pltpu
from jax.sharding import PartitionSpec as P

K = 32
SG = 17
W = 48
MOST = 6
CLASSES = 4
STEEP = 4.0

M = 64
LANES = 128
PAIRS = MOST // 2
AT_PUPILS = W
AT_TAIL = AT_PUPILS + PAIRS * K
ROWS = AT_TAIL + 16
TAIL_PAIR, TAIL_CELL = 8, 12
PIECES = 4
SUMS = 8

f32 = jnp.float32
bf16 = jnp.bfloat16


def split_np(table):
    table = np.asarray(table, np.float32)
    high = table.astype(ml_dtypes.bfloat16)
    low = (table - high.astype(np.float32)).astype(ml_dtypes.bfloat16)
    return high, low


def halves(left, right):
    out = np.zeros((left.shape[0], LANES))
    out[:, : left.shape[1]] = left
    out[:, M : M + right.shape[1]] = right
    return out


@functools.lru_cache(maxsize=None)
def tables(period, span):
    blocks = period // span
    freqs = np.arange(W) - W // 2
    pixels = np.arange(period)
    wide = 2.0 * np.pi / period * ((freqs[:, None] * pixels[None, :]) % period)
    wide_cos, wide_sin = np.cos(wide), np.sin(wide)
    narrow = np.arange(K) - K // 2
    coarse = 2.0 * np.pi / M * ((narrow[:, None] * np.arange(M)[None, :]) % M)
    coarse_cos, coarse_sin = np.cos(coarse), np.sin(coarse)
    near = 2.0 * np.pi / period * ((narrow[:, None] * pixels[None, :]) % period)
    gain = sum(
        (wave * wave.astype(np.float32).astype(ml_dtypes.bfloat16).astype(np.float64)).mean(1)
        for wave in (np.cos(near), np.sin(near))
    )
    rounded_cos, rounded_sin = gain[:, None] * coarse_cos, gain[:, None] * coarse_sin
    high, low = split_np(halves(wide_cos.T, -wide_sin.T))
    spec_cols = np.concatenate([high, low], 1)
    rows = np.concatenate(
        [wide_cos.reshape(W, blocks, span), wide_sin.reshape(W, blocks, span)], 2
    ).transpose(1, 0, 2)
    high, low = split_np(rows / period)
    spec_rows = np.concatenate([high, low], 1)
    def pair_table(cos, sin):
        out = np.zeros((4 * K, 4 * M))
        for slot in range(2):
            real, imag, at = slot * K, (2 + slot) * K, slot * 2 * M
            out[real : real + K, at : at + 2 * M] = np.concatenate([cos, sin], 1)
            out[imag : imag + K, at : at + 2 * M] = np.concatenate([-sin, cos], 1)
        return out

    lift = pair_table(rounded_cos, rounded_sin)
    turned = pair_table(-rounded_sin, rounded_cos)
    high, low = split_np(np.concatenate([lift, turned], 1))
    lift_cols = np.concatenate([high, low], 0)
    lift_rows = np.concatenate(split_np(rounded_cos.T / K) + split_np(rounded_sin.T / K), 1)
    orders = np.arange(-(M // 2 - 1), M // 2)
    places = pixels[:, None] * (M / period) - np.arange(M)[None, :]
    inter = np.cos(2.0 * np.pi / M * places[:, :, None] * orders).sum(-1) / M
    high, low = split_np(inter)
    fine_cols = np.concatenate([high.T, low.T, high.T, low.T], 0)
    fold_cols = np.concatenate([high, low], 1)
    fine_rows = np.concatenate([high, low, high, low], 1).reshape(blocks, span, 4 * M)
    high_t = high.reshape(blocks, span, M).transpose(0, 2, 1)
    low_t = low.reshape(blocks, span, M).transpose(0, 2, 1)
    fold_rows = np.concatenate([high_t, low_t, high_t], 2)
    high, low = split_np(np.concatenate([rounded_cos, rounded_sin], 0))
    drop_rows = np.concatenate([high, low], 1)
    drop = pair_table(coarse_cos, coarse_sin).T
    drop = np.concatenate([drop, drop[:, M:], -drop[:, :M]], 1)
    high, low = split_np(drop)
    drop_cols = np.concatenate([high, low, high], 0)
    rows = np.concatenate(
        [
            wide_cos.reshape(W, blocks, span).transpose(1, 2, 0),
            wide_sin.reshape(W, blocks, span).transpose(1, 2, 0),
        ],
        2,
    )
    high, low = split_np(rows / period)
    grad_rows = np.concatenate([high, low, high], 2)
    padded = [np.pad(part, ((0, M - W), (0, 0))) for part in (wide_cos, wide_sin)]
    high, low = split_np(np.concatenate(padded, 0))
    grad_cols = np.concatenate([high, low], 0)
    chapters = [
        dict(lift_cols=lift_cols, lift_rows=lift_rows),
        dict(fine_cols=fine_cols, fold_cols=fold_cols),
        dict(drop_rows=drop_rows, drop_cols=drop_cols),
        dict(grad_cols=grad_cols),
    ]
    for block in range(blocks):
        chapters.append(dict(fine_rows=fine_rows[block], fold_rows=fold_rows[block]))
    for block in range(blocks):
        chapters.append(dict(grad_rows=grad_rows[block]))
    pages, starts, places, at = [], [], {}, 0
    for chapter in chapters:
        starts.append(at)
        for name, value in chapter.items():
            places[name] = (at - starts[-1], value.shape)
            for lane in range(0, value.shape[1], LANES):
                page = value[:, lane : lane + LANES]
                pages.append(np.pad(page, ((0, 0), (0, LANES - page.shape[1]))))
                at += page.shape[0]
    starts.append(at)
    return spec_cols, spec_rows, Book(np.concatenate(pages, 0), starts, places, blocks)


class Book:
    def __init__(self, pages, starts, places, blocks):
        self.pages, self.starts, self.places, self.blocks = pages, starts, places, blocks

    def rows(self, chapter):
        return self.starts[chapter + 1] - self.starts[chapter]

    def shapes(self, *chapters):
        return [jax.ShapeDtypeStruct((self.rows(chapter), LANES), bf16) for chapter in chapters]

    def where(self, ref, chapter, block=0):
        return ref.at[pl.ds(self.starts[chapter] + block * self.rows(chapter), self.rows(chapter))]

    def read(self, ref, name):
        at, (rows, lanes) = self.places[name]
        pages = [
            ref[at + number * rows : at + (number + 1) * rows, : min(LANES, lanes - lane)]
            for number, lane in enumerate(range(0, lanes, LANES))
        ]
        return pages[0] if len(pages) == 1 else jnp.concatenate(pages, 1)


LIFT, FINE, DROP, GRAD, IMAGE_ROWS = range(5)


def dot(left, right):
    return jnp.dot(left, right, preferred_element_type=f32)


def split(value):
    high = value.astype(bf16)
    return high, (value - high.astype(f32)).astype(bf16)


def lane_of(shape):
    return lax.broadcasted_iota(jnp.int32, shape, len(shape) - 1)


def row_of(shape):
    return lax.broadcasted_iota(jnp.int32, shape, 0)


def swap(value):
    return pltpu.roll(value, M, 1)


def signs(rows, low, high):
    return jnp.where(lane_of((rows, LANES)) < M, f32(low), f32(high))


def my_block():
    return lax.axis_index("src") * lax.axis_size("pix") + lax.axis_index("pix")


def chip_blocks():
    pix, count = lax.axis_index("pix"), lax.axis_size("pix")
    base = lax.axis_index("src") * count
    return [base + jnp.bitwise_xor(pix, step) for step in range(count)]


def copies(sems, *pairs):
    out = [
        pltpu.make_async_copy(source, place, sems.at[number])
        for number, (source, place) in enumerate(pairs)
    ]
    for copy in out:
        copy.start()
    return out


def spectrum_kernel(
    mask_ref, pupil_ref, weight_ref, cell_ref, active_ref, class_ref, thresholds_ref,
    cols_ref, rows_ref,
    part_ref, sent_ref, threshold_ref,
    mask_in, pupil_in, weight_in, cell_in, active_in, thresholds, cols, rows,
    sems, lined, paired,
):
    (
        get_active, get_cell, get_pupil, get_weight, get_mask, get_cols, get_rows,
        get_thresholds,
    ) = copies(
        sems,
        (active_ref, active_in),
        (cell_ref, cell_in),
        (pupil_ref.at[pl.ds(0, 16)], pupil_in),
        (weight_ref, weight_in),
        (mask_ref.at[0], mask_in),
        (cols_ref, cols),
        (rows_ref.at[my_block()], rows),
        (thresholds_ref, thresholds),
    )
    get_active.wait()
    get_cell.wait()
    get_pupil.wait()
    get_weight.wait()
    active = active_in[lax.axis_index("src")]
    raw = pupil_in[...].astype(f32)[:8]
    raw = jnp.where(row_of(raw.shape) < active, raw, 0.0)
    for piece in range(16):
        lined[pl.ds(piece, 8, stride=16), :] = raw[:, piece * LANES : (piece + 1) * LANES]
    quarter = lane_of((8, LANES)) // K
    for pair in range(PAIRS):
        first, second = pair * 32, pair * 32 + 16
        quarters = [lined[pl.ds(start, 8), :] for start in (first, second, first + 8, second + 8)]
        for turn in range(4):
            moved = [
                value if number == turn else pltpu.roll(value, K * (number - turn) % LANES, 1)
                for number, value in enumerate(quarters)
            ]
            out = moved[3]
            for number in range(3):
                out = jnp.where(quarter == number, moved[number], out)
            paired[pl.ds(pair * K + turn, 8, stride=4), :] = out
    sent_ref[: PAIRS * K] = paired[...].astype(bf16)
    shape = (8, LANES)
    weights = jnp.broadcast_to(weight_in[...].astype(f32).reshape(1, -1)[:, :LANES], shape)
    column = jnp.sum(jnp.where(row_of(shape) == lane_of(shape), weights, 0.0), 1, keepdims=True)
    column = jnp.broadcast_to(column, shape)
    tail = [column]
    for pair in range(PAIRS):
        even = lane_of((1, LANES)) // K % 2 == 0
        tail.append(jnp.where(even, column[2 * pair : 2 * pair + 1], column[2 * pair + 1 : 2 * pair + 2]))
    tail.append(jnp.zeros((1, LANES), f32))
    place = lane_of((1, LANES))
    row_code, col_code = jnp.zeros((1, LANES), f32), jnp.zeros((1, LANES), f32)
    for slot in range(MOST):
        cell = cell_in[slot]
        row_code = jnp.where(place == slot, lax.div(cell, SG).astype(f32), row_code)
        col_code = jnp.where(place == slot, lax.rem(cell, SG).astype(f32), col_code)
    tail += [row_code, col_code, jnp.zeros((2, LANES), f32)]
    sent_ref[PAIRS * K :] = jnp.concatenate(tail, 0).astype(bf16)
    get_mask.wait()
    get_cols.wait()
    get_rows.wait()
    high, low = split(mask_in[...])
    both = dot(high, cols[...])
    part = both[:, :LANES] + both[:, LANES:] + dot(low, cols[:, :LANES])
    turned = swap(part) * signs(part.shape[0], 1.0, -1.0)
    high, low = split(jnp.concatenate([part, turned], 0))
    product = dot(rows[...], jnp.concatenate([high, low], 1))
    part_ref[...] = product[:W, :LANES] + product[:W, LANES:] + product[W:, :LANES]
    get_thresholds.wait()
    kind = class_ref[0]
    threshold = thresholds[0]
    for number in range(1, CLASSES):
        threshold = jnp.where(kind == number, thresholds[number], threshold)
    threshold_ref[...] = jnp.full(threshold_ref.shape, threshold, f32)


def pack_kernel(part_ref, *refs):
    *other_refs, sent_ref, out_ref = refs
    part = part_ref[...]
    for ref in other_refs:
        part = part + ref[...]
    high, low = split(part)
    rest = pltpu.roll(low.astype(f32), K, 1)
    out_ref[:W] = jnp.where(lane_of(part.shape) % M < W, high.astype(f32), rest).astype(bf16)
    out_ref[AT_PUPILS:] = sent_ref[...]


def stage_kernel(book, target_ref, book_ref, *refs):
    *out_refs, sems = refs
    target_out, lift_out, fine_out, drop_out, grad_out, grad_rows_out, *rows_out = out_refs
    gets = copies(
        sems,
        (book.where(book_ref, LIFT), lift_out),
        (book.where(book_ref, FINE), fine_out),
        (target_ref.at[0], target_out),
        *(
            (book.where(book_ref, IMAGE_ROWS, block), out)
            for block, out in zip(chip_blocks(), rows_out)
        ),
        (book.where(book_ref, DROP), drop_out),
        (book.where(book_ref, GRAD), grad_out),
        (book.where(book_ref, IMAGE_ROWS + book.blocks, my_block()), grad_rows_out),
    )
    for get in gets:
        get.wait()


def over_owners(refs, body, carry):
    if len(refs) > 1:
        return body(carry, [(ref, place) for place, ref in enumerate(refs)])
    (ref,) = refs
    return lax.fori_loop(
        0, ref.shape[0], lambda owner, carry: body(carry, [(ref.at[owner], owner)]), carry
    )


def codes_of(refs, codes_v):
    def body(none, items):
        for ref, place in items:
            tail = ref[pl.ds(AT_TAIL, 16), :].astype(f32)
            code = tail[TAIL_CELL : TAIL_CELL + 1] * 32.0 + tail[TAIL_CELL + 1 : TAIL_CELL + 2]
            codes_v[pl.ds(place, 1), :] = code.astype(jnp.int32)
        return none

    over_owners(refs, body, 0)


def window_of(codes, place, slot):
    code = codes[place, slot]
    return lax.div(code, 32), lax.rem(code, 32)


def pair_parts(ref, pair):
    value = ref[pl.ds(AT_PUPILS + pair * K, K), :].astype(f32)
    other = swap(value)
    low = lane_of(value.shape) < M
    return jnp.where(low, value, other), jnp.where(low, other, value)


def slot_lanes(rows):
    return lane_of((rows, LANES)) // K % 2 == 0


def image_kernel(book, n_sent, n_pix, *refs):
    sent_refs, refs = refs[:n_sent], refs[n_sent:]
    targets, refs = refs[:n_pix], refs[n_pix:]
    rows_refs, refs = refs[:n_pix], refs[n_pix:]
    (
        threshold_ref, lift, fine,
        intensity_ref, fields, *fold_refs,
        sems, codes_v, codes, spectrum, intensity_out,
    ) = refs
    codes_of(sent_refs, codes_v)
    (get_codes,) = copies(sems, (codes_v, codes))

    def gather(total, items):
        for ref, place in items:
            value = ref[:W].astype(f32)
            rest = jnp.where(lane_of(value.shape) % M < W, 0.0, value)
            total = total + (value + pltpu.roll(rest, LANES - K, 1))
        return total

    spectrum[...] = over_owners(sent_refs, gather, jnp.zeros((W, LANES), f32))
    get_codes.wait()
    lift_cols, lift_rows = book.read(lift, "lift_cols"), book.read(lift, "lift_rows")
    even = slot_lanes(K)
    turn_low = signs(K, -1.0, 1.0)

    def forward(total, items):
        waves = []
        for ref, place in items:
            for pair in range(PAIRS):
                real, imag = pair_parts(ref, pair)
                row, col = window_of(codes, place, 2 * pair)
                left = pltpu.roll(spectrum[pl.ds(row, K), :], lax.rem(LANES - col, LANES), 1)
                row, col = window_of(codes, place, 2 * pair + 1)
                right = pltpu.roll(spectrum[pl.ds(row, K), :], lax.rem(LANES + K - col, LANES), 1)
                window = jnp.where(even, left, right)
                waves.append((real * window + imag * (turn_low * swap(window))).astype(bf16))
        wave = jnp.concatenate(waves, 0)
        wave = dot(jnp.concatenate([wave, wave], 1), lift_cols).astype(bf16)
        number = 0
        for ref, place in items:
            weights = ref[pl.ds(AT_TAIL, 16), :].astype(f32)
            for pair in range(PAIRS):
                here = slice(number * K, (number + 1) * K)
                number += 1
                own, turned = wave[here, : 2 * LANES], wave[here, 2 * LANES :]
                raw = dot(lift_rows, jnp.concatenate([own, own, turned, turned], 0))
                for slot in range(2):
                    field = raw[:, slot * LANES : (slot + 1) * LANES]
                    fields[place * MOST + 2 * pair + slot] = field
                    at = 2 * pair + slot
                    total = total + weights[at : at + 1] * (field * field)
        return total

    power = over_owners(sent_refs, forward, jnp.zeros((M, LANES), f32))
    high, low = split(power + swap(power))
    coarse = jnp.concatenate([high, high, low, low], 0)
    fine_cols, fold_cols = book.read(fine, "fine_cols"), book.read(fine, "fold_cols")
    threshold = threshold_ref[:1, :1]
    grid = jnp.zeros((M, LANES), f32)
    fine_rows = [book.read(rows_ref, "fine_rows") for rows_ref in rows_refs]
    high, low = split(dot(jnp.concatenate(fine_rows, 0), coarse))
    intensities = dot(jnp.concatenate([high, low], 1), fine_cols)
    span = intensity_out.shape[0]
    intensity_out[...] = intensities[:span]
    put = pltpu.make_async_copy(intensity_out, intensity_ref.at[0], sems.at[1])
    put.start()
    slopes = []
    for number, target in enumerate(targets):
        intensity = intensities[number * span : (number + 1) * span]
        resist = 1.0 / (1.0 + jnp.exp(-STEEP * (intensity - threshold)))
        slope = 2.0 * STEEP * (resist - target[...]) * resist * (1.0 - resist)
        slopes.append(slope.astype(bf16))
    folded = dot(jnp.concatenate(slopes, 0), fold_cols)
    high, low = split(folded + swap(folded))
    for number, rows_ref in enumerate(rows_refs):
        here = slice(number * span, (number + 1) * span)
        grid = grid + dot(
            book.read(rows_ref, "fold_rows"),
            jnp.concatenate([high[here], high[here], low[here]], 0),
        )
    lane = lane_of((M // 2, LANES))
    packed = jnp.where(lane < M, grid[: M // 2], grid[M // 2 :])
    for fold_ref in fold_refs:
        fold_ref[: M // 2] = packed

    def weigh(none, items):
        for ref, place in items:
            sums = []
            for slot in range(MOST):
                field = fields[place * MOST + slot]
                sums.append(jnp.sum(grid * (field * field), 0, keepdims=True))
            sums = jnp.concatenate(sums + [jnp.zeros((SUMS - MOST, LANES), f32)], 0)
            if len(fold_refs) > 1:
                fold_refs[place][M // 2 :] = sums
            else:
                start = pl.multiple_of(M // 2 + place * SUMS, SUMS)
                fold_refs[0][pl.ds(start, SUMS), :] = sums
        return none

    over_owners(sent_refs, weigh, 0)
    put.wait()


def gradient_kernel(book, n_fold, n_sent, *refs):
    fold_refs, refs = refs[:n_fold], refs[n_fold:]
    sent_refs, refs = refs[:n_sent], refs[n_sent:]
    (
        fields, drop, grad_table, rows_table,
        mask_grad_ref,
        sems, codes_v, codes, sums, mask_grad_out,
    ) = refs
    codes_of(sent_refs, codes_v)
    (get_codes,) = copies(sems, (codes_v, codes))
    packed = fold_refs[0][: M // 2]
    for ref in fold_refs[1:]:
        packed = packed + ref[: M // 2]
    other = swap(packed)
    low_half = lane_of(packed.shape) < M
    grid = jnp.concatenate(
        [jnp.where(low_half, packed, other), jnp.where(low_half, other, packed)], 0
    )
    for number in range(2):
        sums[number] = jnp.zeros((W, LANES), f32)
    turn = signs(K, 1.0, -1.0)
    even = slot_lanes(K)
    real_or_imag = lane_of((K, LANES)) % M < K
    get_codes.wait()
    drop_rows, drop_cols = book.read(drop, "drop_rows"), book.read(drop, "drop_cols")

    def backward(none, items):
        waves = []
        for ref, place in items:
            for pair in range(PAIRS):
                scaled = [grid * fields[place * MOST + 2 * pair + slot] for slot in range(2)]
                pull = jnp.concatenate(scaled, 1).astype(bf16)
                raw = dot(drop_rows, jnp.concatenate([pull, pull], 0))
                wave = []
                for slot in range(2):
                    mine = raw[:, slot * LANES : (slot + 1) * LANES]
                    wave.append(mine[:K] + turn * swap(mine[K:]))
                waves.append(jnp.concatenate(wave, 1))
        high, low = split(jnp.concatenate(waves, 0))
        back = dot(jnp.concatenate([high, high, low], 1), drop_cols)
        number = 0
        for ref, place in items:
            weights = ref[pl.ds(AT_TAIL, 16), :].astype(f32) * (2.0 / K)
            for pair in range(PAIRS):
                mine = back[number * K : (number + 1) * K]
                number += 1
                real, imag = pair_parts(ref, pair)
                product = real * mine[:, :LANES] + imag * mine[:, LANES:]
                product = weights[TAIL_PAIR + pair : TAIL_PAIR + pair + 1] * product
                for slot in range(2):
                    row, col = window_of(codes, place, 2 * pair + slot)
                    keep = even if slot == 0 else jnp.logical_not(even)
                    shift = lax.rem(col + LANES - slot * K, LANES)
                    moved = pltpu.roll(jnp.where(keep, product, 0.0), shift, 1)
                    sums[slot, pl.ds(row, K), :] += moved
        return none

    over_owners(sent_refs, backward, 0)
    grad_cols = book.read(grad_table, "grad_cols")
    grad = sums[0] + sums[1]
    turn = signs(W, 1.0, -1.0)
    high, low = split(jnp.concatenate([grad * turn, -swap(grad)], 0))
    half = dot(book.read(rows_table, "grad_rows"), jnp.concatenate([high, high, low], 0))
    high, low = split(half)
    both = jnp.concatenate([high, high], 1)
    chunk = grad_cols.shape[1] // PIECES
    puts = []
    for piece in range(PIECES):
        here = slice(piece * chunk, (piece + 1) * chunk)
        mask_grad_out[:, here] = dot(both, grad_cols[:, here]) + dot(low, grad_cols[:LANES, here])
        place = mask_grad_ref.at[0, :, pl.ds(piece * chunk, chunk)]
        puts.append(
            pltpu.make_async_copy(mask_grad_out.at[:, pl.ds(piece * chunk, chunk)], place, sems.at[1 + piece])
        )
        puts[-1].start()
    for put in puts:
        put.wait()


VMEM = pl.BlockSpec(memory_space=pltpu.VMEM)
SMEM = pl.BlockSpec(memory_space=pltpu.SMEM)
HBM = pl.BlockSpec(memory_space=pltpu.HBM)


def room(kib):
    return pltpu.CompilerParams(vmem_limit_bytes=(64 * 1024 - kib) * 1024)


def in_hbm(value):
    return pltpu.with_memory_space_constraint(value, pltpu.HBM)


def exchange(value, axis, step):
    return lax.ppermute(value, axis, [(i, i ^ step) for i in range(lax.axis_size(axis))])


def others(value, axis):
    return [exchange(value, axis, step) for step in range(1, lax.axis_size(axis))]


def like(value):
    return pltpu.VMEM(value.shape, value.dtype)


def shards(
    mask, target, tile_class, thresholds, source_pupil, source_weight, source_cell, active_count
):
    span, period = mask.shape[1:]
    slots = source_pupil.shape[0]
    src_count = lax.axis_size("src")
    few = src_count in (2, 4)
    spec_cols, spec_rows, book = tables(period, span)
    pages = jnp.asarray(book.pages)
    src = lax.axis_index("src")
    sems = pltpu.SemaphoreType.DMA
    smem = pltpu.SMEM

    part, sent, threshold = pl.pallas_call(
        spectrum_kernel,
        in_specs=[HBM] * 5 + [SMEM] + [HBM] * 3,
        out_specs=[VMEM] * 3,
        out_shape=[
            jax.ShapeDtypeStruct((W, LANES), f32),
            jax.ShapeDtypeStruct((ROWS - AT_PUPILS, LANES), bf16),
            jax.ShapeDtypeStruct((8, LANES), f32),
        ],
        scratch_shapes=[
            like(mask[0]),
            like(source_pupil[:16]),
            like(source_weight),
            smem(source_cell.shape, jnp.int32),
            smem(active_count.shape, jnp.int32),
            smem(thresholds.shape, f32),
            like(spec_cols),
            like(spec_rows[0]),
            sems((8,)),
            pltpu.VMEM((LANES, LANES), f32),
            pltpu.VMEM((PAIRS * K, LANES), f32),
        ],
        compiler_params=room(24576),
        name="spectrum",
    )(
        *map(in_hbm, (mask, source_pupil, source_weight, source_cell, active_count)),
        tile_class,
        *map(in_hbm, (thresholds, jnp.asarray(spec_cols), jnp.asarray(spec_rows))),
    )
    from_pix = others(part, "pix")
    sent = pl.pallas_call(
        pack_kernel,
        in_specs=[VMEM] * (2 + len(from_pix)),
        out_specs=VMEM,
        out_shape=jax.ShapeDtypeStruct((ROWS, LANES), bf16),
        compiler_params=room(32768),
        name="pack",
    )(part, *from_pix, sent)
    if few:
        parcels = [sent] + others(sent, "src")
    else:
        parcels = [lax.all_gather(sent, "src")]

    late_target, late_pages, _ = lax.optimization_barrier((target, pages, sent))
    staged_shapes = [
        jax.ShapeDtypeStruct((span, period), f32),
        *book.shapes(LIFT, FINE, DROP, GRAD, IMAGE_ROWS + book.blocks),
        *book.shapes(IMAGE_ROWS) * lax.axis_size("pix"),
    ]
    staged = pl.pallas_call(
        functools.partial(stage_kernel, book),
        in_specs=[HBM] * 2,
        out_specs=[VMEM] * len(staged_shapes),
        out_shape=staged_shapes,
        scratch_shapes=[sems((len(staged_shapes),))],
        compiler_params=room(24576),
        name="stage",
    )(in_hbm(late_target), in_hbm(late_pages))
    near_target, lift, fine, *for_gradient = staged[:6]
    early_target, _ = lax.optimization_barrier((target, from_pix[0]))
    targets = [near_target] + others(early_target[0], "pix")
    image_rows = staged[6:]

    numbers = src_count * MOST
    owners_up = -(-src_count // 8) * 8
    fold_rows = M // 2 + (1 if few else src_count) * SUMS
    fold_count = src_count if few else 1
    codes = [pltpu.VMEM((owners_up, LANES), jnp.int32), smem((owners_up, LANES), jnp.int32)]
    intensity, fields, *folded = pl.pallas_call(
        functools.partial(image_kernel, book, len(parcels), len(targets)),
        in_specs=[VMEM] * (len(parcels) + 2 * len(targets) + 3),
        out_specs=[HBM, VMEM] + [VMEM] * fold_count,
        out_shape=[
            jax.ShapeDtypeStruct((1, span, period), f32),
            jax.ShapeDtypeStruct((numbers, M, LANES), f32),
            *[jax.ShapeDtypeStruct((fold_rows, LANES), f32)] * fold_count,
        ],
        scratch_shapes=[
            sems((2,)),
            *codes,
            pltpu.VMEM((W, LANES), f32),
            like(target[0]),
        ],
        compiler_params=room(24576),
        name="image",
    )(*parcels, *targets, *image_rows, threshold, lift, fine)

    if few:
        folds = [
            value if step == 0 else exchange(value, "src", step)
            for step, value in enumerate(folded)
        ]
        rows = sum(fold[M // 2 :] for fold in folds)
    else:
        folds = [lax.psum(folded[0], "src")]
        rows = lax.dynamic_slice_in_dim(folds[0], M // 2 + src * SUMS, SUMS, 0)
    for other in others(rows, "tile"):
        rows = rows + other
    mask_grad = pl.pallas_call(
        functools.partial(gradient_kernel, book, len(folds), len(parcels)),
        in_specs=[VMEM] * (len(folds) + len(parcels) + 1 + len(for_gradient)),
        out_specs=HBM,
        out_shape=jax.ShapeDtypeStruct((1, span, period), f32),
        scratch_shapes=[
            sems((1 + PIECES,)),
            *codes,
            pltpu.VMEM((2, W, LANES), f32),
            like(mask[0]),
        ],
        compiler_params=room(24576),
        name="gradient",
    )(*folds, *parcels, fields, *for_gradient)
    sums = jnp.sum(rows, 1) * (1.0 / (period * K))
    source_grad = jnp.zeros((slots,), f32).at[:SUMS].set(sums)
    return intensity, mask_grad, source_grad


def solution(mesh):
    in_specs = (
        P(("groups", "tile"), ("src", "pix"), None),
        P(("groups", "tile"), ("src", "pix"), None),
        P(("groups", "tile")),
        P(),
        P("src", None),
        P("src"),
        P("src"),
        P(),
    )
    out_specs = (
        P(("groups", "tile"), ("src", "pix"), None),
        P(("groups", "tile"), ("src", "pix"), None),
        P(("groups", "src")),
    )
    return jax.shard_map(shards, mesh=mesh, in_specs=in_specs, out_specs=out_specs, check_vma=False)
```

```python
import functools

import jax
import jax.numpy as jnp
import ml_dtypes
import numpy as np
from jax import lax
from jax.experimental import pallas as pl
from jax.experimental.pallas import tpu as pltpu
from jax.sharding import PartitionSpec as P

K = 32
SG = 17
W = 48
MOST = 6
CLASSES = 4
STEEP = 4.0

M = 64
LANES = 128
PAIRS = MOST // 2
AT_PUPILS = W
AT_TAIL = AT_PUPILS + PAIRS * K
ROWS = AT_TAIL + 16
TAIL_PAIR, TAIL_CELL = 8, 12
PIECES = 4
SUMS = 8

f32 = jnp.float32
bf16 = jnp.bfloat16


def split_np(table):
    table = np.asarray(table, np.float32)
    high = table.astype(ml_dtypes.bfloat16)
    low = (table - high.astype(np.float32)).astype(ml_dtypes.bfloat16)
    return high, low


def halves(left, right):
    out = np.zeros((left.shape[0], LANES))
    out[:, : left.shape[1]] = left
    out[:, M : M + right.shape[1]] = right
    return out


@functools.lru_cache(maxsize=None)
def tables(period, span):
    blocks = period // span
    freqs = np.arange(W) - W // 2
    pixels = np.arange(period)
    wide = 2.0 * np.pi / period * ((freqs[:, None] * pixels[None, :]) % period)
    wide_cos, wide_sin = np.cos(wide), np.sin(wide)
    narrow = np.arange(K) - K // 2
    coarse = 2.0 * np.pi / M * ((narrow[:, None] * np.arange(M)[None, :]) % M)
    coarse_cos, coarse_sin = np.cos(coarse), np.sin(coarse)
    near = 2.0 * np.pi / period * ((narrow[:, None] * pixels[None, :]) % period)
    gain = sum(
        (wave * wave.astype(np.float32).astype(ml_dtypes.bfloat16).astype(np.float64)).mean(1)
        for wave in (np.cos(near), np.sin(near))
    )
    rounded_cos, rounded_sin = gain[:, None] * coarse_cos, gain[:, None] * coarse_sin
    high, low = split_np(halves(wide_cos.T, -wide_sin.T))
    spec_cols = np.concatenate([high, low], 1)
    rows = np.concatenate(
        [wide_cos.reshape(W, blocks, span), wide_sin.reshape(W, blocks, span)], 2
    ).transpose(1, 0, 2)
    high, low = split_np(rows / period)
    spec_rows = np.concatenate([high, low], 1)
    def pair_table(cos, sin):
        out = np.zeros((4 * K, 4 * M))
        for slot in range(2):
            real, imag, at = slot * K, (2 + slot) * K, slot * 2 * M
            out[real : real + K, at : at + 2 * M] = np.concatenate([cos, sin], 1)
            out[imag : imag + K, at : at + 2 * M] = np.concatenate([-sin, cos], 1)
        return out

    lift = pair_table(rounded_cos, rounded_sin)
    turned = pair_table(-rounded_sin, rounded_cos)
    high, low = split_np(np.concatenate([lift, turned], 1))
    lift_cols = np.concatenate([high, low], 0)
    lift_rows = np.concatenate(split_np(rounded_cos.T / K) + split_np(rounded_sin.T / K), 1)
    orders = np.arange(-(M // 2 - 1), M // 2)
    places = pixels[:, None] * (M / period) - np.arange(M)[None, :]
    inter = np.cos(2.0 * np.pi / M * places[:, :, None] * orders).sum(-1) / M
    high, low = split_np(inter)
    fine_cols = np.concatenate([high.T, low.T, high.T, low.T], 0)
    fold_cols = np.concatenate([high, low], 1)
    fine_rows = np.concatenate([high, low, high, low], 1).reshape(blocks, span, 4 * M)
    high_t = high.reshape(blocks, span, M).transpose(0, 2, 1)
    low_t = low.reshape(blocks, span, M).transpose(0, 2, 1)
    fold_rows = np.concatenate([high_t, low_t, high_t], 2)
    high, low = split_np(np.concatenate([rounded_cos, rounded_sin], 0))
    drop_rows = np.concatenate([high, low], 1)
    drop = pair_table(coarse_cos, coarse_sin).T
    drop = np.concatenate([drop, drop[:, M:], -drop[:, :M]], 1)
    high, low = split_np(drop)
    drop_cols = np.concatenate([high, low, high], 0)
    rows = np.concatenate(
        [
            wide_cos.reshape(W, blocks, span).transpose(1, 2, 0),
            wide_sin.reshape(W, blocks, span).transpose(1, 2, 0),
        ],
        2,
    )
    high, low = split_np(rows / period)
    grad_rows = np.concatenate([high, low, high], 2)
    padded = [np.pad(part, ((0, M - W), (0, 0))) for part in (wide_cos, wide_sin)]
    high, low = split_np(np.concatenate(padded, 0))
    grad_cols = np.concatenate([high, low], 0)
    chapters = [
        dict(lift_cols=lift_cols, lift_rows=lift_rows),
        dict(fine_cols=fine_cols, fold_cols=fold_cols),
        dict(drop_rows=drop_rows, drop_cols=drop_cols),
        dict(grad_cols=grad_cols),
    ]
    for block in range(blocks):
        chapters.append(dict(fine_rows=fine_rows[block], fold_rows=fold_rows[block]))
    for block in range(blocks):
        chapters.append(dict(grad_rows=grad_rows[block]))
    pages, starts, places, at = [], [], {}, 0
    for chapter in chapters:
        starts.append(at)
        for name, value in chapter.items():
            places[name] = (at - starts[-1], value.shape)
            for lane in range(0, value.shape[1], LANES):
                page = value[:, lane : lane + LANES]
                pages.append(np.pad(page, ((0, 0), (0, LANES - page.shape[1]))))
                at += page.shape[0]
    starts.append(at)
    return spec_cols, spec_rows, Book(np.concatenate(pages, 0), starts, places, blocks)


class Book:
    def __init__(self, pages, starts, places, blocks):
        self.pages, self.starts, self.places, self.blocks = pages, starts, places, blocks

    def rows(self, chapter):
        return self.starts[chapter + 1] - self.starts[chapter]

    def shapes(self, *chapters):
        return [jax.ShapeDtypeStruct((self.rows(chapter), LANES), bf16) for chapter in chapters]

    def where(self, ref, chapter, block=0):
        return ref.at[pl.ds(self.starts[chapter] + block * self.rows(chapter), self.rows(chapter))]

    def read(self, ref, name):
        at, (rows, lanes) = self.places[name]
        pages = [
            ref[at + number * rows : at + (number + 1) * rows, : min(LANES, lanes - lane)]
            for number, lane in enumerate(range(0, lanes, LANES))
        ]
        return pages[0] if len(pages) == 1 else jnp.concatenate(pages, 1)


LIFT, FINE, DROP, GRAD, IMAGE_ROWS = range(5)


def dot(left, right):
    return jnp.dot(left, right, preferred_element_type=f32)


def split(value):
    high = value.astype(bf16)
    return high, (value - high.astype(f32)).astype(bf16)


def lane_of(shape):
    return lax.broadcasted_iota(jnp.int32, shape, len(shape) - 1)


def row_of(shape):
    return lax.broadcasted_iota(jnp.int32, shape, 0)


def swap(value):
    return pltpu.roll(value, M, 1)


def signs(rows, low, high):
    return jnp.where(lane_of((rows, LANES)) < M, f32(low), f32(high))


def place_is_static(place):
    return isinstance(place, int)


def my_block():
    return lax.axis_index("src") * lax.axis_size("pix") + lax.axis_index("pix")


def chip_blocks():
    pix, count = lax.axis_index("pix"), lax.axis_size("pix")
    base = lax.axis_index("src") * count
    return [base + jnp.bitwise_xor(pix, step) for step in range(count)]


def copies(sems, *pairs):
    out = [
        pltpu.make_async_copy(source, place, sems.at[number])
        for number, (source, place) in enumerate(pairs)
    ]
    for copy in out:
        copy.start()
    return out


def spectrum_kernel(
    mask_ref, pupil_ref, weight_ref, cell_ref, active_ref, class_ref, thresholds_ref,
    cols_ref, rows_ref,
    part_ref, sent_ref, threshold_ref,
    mask_in, pupil_in, weight_in, cell_in, active_in, thresholds, cols, rows,
    sems, lined, paired,
):
    (
        get_pupil, get_mask, get_cols, get_active, get_cell, get_weight, get_rows,
        get_thresholds,
    ) = copies(
        sems,
        (pupil_ref.at[pl.ds(0, 16)], pupil_in),
        (mask_ref.at[0], mask_in),
        (cols_ref, cols),
        (active_ref, active_in),
        (cell_ref, cell_in),
        (weight_ref, weight_in),
        (rows_ref.at[my_block()], rows),
        (thresholds_ref, thresholds),
    )
    get_active.wait()
    get_cell.wait()
    get_pupil.wait()
    get_weight.wait()
    active = active_in[lax.axis_index("src")]
    raw = pupil_in[...].astype(f32)[:8]
    raw = jnp.where(row_of(raw.shape) < active, raw, 0.0)
    for piece in range(16):
        lined[pl.ds(piece, 8, stride=16), :] = raw[:, piece * LANES : (piece + 1) * LANES]
    quarter = lane_of((8, LANES)) // K
    for pair in range(PAIRS):
        first, second = pair * 32, pair * 32 + 16
        quarters = [lined[pl.ds(start, 8), :] for start in (first, second, first + 8, second + 8)]
        for turn in range(4):
            moved = [
                value if number == turn else pltpu.roll(value, K * (number - turn) % LANES, 1)
                for number, value in enumerate(quarters)
            ]
            out = moved[3]
            for number in range(3):
                out = jnp.where(quarter == number, moved[number], out)
            paired[pl.ds(pair * K + turn, 8, stride=4), :] = out
    sent_ref[: PAIRS * K] = paired[...].astype(bf16)
    shape = (8, LANES)
    weights = jnp.broadcast_to(weight_in[...].astype(f32).reshape(1, -1)[:, :LANES], shape)
    column = jnp.sum(jnp.where(row_of(shape) == lane_of(shape), weights, 0.0), 1, keepdims=True)
    column = jnp.broadcast_to(column, shape)
    tail = [column]
    for pair in range(PAIRS):
        even = lane_of((1, LANES)) // K % 2 == 0
        tail.append(jnp.where(even, column[2 * pair : 2 * pair + 1], column[2 * pair + 1 : 2 * pair + 2]))
    tail.append(jnp.zeros((1, LANES), f32))
    place = lane_of((1, LANES))
    row_code, col_code = jnp.zeros((1, LANES), f32), jnp.zeros((1, LANES), f32)
    for slot in range(MOST):
        cell = cell_in[slot]
        row_code = jnp.where(place == slot, lax.div(cell, SG).astype(f32), row_code)
        col_code = jnp.where(place == slot, lax.rem(cell, SG).astype(f32), col_code)
    tail += [row_code, col_code, jnp.zeros((2, LANES), f32)]
    sent_ref[PAIRS * K :] = jnp.concatenate(tail, 0).astype(bf16)
    get_mask.wait()
    get_cols.wait()
    get_rows.wait()
    high, low = split(mask_in[...])
    both = dot(high, cols[...])
    part = both[:, :LANES] + both[:, LANES:] + dot(low, cols[:, :LANES])
    turned = swap(part) * signs(part.shape[0], 1.0, -1.0)
    high, low = split(jnp.concatenate([part, turned], 0))
    product = dot(rows[...], jnp.concatenate([high, low], 1))
    part_ref[...] = product[:W, :LANES] + product[:W, LANES:] + product[W:, :LANES]
    get_thresholds.wait()
    kind = class_ref[0]
    threshold = thresholds[0]
    for number in range(1, CLASSES):
        threshold = jnp.where(kind == number, thresholds[number], threshold)
    threshold_ref[...] = jnp.full(threshold_ref.shape, threshold, f32)


def pack_kernel(part_ref, *refs):
    *other_refs, sent_ref, out_ref = refs
    part = part_ref[...]
    for ref in other_refs:
        part = part + ref[...]
    high, low = split(part)
    rest = pltpu.roll(low.astype(f32), K, 1)
    out_ref[:W] = jnp.where(lane_of(part.shape) % M < W, high.astype(f32), rest).astype(bf16)
    out_ref[AT_PUPILS:] = sent_ref[...]


def stage_kernel(book, target_ref, book_ref, *refs):
    *out_refs, sems = refs
    target_out, lift_out, fine_out, drop_out, grad_out, grad_rows_out, *rows_out = out_refs
    gets = copies(
        sems,
        (book.where(book_ref, LIFT), lift_out),
        (book.where(book_ref, FINE), fine_out),
        (target_ref.at[0], target_out),
        *(
            (book.where(book_ref, IMAGE_ROWS, block), out)
            for block, out in zip(chip_blocks(), rows_out)
        ),
        (book.where(book_ref, DROP), drop_out),
        (book.where(book_ref, GRAD), grad_out),
        (book.where(book_ref, IMAGE_ROWS + book.blocks, my_block()), grad_rows_out),
    )
    for get in gets:
        get.wait()


def over_owners(refs, body, carry):
    if len(refs) > 1:
        return body(carry, [(ref, place) for place, ref in enumerate(refs)])
    (ref,) = refs
    return lax.fori_loop(
        0, ref.shape[0], lambda owner, carry: body(carry, [(ref.at[owner], owner)]), carry
    )


def codes_of(refs, codes_v):
    def body(none, items):
        for ref, place in items:
            tail = ref[pl.ds(AT_TAIL, 16), :].astype(f32)
            code = tail[TAIL_CELL : TAIL_CELL + 1] * 32.0 + tail[TAIL_CELL + 1 : TAIL_CELL + 2]
            codes_v[pl.ds(place, 1), :] = code.astype(jnp.int32)
        return none

    over_owners(refs, body, 0)


def window_of(codes, place, slot):
    code = codes[place, slot]
    return lax.div(code, 32), lax.rem(code, 32)


def pair_parts(ref, pair):
    value = ref[pl.ds(AT_PUPILS + pair * K, K), :].astype(f32)
    other = swap(value)
    low = lane_of(value.shape) < M
    return jnp.where(low, value, other), jnp.where(low, other, value)


def slot_lanes(rows):
    return lane_of((rows, LANES)) // K % 2 == 0


def image_kernel(book, n_sent, n_pix, *refs):
    sent_refs, refs = refs[:n_sent], refs[n_sent:]
    targets, refs = refs[:n_pix], refs[n_pix:]
    rows_refs, refs = refs[:n_pix], refs[n_pix:]
    (
        threshold_ref, lift, fine,
        intensity_ref, fields, *fold_refs,
        sems, codes_v, codes, spectrum, intensity_out,
    ) = refs
    codes_of(sent_refs, codes_v)
    (get_codes,) = copies(sems, (codes_v, codes))

    def gather(total, items):
        for ref, place in items:
            value = ref[:W].astype(f32)
            rest = jnp.where(lane_of(value.shape) % M < W, 0.0, value)
            total = total + (value + pltpu.roll(rest, LANES - K, 1))
        return total

    spectrum[...] = over_owners(sent_refs, gather, jnp.zeros((W, LANES), f32))
    if len(sent_refs) == 1:
        get_codes.wait()
    lift_cols, lift_rows = book.read(lift, "lift_cols"), book.read(lift, "lift_rows")
    even = slot_lanes(K)
    turn_low = signs(K, -1.0, 1.0)

    def forward(total, items):
        waves = []
        parts = [pair_parts(ref, pair) for ref, place in items for pair in range(PAIRS)]
        if len(items) > 1:
            get_codes.wait()
        for ref, place in items:
            for pair in range(PAIRS):
                real, imag = parts.pop(0)
                row, col = window_of(codes, place, 2 * pair)
                left = pltpu.roll(spectrum[pl.ds(row, K), :], lax.rem(LANES - col, LANES), 1)
                row, col = window_of(codes, place, 2 * pair + 1)
                right = pltpu.roll(spectrum[pl.ds(row, K), :], lax.rem(LANES + K - col, LANES), 1)
                window = jnp.where(even, left, right)
                waves.append((real * window + imag * (turn_low * swap(window))).astype(bf16))
        wave = jnp.concatenate(waves, 0)
        wave = dot(jnp.concatenate([wave, wave], 1), lift_cols).astype(bf16)
        number = 0
        for ref, place in items:
            weights = ref[pl.ds(AT_TAIL, 16), :].astype(f32)
            for pair in range(PAIRS):
                here = slice(number * K, (number + 1) * K)
                number += 1
                own, turned = wave[here, : 2 * LANES], wave[here, 2 * LANES :]
                raw = dot(lift_rows, jnp.concatenate([own, own, turned, turned], 0))
                for slot in range(2):
                    field = raw[:, slot * LANES : (slot + 1) * LANES]
                    fields[place * MOST + 2 * pair + slot] = field
                    at = 2 * pair + slot
                    total = total + weights[at : at + 1] * (field * field)
        return total

    power = over_owners(sent_refs, forward, jnp.zeros((M, LANES), f32))
    high, low = split(power + swap(power))
    coarse = jnp.concatenate([high, high, low, low], 0)
    fine_cols, fold_cols = book.read(fine, "fine_cols"), book.read(fine, "fold_cols")
    threshold = threshold_ref[:1, :1]
    grid = jnp.zeros((M, LANES), f32)
    fine_rows = [book.read(rows_ref, "fine_rows") for rows_ref in rows_refs]
    high, low = split(dot(jnp.concatenate(fine_rows, 0), coarse))
    intensities = dot(jnp.concatenate([high, low], 1), fine_cols)
    span = intensity_out.shape[0]
    intensity_out[...] = intensities[:span]
    put = pltpu.make_async_copy(intensity_out, intensity_ref.at[0], sems.at[1])
    put.start()
    slopes = []
    for number, target in enumerate(targets):
        intensity = intensities[number * span : (number + 1) * span]
        resist = 1.0 / (1.0 + jnp.exp(-STEEP * (intensity - threshold)))
        slope = 2.0 * STEEP * (resist - target[...]) * resist * (1.0 - resist)
        slopes.append(slope.astype(bf16))
    folded = dot(jnp.concatenate(slopes, 0), fold_cols)
    high, low = split(folded + swap(folded))
    for number, rows_ref in enumerate(rows_refs):
        here = slice(number * span, (number + 1) * span)
        grid = grid + dot(
            book.read(rows_ref, "fold_rows"),
            jnp.concatenate([high[here], high[here], low[here]], 0),
        )
    lane = lane_of((M // 2, LANES))
    packed = jnp.where(lane < M, grid[: M // 2], grid[M // 2 :])
    for fold_ref in fold_refs:
        fold_ref[: M // 2] = packed.astype(fold_ref.dtype)

    def weigh(none, items):
        for ref, place in items:
            sums = []
            for slot in range(MOST):
                field = fields[place * MOST + slot]
                sums.append(jnp.sum(grid * (field * field), 0, keepdims=True))
            sums = jnp.concatenate(sums + [jnp.zeros((SUMS - MOST, LANES), f32)], 0)
            if place_is_static(place) and place > 0:
                high, low = split(sums)
                fold_refs[place][M // 2 :] = jnp.concatenate([high, low], 0)
            elif len(fold_refs) > 1:
                fold_refs[place][M // 2 :] = sums
            else:
                start = pl.multiple_of(M // 2 + place * SUMS, SUMS)
                fold_refs[0][pl.ds(start, SUMS), :] = sums
        return none

    over_owners(sent_refs, weigh, 0)
    put.wait()


def gradient_kernel(book, n_fold, n_sent, *refs):
    fold_refs, refs = refs[:n_fold], refs[n_fold:]
    sent_refs, refs = refs[:n_sent], refs[n_sent:]
    (
        fields, drop, grad_table, rows_table,
        mask_grad_ref,
        sems, codes_v, codes, sums, mask_grad_out,
    ) = refs
    codes_of(sent_refs, codes_v)
    (get_codes,) = copies(sems, (codes_v, codes))
    packed = fold_refs[0][: M // 2]
    for ref in fold_refs[1:]:
        packed = packed + ref[: M // 2].astype(f32)
    other = swap(packed)
    low_half = lane_of(packed.shape) < M
    grid = jnp.concatenate(
        [jnp.where(low_half, packed, other), jnp.where(low_half, other, packed)], 0
    )
    for number in range(2):
        sums[number] = jnp.zeros((W, LANES), f32)
    turn = signs(K, 1.0, -1.0)
    even = slot_lanes(K)
    real_or_imag = lane_of((K, LANES)) % M < K
    get_codes.wait()
    drop_rows, drop_cols = book.read(drop, "drop_rows"), book.read(drop, "drop_cols")

    def backward(none, items):
        waves = []
        for ref, place in items:
            for pair in range(PAIRS):
                scaled = [grid * fields[place * MOST + 2 * pair + slot] for slot in range(2)]
                pull = jnp.concatenate(scaled, 1).astype(bf16)
                raw = dot(drop_rows, jnp.concatenate([pull, pull], 0))
                wave = []
                for slot in range(2):
                    mine = raw[:, slot * LANES : (slot + 1) * LANES]
                    wave.append(mine[:K] + turn * swap(mine[K:]))
                waves.append(jnp.concatenate(wave, 1))
        high, low = split(jnp.concatenate(waves, 0))
        back = dot(jnp.concatenate([high, high, low], 1), drop_cols)
        number = 0
        for ref, place in items:
            weights = ref[pl.ds(AT_TAIL, 16), :].astype(f32) * (2.0 / K)
            for pair in range(PAIRS):
                mine = back[number * K : (number + 1) * K]
                number += 1
                real, imag = pair_parts(ref, pair)
                product = real * mine[:, :LANES] + imag * mine[:, LANES:]
                product = weights[TAIL_PAIR + pair : TAIL_PAIR + pair + 1] * product
                for slot in range(2):
                    row, col = window_of(codes, place, 2 * pair + slot)
                    keep = even if slot == 0 else jnp.logical_not(even)
                    shift = lax.rem(col + LANES - slot * K, LANES)
                    moved = pltpu.roll(jnp.where(keep, product, 0.0), shift, 1)
                    sums[slot, pl.ds(row, K), :] += moved
        return none

    over_owners(sent_refs, backward, 0)
    grad_cols = book.read(grad_table, "grad_cols")
    grad = sums[0] + sums[1]
    turn = signs(W, 1.0, -1.0)
    high, low = split(jnp.concatenate([grad * turn, -swap(grad)], 0))
    half = dot(book.read(rows_table, "grad_rows"), jnp.concatenate([high, high, low], 0))
    high, low = split(half)
    both = jnp.concatenate([high, high], 1)
    chunk = grad_cols.shape[1] // PIECES
    puts = []
    for piece in range(PIECES):
        here = slice(piece * chunk, (piece + 1) * chunk)
        mask_grad_out[:, here] = dot(both, grad_cols[:, here]) + dot(low, grad_cols[:LANES, here])
        place = mask_grad_ref.at[0, :, pl.ds(piece * chunk, chunk)]
        puts.append(
            pltpu.make_async_copy(mask_grad_out.at[:, pl.ds(piece * chunk, chunk)], place, sems.at[1 + piece])
        )
        puts[-1].start()
    for put in puts:
        put.wait()


VMEM = pl.BlockSpec(memory_space=pltpu.VMEM)
SMEM = pl.BlockSpec(memory_space=pltpu.SMEM)
HBM = pl.BlockSpec(memory_space=pltpu.HBM)


def room(kib):
    return pltpu.CompilerParams(vmem_limit_bytes=(64 * 1024 - kib) * 1024)


def in_hbm(value):
    return pltpu.with_memory_space_constraint(value, pltpu.HBM)


def exchange(value, axis, step):
    return lax.ppermute(value, axis, [(i, i ^ step) for i in range(lax.axis_size(axis))])


def others(value, axis):
    return [exchange(value, axis, step) for step in range(1, lax.axis_size(axis))]


def like(value):
    return pltpu.VMEM(value.shape, value.dtype)


def shards(
    mask, target, tile_class, thresholds, source_pupil, source_weight, source_cell, active_count
):
    span, period = mask.shape[1:]
    slots = source_pupil.shape[0]
    src_count = lax.axis_size("src")
    few = src_count in (2, 4)
    spec_cols, spec_rows, book = tables(period, span)
    pages = jnp.asarray(book.pages)
    src = lax.axis_index("src")
    sems = pltpu.SemaphoreType.DMA
    smem = pltpu.SMEM

    part, sent, threshold = pl.pallas_call(
        spectrum_kernel,
        in_specs=[HBM] * 5 + [SMEM] + [HBM] * 3,
        out_specs=[VMEM] * 3,
        out_shape=[
            jax.ShapeDtypeStruct((W, LANES), f32),
            jax.ShapeDtypeStruct((ROWS - AT_PUPILS, LANES), bf16),
            jax.ShapeDtypeStruct((8, LANES), f32),
        ],
        scratch_shapes=[
            like(mask[0]),
            like(source_pupil[:16]),
            like(source_weight),
            smem(source_cell.shape, jnp.int32),
            smem(active_count.shape, jnp.int32),
            smem(thresholds.shape, f32),
            like(spec_cols),
            like(spec_rows[0]),
            sems((8,)),
            pltpu.VMEM((LANES, LANES), f32),
            pltpu.VMEM((PAIRS * K, LANES), f32),
        ],
        compiler_params=room(24576),
        name="spectrum",
    )(
        *map(in_hbm, (mask, source_pupil, source_weight, source_cell, active_count)),
        tile_class,
        *map(in_hbm, (thresholds, jnp.asarray(spec_cols), jnp.asarray(spec_rows))),
    )
    from_pix = others(part, "pix")
    sent = pl.pallas_call(
        pack_kernel,
        in_specs=[VMEM] * (2 + len(from_pix)),
        out_specs=VMEM,
        out_shape=jax.ShapeDtypeStruct((ROWS, LANES), bf16),
        compiler_params=room(32768),
        name="pack",
    )(part, *from_pix, sent)
    if few:
        parcels = [sent] + others(sent, "src")
    else:
        parcels = [lax.all_gather(sent, "src")]

    late_target, late_pages, _ = lax.optimization_barrier((target, pages, sent))
    staged_shapes = [
        jax.ShapeDtypeStruct((span, period), f32),
        *book.shapes(LIFT, FINE, DROP, GRAD, IMAGE_ROWS + book.blocks),
        *book.shapes(IMAGE_ROWS) * lax.axis_size("pix"),
    ]
    staged = pl.pallas_call(
        functools.partial(stage_kernel, book),
        in_specs=[HBM] * 2,
        out_specs=[VMEM] * len(staged_shapes),
        out_shape=staged_shapes,
        scratch_shapes=[sems((len(staged_shapes),))],
        compiler_params=room(24576),
        name="stage",
    )(in_hbm(late_target), in_hbm(late_pages))
    near_target, lift, fine, *for_gradient = staged[:6]
    early_target, _ = lax.optimization_barrier((target, from_pix[0]))
    targets = [near_target] + others(early_target[0], "pix")
    image_rows = staged[6:]

    numbers = src_count * MOST
    owners_up = -(-src_count // 8) * 8
    fold_rows = M // 2 + (1 if few else src_count) * SUMS
    fold_count = src_count if few else 1
    codes = [pltpu.VMEM((owners_up, LANES), jnp.int32), smem((owners_up, LANES), jnp.int32)]
    intensity, fields, *folded = pl.pallas_call(
        functools.partial(image_kernel, book, len(parcels), len(targets)),
        in_specs=[VMEM] * (len(parcels) + 2 * len(targets) + 3),
        out_specs=[HBM, VMEM] + [VMEM] * fold_count,
        out_shape=[
            jax.ShapeDtypeStruct((1, span, period), f32),
            jax.ShapeDtypeStruct((numbers, M, LANES), f32),
            jax.ShapeDtypeStruct((fold_rows, LANES), f32),
            *[jax.ShapeDtypeStruct((M // 2 + 2 * SUMS, LANES), bf16)] * (fold_count - 1),
        ],
        scratch_shapes=[
            sems((2,)),
            *codes,
            pltpu.VMEM((W, LANES), f32),
            like(target[0]),
        ],
        compiler_params=room(24576),
        name="image",
    )(*parcels, *targets, *image_rows, threshold, lift, fine)

    if few:
        folds = [
            value if step == 0 else exchange(value, "src", step)
            for step, value in enumerate(folded)
        ]
        rows = folds[0][M // 2 :]
        for fold in folds[1:]:
            sums = fold[M // 2 :].astype(f32)
            rows = rows + (sums[:SUMS] + sums[SUMS:])
    else:
        folds = [lax.psum(folded[0], "src")]
        rows = lax.dynamic_slice_in_dim(folds[0], M // 2 + src * SUMS, SUMS, 0)
    for other in others(rows, "tile"):
        rows = rows + other
    mask_grad = pl.pallas_call(
        functools.partial(gradient_kernel, book, len(folds), len(parcels)),
        in_specs=[VMEM] * (len(folds) + len(parcels) + 1 + len(for_gradient)),
        out_specs=HBM,
        out_shape=jax.ShapeDtypeStruct((1, span, period), f32),
        scratch_shapes=[
            sems((1 + PIECES,)),
            *codes,
            pltpu.VMEM((2, W, LANES), f32),
            like(mask[0]),
        ],
        compiler_params=room(24576),
        name="gradient",
    )(*folds, *parcels, fields, *for_gradient)
    sums = jnp.sum(rows, 1) * (1.0 / (period * K))
    source_grad = jnp.zeros((slots,), f32).at[:SUMS].set(sums)
    return intensity, mask_grad, source_grad


def solution(mesh):
    in_specs = (
        P(("groups", "tile"), ("src", "pix"), None),
        P(("groups", "tile"), ("src", "pix"), None),
        P(("groups", "tile")),
        P(),
        P("src", None),
        P("src"),
        P("src"),
        P(),
    )
    out_specs = (
        P(("groups", "tile"), ("src", "pix"), None),
        P(("groups", "tile"), ("src", "pix"), None),
        P(("groups", "src")),
    )
    return jax.shard_map(shards, mesh=mesh, in_specs=in_specs, out_specs=out_specs, check_vma=False)
```

```python
import functools

import jax
import jax.numpy as jnp
import ml_dtypes
import numpy as np
from jax import lax
from jax.experimental import pallas as pl
from jax.experimental.pallas import tpu as pltpu
from jax.sharding import PartitionSpec as P

K = 32
SG = 17
W = 48
MOST = 6
CLASSES = 4
STEEP = 4.0

M = 64
LANES = 128
PAIRS = MOST // 2
AT_PUPILS = W
AT_TAIL = AT_PUPILS + PAIRS * K
ROWS = AT_TAIL + 16
TAIL_PAIR, TAIL_CELL = 8, 12
PIECES = 4
SUMS = 8

f32 = jnp.float32
bf16 = jnp.bfloat16


def split_np(table):
    table = np.asarray(table, np.float32)
    high = table.astype(ml_dtypes.bfloat16)
    low = (table - high.astype(np.float32)).astype(ml_dtypes.bfloat16)
    return high, low


def halves(left, right):
    out = np.zeros((left.shape[0], LANES))
    out[:, : left.shape[1]] = left
    out[:, M : M + right.shape[1]] = right
    return out


@functools.lru_cache(maxsize=None)
def tables(period, span):
    blocks = period // span
    freqs = np.arange(W) - W // 2
    pixels = np.arange(period)
    wide = 2.0 * np.pi / period * ((freqs[:, None] * pixels[None, :]) % period)
    wide_cos, wide_sin = np.cos(wide), np.sin(wide)
    narrow = np.arange(K) - K // 2
    coarse = 2.0 * np.pi / M * ((narrow[:, None] * np.arange(M)[None, :]) % M)
    coarse_cos, coarse_sin = np.cos(coarse), np.sin(coarse)
    near = 2.0 * np.pi / period * ((narrow[:, None] * pixels[None, :]) % period)
    gain = sum(
        (wave * wave.astype(np.float32).astype(ml_dtypes.bfloat16).astype(np.float64)).mean(1)
        for wave in (np.cos(near), np.sin(near))
    )
    rounded_cos, rounded_sin = gain[:, None] * coarse_cos, gain[:, None] * coarse_sin
    high, low = split_np(halves(wide_cos.T, -wide_sin.T))
    spec_cols = np.concatenate([high, low], 1)
    rows = np.concatenate(
        [wide_cos.reshape(W, blocks, span), wide_sin.reshape(W, blocks, span)], 2
    ).transpose(1, 0, 2)
    high, low = split_np(rows / period)
    spec_rows = np.concatenate([high, low], 1)
    def pair_table(cos, sin):
        out = np.zeros((4 * K, 4 * M))
        for slot in range(2):
            real, imag, at = slot * K, (2 + slot) * K, slot * 2 * M
            out[real : real + K, at : at + 2 * M] = np.concatenate([cos, sin], 1)
            out[imag : imag + K, at : at + 2 * M] = np.concatenate([-sin, cos], 1)
        return out

    lift = pair_table(rounded_cos, rounded_sin)
    turned = pair_table(-rounded_sin, rounded_cos)
    high, low = split_np(np.concatenate([lift, turned], 1))
    lift_cols = np.concatenate([high, low], 0)
    lift_rows = np.concatenate(split_np(rounded_cos.T / K) + split_np(rounded_sin.T / K), 1)
    orders = np.arange(-(M // 2 - 1), M // 2)
    places = pixels[:, None] * (M / period) - np.arange(M)[None, :]
    inter = np.cos(2.0 * np.pi / M * places[:, :, None] * orders).sum(-1) / M
    high, low = split_np(inter)
    fine_cols = np.concatenate([high.T, low.T, high.T, low.T], 0)
    fold_cols = np.concatenate([high, low], 1)
    fine_rows = np.concatenate([high, low, high, low], 1).reshape(blocks, span, 4 * M)
    high_t = high.reshape(blocks, span, M).transpose(0, 2, 1)
    low_t = low.reshape(blocks, span, M).transpose(0, 2, 1)
    fold_rows = np.concatenate([high_t, low_t, high_t], 2)
    high, low = split_np(np.concatenate([rounded_cos, rounded_sin], 0))
    drop_rows = np.concatenate([high, low], 1)
    drop = pair_table(coarse_cos, coarse_sin).T
    drop = np.concatenate([drop, drop[:, M:], -drop[:, :M]], 1)
    high, low = split_np(drop)
    drop_cols = np.concatenate([high, low], 0)
    rows = np.concatenate(
        [
            wide_cos.reshape(W, blocks, span).transpose(1, 2, 0),
            wide_sin.reshape(W, blocks, span).transpose(1, 2, 0),
        ],
        2,
    )
    high, low = split_np(rows / period)
    grad_rows = np.concatenate([high, low, high], 2)
    padded = [np.pad(part, ((0, M - W), (0, 0))) for part in (wide_cos, wide_sin)]
    high, low = split_np(np.concatenate(padded, 0))
    grad_cols = np.concatenate([high, low], 0)
    chapters = [
        dict(lift_cols=lift_cols, lift_rows=lift_rows),
        dict(fine_cols=fine_cols, fold_cols=fold_cols),
        dict(drop_rows=drop_rows, drop_cols=drop_cols),
        dict(grad_cols=grad_cols),
    ]
    for block in range(blocks):
        chapters.append(dict(fine_rows=fine_rows[block], fold_rows=fold_rows[block]))
    for block in range(blocks):
        chapters.append(dict(grad_rows=grad_rows[block]))
    pages, starts, places, at = [], [], {}, 0
    for chapter in chapters:
        starts.append(at)
        for name, value in chapter.items():
            places[name] = (at - starts[-1], value.shape)
            for lane in range(0, value.shape[1], LANES):
                page = value[:, lane : lane + LANES]
                pages.append(np.pad(page, ((0, 0), (0, LANES - page.shape[1]))))
                at += page.shape[0]
    starts.append(at)
    return spec_cols, spec_rows, Book(np.concatenate(pages, 0), starts, places, blocks)


class Book:
    def __init__(self, pages, starts, places, blocks):
        self.pages, self.starts, self.places, self.blocks = pages, starts, places, blocks

    def rows(self, chapter):
        return self.starts[chapter + 1] - self.starts[chapter]

    def shapes(self, *chapters):
        return [jax.ShapeDtypeStruct((self.rows(chapter), LANES), bf16) for chapter in chapters]

    def where(self, ref, chapter, block=0):
        return ref.at[pl.ds(self.starts[chapter] + block * self.rows(chapter), self.rows(chapter))]

    def read(self, ref, name):
        at, (rows, lanes) = self.places[name]
        pages = [
            ref[at + number * rows : at + (number + 1) * rows, : min(LANES, lanes - lane)]
            for number, lane in enumerate(range(0, lanes, LANES))
        ]
        return pages[0] if len(pages) == 1 else jnp.concatenate(pages, 1)


LIFT, FINE, DROP, GRAD, IMAGE_ROWS = range(5)


def dot(left, right):
    return jnp.dot(left, right, preferred_element_type=f32)


def split(value):
    high = value.astype(bf16)
    return high, (value - high.astype(f32)).astype(bf16)


def lane_of(shape):
    return lax.broadcasted_iota(jnp.int32, shape, len(shape) - 1)


def row_of(shape):
    return lax.broadcasted_iota(jnp.int32, shape, 0)


def swap(value):
    return pltpu.roll(value, M, 1)


def signs(rows, low, high):
    return jnp.where(lane_of((rows, LANES)) < M, f32(low), f32(high))


def place_is_static(place):
    return isinstance(place, int)


def my_block():
    return lax.axis_index("src") * lax.axis_size("pix") + lax.axis_index("pix")


def chip_blocks():
    pix, count = lax.axis_index("pix"), lax.axis_size("pix")
    base = lax.axis_index("src") * count
    return [base + jnp.bitwise_xor(pix, step) for step in range(count)]


def copies(sems, *pairs):
    out = [
        pltpu.make_async_copy(source, place, sems.at[number])
        for number, (source, place) in enumerate(pairs)
    ]
    for copy in out:
        copy.start()
    return out


def spectrum_kernel(
    mask_ref, pupil_ref, weight_ref, cell_ref, active_ref, class_ref, thresholds_ref,
    cols_ref, rows_ref,
    part_ref, sent_ref, threshold_ref,
    mask_in, pupil_in, weight_in, cell_in, active_in, thresholds, cols, rows,
    sems, lined, paired,
):
    (
        get_pupil, get_mask, get_cols, get_active, get_cell, get_weight, get_rows,
        get_thresholds,
    ) = copies(
        sems,
        (pupil_ref.at[pl.ds(0, 16)], pupil_in),
        (mask_ref.at[0], mask_in),
        (cols_ref, cols),
        (active_ref, active_in),
        (cell_ref, cell_in),
        (weight_ref, weight_in),
        (rows_ref.at[my_block()], rows),
        (thresholds_ref, thresholds),
    )
    get_active.wait()
    get_cell.wait()
    get_pupil.wait()
    get_weight.wait()
    active = active_in[lax.axis_index("src")]
    raw = pupil_in[...].astype(f32)[:8]
    raw = jnp.where(row_of(raw.shape) < active, raw, 0.0)
    for piece in range(16):
        lined[pl.ds(piece, 8, stride=16), :] = raw[:, piece * LANES : (piece + 1) * LANES]
    quarter = lane_of((8, LANES)) // K
    for pair in range(PAIRS):
        first, second = pair * 32, pair * 32 + 16
        quarters = [lined[pl.ds(start, 8), :] for start in (first, second, first + 8, second + 8)]
        for turn in range(4):
            moved = [
                value if number == turn else pltpu.roll(value, K * (number - turn) % LANES, 1)
                for number, value in enumerate(quarters)
            ]
            out = moved[3]
            for number in range(3):
                out = jnp.where(quarter == number, moved[number], out)
            paired[pl.ds(pair * K + turn, 8, stride=4), :] = out
    sent_ref[: PAIRS * K] = paired[...].astype(bf16)
    shape = (8, LANES)
    weights = jnp.broadcast_to(weight_in[...].astype(f32).reshape(1, -1)[:, :LANES], shape)
    column = jnp.sum(jnp.where(row_of(shape) == lane_of(shape), weights, 0.0), 1, keepdims=True)
    column = jnp.broadcast_to(column, shape)
    tail = [column]
    for pair in range(PAIRS):
        even = lane_of((1, LANES)) // K % 2 == 0
        tail.append(jnp.where(even, column[2 * pair : 2 * pair + 1], column[2 * pair + 1 : 2 * pair + 2]))
    tail.append(jnp.zeros((1, LANES), f32))
    place = lane_of((1, LANES))
    row_code, col_code = jnp.zeros((1, LANES), f32), jnp.zeros((1, LANES), f32)
    for slot in range(MOST):
        cell = cell_in[slot]
        row_code = jnp.where(place == slot, lax.div(cell, SG).astype(f32), row_code)
        col_code = jnp.where(place == slot, lax.rem(cell, SG).astype(f32), col_code)
    tail += [row_code, col_code, jnp.zeros((2, LANES), f32)]
    sent_ref[PAIRS * K :] = jnp.concatenate(tail, 0).astype(bf16)
    get_mask.wait()
    get_cols.wait()
    get_rows.wait()
    high, low = split(mask_in[...])
    both = dot(high, cols[...])
    part = both[:, :LANES] + both[:, LANES:] + dot(low, cols[:, :LANES])
    turned = swap(part) * signs(part.shape[0], 1.0, -1.0)
    high, low = split(jnp.concatenate([part, turned], 0))
    product = dot(rows[...], jnp.concatenate([high, low], 1))
    part_ref[...] = product[:W, :LANES] + product[:W, LANES:] + product[W:, :LANES]
    get_thresholds.wait()
    kind = class_ref[0]
    threshold = thresholds[0]
    for number in range(1, CLASSES):
        threshold = jnp.where(kind == number, thresholds[number], threshold)
    threshold_ref[...] = jnp.full(threshold_ref.shape, threshold, f32)


def pack_kernel(part_ref, *refs):
    *other_refs, sent_ref, out_ref = refs
    part = part_ref[...]
    for ref in other_refs:
        part = part + ref[...]
    high, low = split(part)
    rest = pltpu.roll(low.astype(f32), K, 1)
    out_ref[:W] = jnp.where(lane_of(part.shape) % M < W, high.astype(f32), rest).astype(bf16)
    out_ref[AT_PUPILS:] = sent_ref[...]


def stage_kernel(book, target_ref, book_ref, *refs):
    *out_refs, sems = refs
    target_out, lift_out, fine_out, drop_out, grad_out, grad_rows_out, *rows_out = out_refs
    gets = copies(
        sems,
        (book.where(book_ref, LIFT), lift_out),
        (book.where(book_ref, FINE), fine_out),
        (target_ref.at[0], target_out),
        *(
            (book.where(book_ref, IMAGE_ROWS, block), out)
            for block, out in zip(chip_blocks(), rows_out)
        ),
        (book.where(book_ref, DROP), drop_out),
        (book.where(book_ref, GRAD), grad_out),
        (book.where(book_ref, IMAGE_ROWS + book.blocks, my_block()), grad_rows_out),
    )
    for get in gets:
        get.wait()


def over_owners(refs, body, carry):
    if len(refs) > 1:
        return body(carry, [(ref, place) for place, ref in enumerate(refs)])
    (ref,) = refs
    return lax.fori_loop(
        0, ref.shape[0], lambda owner, carry: body(carry, [(ref.at[owner], owner)]), carry
    )


def codes_of(refs, codes_v):
    def body(none, items):
        for ref, place in items:
            tail = ref[pl.ds(AT_TAIL, 16), :].astype(f32)
            code = tail[TAIL_CELL : TAIL_CELL + 1] * 32.0 + tail[TAIL_CELL + 1 : TAIL_CELL + 2]
            codes_v[pl.ds(place, 1), :] = code.astype(jnp.int32)
        return none

    over_owners(refs, body, 0)


def window_of(codes, place, slot):
    code = codes[place, slot]
    return lax.div(code, 32), lax.rem(code, 32)


def pair_parts(ref, pair):
    value = ref[pl.ds(AT_PUPILS + pair * K, K), :].astype(f32)
    other = swap(value)
    low = lane_of(value.shape) < M
    return jnp.where(low, value, other), jnp.where(low, other, value)


def slot_lanes(rows):
    return lane_of((rows, LANES)) // K % 2 == 0


def image_kernel(book, n_sent, n_pix, *refs):
    sent_refs, refs = refs[:n_sent], refs[n_sent:]
    targets, refs = refs[:n_pix], refs[n_pix:]
    rows_refs, refs = refs[:n_pix], refs[n_pix:]
    (
        threshold_ref, lift, fine,
        intensity_ref, fields, *fold_refs,
        sems, codes_v, codes, spectrum, intensity_out,
    ) = refs
    codes_of(sent_refs, codes_v)
    (get_codes,) = copies(sems, (codes_v, codes))

    def gather(total, items):
        for ref, place in items:
            value = ref[:W].astype(f32)
            rest = jnp.where(lane_of(value.shape) % M < W, 0.0, value)
            total = total + (value + pltpu.roll(rest, LANES - K, 1))
        return total

    spectrum[...] = over_owners(sent_refs, gather, jnp.zeros((W, LANES), f32))
    if len(sent_refs) == 1:
        get_codes.wait()
    lift_cols, lift_rows = book.read(lift, "lift_cols"), book.read(lift, "lift_rows")
    even = slot_lanes(K)
    turn_low = signs(K, -1.0, 1.0)

    def forward(total, items):
        waves = []
        parts = [pair_parts(ref, pair) for ref, place in items for pair in range(PAIRS)]
        if len(items) > 1:
            get_codes.wait()
        for ref, place in items:
            for pair in range(PAIRS):
                real, imag = parts.pop(0)
                row, col = window_of(codes, place, 2 * pair)
                left = pltpu.roll(spectrum[pl.ds(row, K), :], lax.rem(LANES - col, LANES), 1)
                row, col = window_of(codes, place, 2 * pair + 1)
                right = pltpu.roll(spectrum[pl.ds(row, K), :], lax.rem(LANES + K - col, LANES), 1)
                window = jnp.where(even, left, right)
                waves.append((real * window + imag * (turn_low * swap(window))).astype(bf16))
        wave = jnp.concatenate(waves, 0)
        wave = dot(jnp.concatenate([wave, wave], 1), lift_cols).astype(bf16)
        number = 0
        for ref, place in items:
            weights = ref[pl.ds(AT_TAIL, 16), :].astype(f32)
            for pair in range(PAIRS):
                here = slice(number * K, (number + 1) * K)
                number += 1
                own, turned = wave[here, : 2 * LANES], wave[here, 2 * LANES :]
                raw = dot(lift_rows, jnp.concatenate([own, own, turned, turned], 0))
                for slot in range(2):
                    field = raw[:, slot * LANES : (slot + 1) * LANES]
                    fields[place * MOST + 2 * pair + slot] = field
                    at = 2 * pair + slot
                    total = total + weights[at : at + 1] * (field * field)
        return total

    power = over_owners(sent_refs, forward, jnp.zeros((M, LANES), f32))
    high, low = split(power + swap(power))
    coarse = jnp.concatenate([high, high, low, low], 0)
    fine_cols, fold_cols = book.read(fine, "fine_cols"), book.read(fine, "fold_cols")
    threshold = threshold_ref[:1, :1]
    grid = jnp.zeros((M, LANES), f32)
    fine_rows = [book.read(rows_ref, "fine_rows") for rows_ref in rows_refs]
    high, low = split(dot(jnp.concatenate(fine_rows, 0), coarse))
    intensities = dot(jnp.concatenate([high, low], 1), fine_cols)
    span = intensity_out.shape[0]
    intensity_out[...] = intensities[:span]
    put = pltpu.make_async_copy(intensity_out, intensity_ref.at[0], sems.at[1])
    put.start()
    slopes = []
    for number, target in enumerate(targets):
        intensity = intensities[number * span : (number + 1) * span]
        resist = 1.0 / (1.0 + jnp.exp(-STEEP * (intensity - threshold)))
        slope = 2.0 * STEEP * (resist - target[...]) * resist * (1.0 - resist)
        slopes.append(slope.astype(bf16))
    folded = dot(jnp.concatenate(slopes, 0), fold_cols)
    high, low = split(folded + swap(folded))
    for number, rows_ref in enumerate(rows_refs):
        here = slice(number * span, (number + 1) * span)
        grid = grid + dot(
            book.read(rows_ref, "fold_rows"),
            jnp.concatenate([high[here], high[here], low[here]], 0),
        )
    lane = lane_of((M // 2, LANES))
    packed = jnp.where(lane < M, grid[: M // 2], grid[M // 2 :])
    for fold_ref in fold_refs:
        fold_ref[: M // 2] = packed.astype(fold_ref.dtype)

    def weigh(none, items):
        for ref, place in items:
            sums = []
            for slot in range(MOST):
                field = fields[place * MOST + slot]
                sums.append(jnp.sum(grid * (field * field), 0, keepdims=True))
            sums = jnp.concatenate(sums + [jnp.zeros((SUMS - MOST, LANES), f32)], 0)
            if place_is_static(place) and place > 0:
                high, low = split(sums)
                fold_refs[place][M // 2 :] = jnp.concatenate([high, low], 0)
            elif len(fold_refs) > 1:
                fold_refs[place][M // 2 :] = sums
            else:
                start = pl.multiple_of(M // 2 + place * SUMS, SUMS)
                fold_refs[0][pl.ds(start, SUMS), :] = sums
        return none

    over_owners(sent_refs, weigh, 0)
    put.wait()


def gradient_kernel(book, n_fold, n_sent, *refs):
    fold_refs, refs = refs[:n_fold], refs[n_fold:]
    sent_refs, refs = refs[:n_sent], refs[n_sent:]
    (
        fields, drop, grad_table, rows_table,
        mask_grad_ref,
        sems, codes_v, codes, sums, mask_grad_out,
    ) = refs
    codes_of(sent_refs, codes_v)
    (get_codes,) = copies(sems, (codes_v, codes))
    packed = fold_refs[0][: M // 2]
    for ref in fold_refs[1:]:
        packed = packed + ref[: M // 2].astype(f32)
    other = swap(packed)
    low_half = lane_of(packed.shape) < M
    grid = jnp.concatenate(
        [jnp.where(low_half, packed, other), jnp.where(low_half, other, packed)], 0
    )
    for number in range(2):
        sums[number] = jnp.zeros((W, LANES), f32)
    turn = signs(K, 1.0, -1.0)
    even = slot_lanes(K)
    real_or_imag = lane_of((K, LANES)) % M < K
    get_codes.wait()
    drop_rows, drop_cols = book.read(drop, "drop_rows"), book.read(drop, "drop_cols")

    def backward(none, items):
        waves = []
        for ref, place in items:
            for pair in range(PAIRS):
                scaled = [grid * fields[place * MOST + 2 * pair + slot] for slot in range(2)]
                pull = jnp.concatenate(scaled, 1).astype(bf16)
                raw = dot(drop_rows, jnp.concatenate([pull, pull], 0))
                wave = []
                for slot in range(2):
                    mine = raw[:, slot * LANES : (slot + 1) * LANES]
                    wave.append(mine[:K] + turn * swap(mine[K:]))
                waves.append(jnp.concatenate(wave, 1))
        wave = jnp.concatenate(waves, 0).astype(bf16)
        back = dot(jnp.concatenate([wave, wave], 1), drop_cols)
        number = 0
        for ref, place in items:
            weights = ref[pl.ds(AT_TAIL, 16), :].astype(f32) * (2.0 / K)
            for pair in range(PAIRS):
                mine = back[number * K : (number + 1) * K]
                number += 1
                real, imag = pair_parts(ref, pair)
                product = real * mine[:, :LANES] + imag * mine[:, LANES:]
                product = weights[TAIL_PAIR + pair : TAIL_PAIR + pair + 1] * product
                for slot in range(2):
                    row, col = window_of(codes, place, 2 * pair + slot)
                    keep = even if slot == 0 else jnp.logical_not(even)
                    shift = lax.rem(col + LANES - slot * K, LANES)
                    moved = pltpu.roll(jnp.where(keep, product, 0.0), shift, 1)
                    sums[slot, pl.ds(row, K), :] += moved
        return none

    over_owners(sent_refs, backward, 0)
    grad_cols = book.read(grad_table, "grad_cols")
    grad = sums[0] + sums[1]
    turn = signs(W, 1.0, -1.0)
    high, low = split(jnp.concatenate([grad * turn, -swap(grad)], 0))
    half = dot(book.read(rows_table, "grad_rows"), jnp.concatenate([high, high, low], 0))
    half = half.astype(bf16)
    both = jnp.concatenate([half, half], 1)
    chunk = grad_cols.shape[1] // PIECES
    puts = []
    for piece in range(PIECES):
        here = slice(piece * chunk, (piece + 1) * chunk)
        mask_grad_out[:, here] = dot(both, grad_cols[:, here])
        place = mask_grad_ref.at[0, :, pl.ds(piece * chunk, chunk)]
        puts.append(
            pltpu.make_async_copy(mask_grad_out.at[:, pl.ds(piece * chunk, chunk)], place, sems.at[1 + piece])
        )
        puts[-1].start()
    for put in puts:
        put.wait()


VMEM = pl.BlockSpec(memory_space=pltpu.VMEM)
SMEM = pl.BlockSpec(memory_space=pltpu.SMEM)
HBM = pl.BlockSpec(memory_space=pltpu.HBM)


def room(kib):
    return pltpu.CompilerParams(vmem_limit_bytes=(64 * 1024 - kib) * 1024)


def in_hbm(value):
    return pltpu.with_memory_space_constraint(value, pltpu.HBM)


def exchange(value, axis, step):
    return lax.ppermute(value, axis, [(i, i ^ step) for i in range(lax.axis_size(axis))])


def others(value, axis):
    return [exchange(value, axis, step) for step in range(1, lax.axis_size(axis))]


def like(value):
    return pltpu.VMEM(value.shape, value.dtype)


def shards(
    mask, target, tile_class, thresholds, source_pupil, source_weight, source_cell, active_count
):
    span, period = mask.shape[1:]
    slots = source_pupil.shape[0]
    src_count = lax.axis_size("src")
    few = src_count in (2, 4)
    spec_cols, spec_rows, book = tables(period, span)
    pages = jnp.asarray(book.pages)
    src = lax.axis_index("src")
    sems = pltpu.SemaphoreType.DMA
    smem = pltpu.SMEM

    part, sent, threshold = pl.pallas_call(
        spectrum_kernel,
        in_specs=[HBM] * 5 + [SMEM] + [HBM] * 3,
        out_specs=[VMEM] * 3,
        out_shape=[
            jax.ShapeDtypeStruct((W, LANES), f32),
            jax.ShapeDtypeStruct((ROWS - AT_PUPILS, LANES), bf16),
            jax.ShapeDtypeStruct((8, LANES), f32),
        ],
        scratch_shapes=[
            like(mask[0]),
            like(source_pupil[:16]),
            like(source_weight),
            smem(source_cell.shape, jnp.int32),
            smem(active_count.shape, jnp.int32),
            smem(thresholds.shape, f32),
            like(spec_cols),
            like(spec_rows[0]),
            sems((8,)),
            pltpu.VMEM((LANES, LANES), f32),
            pltpu.VMEM((PAIRS * K, LANES), f32),
        ],
        compiler_params=room(24576),
        name="spectrum",
    )(
        *map(in_hbm, (mask, source_pupil, source_weight, source_cell, active_count)),
        tile_class,
        *map(in_hbm, (thresholds, jnp.asarray(spec_cols), jnp.asarray(spec_rows))),
    )
    from_pix = others(part, "pix")
    sent = pl.pallas_call(
        pack_kernel,
        in_specs=[VMEM] * (2 + len(from_pix)),
        out_specs=VMEM,
        out_shape=jax.ShapeDtypeStruct((ROWS, LANES), bf16),
        compiler_params=room(32768),
        name="pack",
    )(part, *from_pix, sent)
    if few:
        parcels = [sent] + others(sent, "src")
    else:
        parcels = [lax.all_gather(sent, "src")]

    late_target, late_pages, _ = lax.optimization_barrier((target, pages, sent))
    staged_shapes = [
        jax.ShapeDtypeStruct((span, period), f32),
        *book.shapes(LIFT, FINE, DROP, GRAD, IMAGE_ROWS + book.blocks),
        *book.shapes(IMAGE_ROWS) * lax.axis_size("pix"),
    ]
    staged = pl.pallas_call(
        functools.partial(stage_kernel, book),
        in_specs=[HBM] * 2,
        out_specs=[VMEM] * len(staged_shapes),
        out_shape=staged_shapes,
        scratch_shapes=[sems((len(staged_shapes),))],
        compiler_params=room(24576),
        name="stage",
    )(in_hbm(late_target), in_hbm(late_pages))
    near_target, lift, fine, *for_gradient = staged[:6]
    early_target, _ = lax.optimization_barrier((target, from_pix[0]))
    targets = [near_target] + others(early_target[0], "pix")
    image_rows = staged[6:]

    numbers = src_count * MOST
    owners_up = -(-src_count // 8) * 8
    fold_rows = M // 2 + (1 if few else src_count) * SUMS
    fold_count = src_count if few else 1
    codes = [pltpu.VMEM((owners_up, LANES), jnp.int32), smem((owners_up, LANES), jnp.int32)]
    intensity, fields, *folded = pl.pallas_call(
        functools.partial(image_kernel, book, len(parcels), len(targets)),
        in_specs=[VMEM] * (len(parcels) + 2 * len(targets) + 3),
        out_specs=[HBM, VMEM] + [VMEM] * fold_count,
        out_shape=[
            jax.ShapeDtypeStruct((1, span, period), f32),
            jax.ShapeDtypeStruct((numbers, M, LANES), f32),
            jax.ShapeDtypeStruct((fold_rows, LANES), f32),
            *[jax.ShapeDtypeStruct((M // 2 + 2 * SUMS, LANES), bf16)] * (fold_count - 1),
        ],
        scratch_shapes=[
            sems((2,)),
            *codes,
            pltpu.VMEM((W, LANES), f32),
            like(target[0]),
        ],
        compiler_params=room(24576),
        name="image",
    )(*parcels, *targets, *image_rows, threshold, lift, fine)

    if few:
        folds = [
            value if step == 0 else exchange(value, "src", step)
            for step, value in enumerate(folded)
        ]
        rows = folds[0][M // 2 :]
        for fold in folds[1:]:
            sums = fold[M // 2 :].astype(f32)
            rows = rows + (sums[:SUMS] + sums[SUMS:])
    else:
        folds = [lax.psum(folded[0], "src")]
        rows = lax.dynamic_slice_in_dim(folds[0], M // 2 + src * SUMS, SUMS, 0)
    for other in others(rows, "tile"):
        rows = rows + other
    mask_grad = pl.pallas_call(
        functools.partial(gradient_kernel, book, len(folds), len(parcels)),
        in_specs=[VMEM] * (len(folds) + len(parcels) + 1 + len(for_gradient)),
        out_specs=HBM,
        out_shape=jax.ShapeDtypeStruct((1, span, period), f32),
        scratch_shapes=[
            sems((1 + PIECES,)),
            *codes,
            pltpu.VMEM((2, W, LANES), f32),
            like(mask[0]),
        ],
        compiler_params=room(24576),
        name="gradient",
    )(*folds, *parcels, fields, *for_gradient)
    sums = jnp.sum(rows, 1) * (1.0 / (period * K))
    source_grad = jnp.zeros((slots,), f32).at[:SUMS].set(sums)
    return intensity, mask_grad, source_grad


def solution(mesh):
    in_specs = (
        P(("groups", "tile"), ("src", "pix"), None),
        P(("groups", "tile"), ("src", "pix"), None),
        P(("groups", "tile")),
        P(),
        P("src", None),
        P("src"),
        P("src"),
        P(),
    )
    out_specs = (
        P(("groups", "tile"), ("src", "pix"), None),
        P(("groups", "tile"), ("src", "pix"), None),
        P(("groups", "src")),
    )
    return jax.shard_map(shards, mesh=mesh, in_specs=in_specs, out_specs=out_specs, check_vma=False)
```

```python
import functools

import jax
import jax.numpy as jnp
import ml_dtypes
import numpy as np
from jax import lax
from jax.experimental import pallas as pl
from jax.experimental.pallas import tpu as pltpu
from jax.sharding import PartitionSpec as P

K = 32
SG = 17
W = 48
MOST = 6
CLASSES = 4
STEEP = 4.0

M = 64
LANES = 128
PAIRS = MOST // 2
AT_PUPILS = W
ROWS = AT_PUPILS + PAIRS * K
FACTS = M - 1
PIECES = 4
SUMS = 8

f32 = jnp.float32
bf16 = jnp.bfloat16


def split_np(table):
    table = np.asarray(table, np.float32)
    high = table.astype(ml_dtypes.bfloat16)
    low = (table - high.astype(np.float32)).astype(ml_dtypes.bfloat16)
    return high, low


def halves(left, right):
    out = np.zeros((left.shape[0], LANES))
    out[:, : left.shape[1]] = left
    out[:, M : M + right.shape[1]] = right
    return out


@functools.lru_cache(maxsize=None)
def tables(period, span):
    blocks = period // span
    freqs = np.arange(W) - W // 2
    pixels = np.arange(period)
    wide = 2.0 * np.pi / period * ((freqs[:, None] * pixels[None, :]) % period)
    wide_cos, wide_sin = np.cos(wide), np.sin(wide)
    narrow = np.arange(K) - K // 2
    coarse = 2.0 * np.pi / M * ((narrow[:, None] * np.arange(M)[None, :]) % M)
    coarse_cos, coarse_sin = np.cos(coarse), np.sin(coarse)
    near = 2.0 * np.pi / period * ((narrow[:, None] * pixels[None, :]) % period)
    gain = sum(
        (wave * wave.astype(np.float32).astype(ml_dtypes.bfloat16).astype(np.float64)).mean(1)
        for wave in (np.cos(near), np.sin(near))
    )
    rounded_cos, rounded_sin = gain[:, None] * coarse_cos, gain[:, None] * coarse_sin
    high, low = split_np(halves(wide_cos.T, -wide_sin.T))
    spec_cols = np.concatenate([high, low], 1)
    rows = np.concatenate(
        [wide_cos.reshape(W, blocks, span), wide_sin.reshape(W, blocks, span)], 2
    ).transpose(1, 0, 2)
    high, low = split_np(rows / period)
    spec_rows = np.concatenate([high, low], 1)
    def pair_table(cos, sin):
        out = np.zeros((4 * K, 4 * M))
        for slot in range(2):
            real, imag, at = slot * K, (2 + slot) * K, slot * 2 * M
            out[real : real + K, at : at + 2 * M] = np.concatenate([cos, sin], 1)
            out[imag : imag + K, at : at + 2 * M] = np.concatenate([-sin, cos], 1)
        return out

    lift = pair_table(rounded_cos, rounded_sin)
    turned = pair_table(-rounded_sin, rounded_cos)
    high, low = split_np(np.concatenate([lift, turned], 1))
    lift_cols = np.concatenate([high, low], 0)
    lift_rows = np.concatenate(split_np(rounded_cos.T / K) + split_np(rounded_sin.T / K), 1)
    orders = np.arange(-(M // 2 - 1), M // 2)
    places = pixels[:, None] * (M / period) - np.arange(M)[None, :]
    inter = np.cos(2.0 * np.pi / M * places[:, :, None] * orders).sum(-1) / M
    high, low = split_np(inter)
    fine_cols = np.concatenate([high.T, low.T, high.T, low.T], 0)
    fold_cols = np.concatenate([high, low], 1)
    fine_rows = np.concatenate([high, low, high, low], 1).reshape(blocks, span, 4 * M)
    high_t = high.reshape(blocks, span, M).transpose(0, 2, 1)
    low_t = low.reshape(blocks, span, M).transpose(0, 2, 1)
    fold_rows = np.concatenate([high_t, low_t, high_t], 2)
    high, low = split_np(np.concatenate([rounded_cos, rounded_sin], 0))
    drop_rows = np.concatenate([high, low], 1)
    drop = pair_table(coarse_cos, coarse_sin).T
    drop = np.concatenate([drop, drop[:, M:], -drop[:, :M]], 1)
    high, low = split_np(drop)
    drop_cols = np.concatenate([high, low], 0)
    rows = np.concatenate(
        [
            wide_cos.reshape(W, blocks, span).transpose(1, 2, 0),
            wide_sin.reshape(W, blocks, span).transpose(1, 2, 0),
        ],
        2,
    )
    high, low = split_np(rows / period)
    grad_rows = np.concatenate([high, low, high], 2)
    padded = [np.pad(part, ((0, M - W), (0, 0))) for part in (wide_cos, wide_sin)]
    high, low = split_np(np.concatenate(padded, 0))
    grad_cols = np.concatenate([high, low], 0)
    chapters = [
        dict(lift_cols=lift_cols, lift_rows=lift_rows),
        dict(fine_cols=fine_cols, fold_cols=fold_cols),
        dict(drop_rows=drop_rows, drop_cols=drop_cols),
        dict(grad_cols=grad_cols),
    ]
    for block in range(blocks):
        chapters.append(dict(fine_rows=fine_rows[block], fold_rows=fold_rows[block]))
    for block in range(blocks):
        chapters.append(dict(grad_rows=grad_rows[block]))
    pages, starts, places, at = [], [], {}, 0
    for chapter in chapters:
        starts.append(at)
        for name, value in chapter.items():
            places[name] = (at - starts[-1], value.shape)
            for lane in range(0, value.shape[1], LANES):
                page = value[:, lane : lane + LANES]
                pages.append(np.pad(page, ((0, 0), (0, LANES - page.shape[1]))))
                at += page.shape[0]
    starts.append(at)
    return spec_cols, spec_rows, Book(np.concatenate(pages, 0), starts, places, blocks)


class Book:
    def __init__(self, pages, starts, places, blocks):
        self.pages, self.starts, self.places, self.blocks = pages, starts, places, blocks

    def rows(self, chapter):
        return self.starts[chapter + 1] - self.starts[chapter]

    def shapes(self, *chapters):
        return [jax.ShapeDtypeStruct((self.rows(chapter), LANES), bf16) for chapter in chapters]

    def where(self, ref, chapter, block=0):
        return ref.at[pl.ds(self.starts[chapter] + block * self.rows(chapter), self.rows(chapter))]

    def read(self, ref, name):
        at, (rows, lanes) = self.places[name]
        pages = [
            ref[at + number * rows : at + (number + 1) * rows, : min(LANES, lanes - lane)]
            for number, lane in enumerate(range(0, lanes, LANES))
        ]
        return pages[0] if len(pages) == 1 else jnp.concatenate(pages, 1)


LIFT, FINE, DROP, GRAD, IMAGE_ROWS = range(5)


def dot(left, right):
    return jnp.dot(left, right, preferred_element_type=f32)


def split(value):
    high = value.astype(bf16)
    return high, (value - high.astype(f32)).astype(bf16)


def lane_of(shape):
    return lax.broadcasted_iota(jnp.int32, shape, len(shape) - 1)


def row_of(shape):
    return lax.broadcasted_iota(jnp.int32, shape, 0)


def swap(value):
    return pltpu.roll(value, M, 1)


def signs(rows, low, high):
    return jnp.where(lane_of((rows, LANES)) < M, f32(low), f32(high))


def place_is_static(place):
    return isinstance(place, int)


def my_block():
    return lax.axis_index("src") * lax.axis_size("pix") + lax.axis_index("pix")


def chip_blocks():
    pix, count = lax.axis_index("pix"), lax.axis_size("pix")
    base = lax.axis_index("src") * count
    return [base + jnp.bitwise_xor(pix, step) for step in range(count)]


def copies(sems, *pairs):
    out = [
        pltpu.make_async_copy(source, place, sems.at[number])
        for number, (source, place) in enumerate(pairs)
    ]
    for copy in out:
        copy.start()
    return out


def spectrum_kernel(
    mask_ref, pupil_ref, weight_ref, cell_ref, active_ref, class_ref, thresholds_ref,
    cols_ref, rows_ref,
    part_ref, sent_ref, threshold_ref,
    mask_in, pupil_in, weight_in, cell_in, active_in, thresholds, cols, rows,
    sems, lined, paired,
):
    (
        get_pupil, get_mask, get_cols, get_active, get_cell, get_weight, get_rows,
        get_thresholds,
    ) = copies(
        sems,
        (pupil_ref.at[pl.ds(0, 16)], pupil_in),
        (mask_ref.at[0], mask_in),
        (cols_ref, cols),
        (active_ref, active_in),
        (cell_ref, cell_in),
        (weight_ref, weight_in),
        (rows_ref.at[my_block()], rows),
        (thresholds_ref, thresholds),
    )
    get_active.wait()
    get_cell.wait()
    get_pupil.wait()
    get_weight.wait()
    active = active_in[lax.axis_index("src")]
    raw = pupil_in[...].astype(f32)[:8]
    raw = jnp.where(row_of(raw.shape) < active, raw, 0.0)
    for piece in range(16):
        lined[pl.ds(piece, 8, stride=16), :] = raw[:, piece * LANES : (piece + 1) * LANES]
    quarter = lane_of((8, LANES)) // K
    for pair in range(PAIRS):
        first, second = pair * 32, pair * 32 + 16
        quarters = [lined[pl.ds(start, 8), :] for start in (first, second, first + 8, second + 8)]
        for turn in range(4):
            moved = [
                value if number == turn else pltpu.roll(value, K * (number - turn) % LANES, 1)
                for number, value in enumerate(quarters)
            ]
            out = moved[3]
            for number in range(3):
                out = jnp.where(quarter == number, moved[number], out)
            paired[pl.ds(pair * K + turn, 8, stride=4), :] = out
    sent_ref[: PAIRS * K] = paired[...].astype(bf16)
    shape = (8, LANES)
    weights = jnp.broadcast_to(weight_in[...].astype(f32).reshape(1, -1)[:, :LANES], shape)
    column = jnp.sum(jnp.where(row_of(shape) == lane_of(shape), weights, 0.0), 1, keepdims=True)
    row_code, col_code = jnp.zeros(shape, f32), jnp.zeros(shape, f32)
    for slot in range(MOST):
        cell = cell_in[slot]
        row_code = jnp.where(row_of(shape) == slot, lax.div(cell, SG).astype(f32), row_code)
        col_code = jnp.where(row_of(shape) == slot, lax.rem(cell, SG).astype(f32), col_code)
    facts = [jnp.broadcast_to(column, shape), row_code, col_code, jnp.zeros((W - 24, LANES), f32)]
    sent_ref[PAIRS * K :] = jnp.concatenate(facts, 0).astype(bf16)
    get_mask.wait()
    get_cols.wait()
    get_rows.wait()
    high, low = split(mask_in[...])
    both = dot(high, cols[...])
    part = both[:, :LANES] + both[:, LANES:] + dot(low, cols[:, :LANES])
    turned = swap(part) * signs(part.shape[0], 1.0, -1.0)
    high, low = split(jnp.concatenate([part, turned], 0))
    product = dot(rows[...], jnp.concatenate([high, low], 1))
    part_ref[...] = product[:W, :LANES] + product[:W, LANES:] + product[W:, :LANES]
    get_thresholds.wait()
    kind = class_ref[0]
    threshold = thresholds[0]
    for number in range(1, CLASSES):
        threshold = jnp.where(kind == number, thresholds[number], threshold)
    threshold_ref[...] = jnp.full(threshold_ref.shape, threshold, f32)


def pack_kernel(part_ref, *refs):
    *other_refs, sent_ref, out_ref = refs
    part = part_ref[...]
    for ref in other_refs:
        part = part + ref[...]
    high, low = split(part)
    rest = pltpu.roll(low.astype(f32), K, 1)
    lane = lane_of(part.shape)
    mixed = jnp.where(lane % M < W, high.astype(f32), rest)
    facts = sent_ref[PAIRS * K :].astype(f32)
    out_ref[:W] = jnp.where(lane == FACTS, facts, mixed).astype(bf16)
    out_ref[AT_PUPILS:] = sent_ref[: PAIRS * K]


def stage_kernel(book, target_ref, book_ref, *refs):
    *out_refs, sems = refs
    target_out, lift_out, fine_out, drop_out, grad_out, grad_rows_out, *rows_out = out_refs
    gets = copies(
        sems,
        (book.where(book_ref, LIFT), lift_out),
        (book.where(book_ref, FINE), fine_out),
        (target_ref.at[0], target_out),
        *(
            (book.where(book_ref, IMAGE_ROWS, block), out)
            for block, out in zip(chip_blocks(), rows_out)
        ),
        (book.where(book_ref, DROP), drop_out),
        (book.where(book_ref, GRAD), grad_out),
        (book.where(book_ref, IMAGE_ROWS + book.blocks, my_block()), grad_rows_out),
    )
    for get in gets:
        get.wait()


def over_owners(refs, body, carry):
    if len(refs) > 1:
        return body(carry, [(ref, place) for place, ref in enumerate(refs)])
    (ref,) = refs
    return lax.fori_loop(
        0, ref.shape[0], lambda owner, carry: body(carry, [(ref.at[owner], owner)]), carry
    )


def codes_of(refs, codes_v):
    def body(none, items):
        for ref, place in items:
            facts = ref[:W].astype(f32)[:, FACTS : FACTS + 1]
            shape = (8, LANES)
            code = jnp.broadcast_to(facts[8:16] * 32.0 + facts[16:24], shape)
            code = jnp.sum(jnp.where(row_of(shape) == lane_of(shape), code, 0.0), 0, keepdims=True)
            codes_v[pl.ds(place, 1), :] = code.astype(jnp.int32)
        return none

    over_owners(refs, body, 0)


def weights_of(ref):
    return jnp.broadcast_to(ref[:16].astype(f32)[:8, FACTS : FACTS + 1], (8, LANES))


def window_of(codes, place, slot):
    code = codes[place, slot]
    return lax.div(code, 32), lax.rem(code, 32)


def pair_parts(ref, pair):
    value = ref[pl.ds(AT_PUPILS + pair * K, K), :].astype(f32)
    other = swap(value)
    low = lane_of(value.shape) < M
    return jnp.where(low, value, other), jnp.where(low, other, value)


def slot_lanes(rows):
    return lane_of((rows, LANES)) // K % 2 == 0


def image_kernel(book, n_sent, n_pix, *refs):
    sent_refs, refs = refs[:n_sent], refs[n_sent:]
    targets, refs = refs[:n_pix], refs[n_pix:]
    rows_refs, refs = refs[:n_pix], refs[n_pix:]
    (
        threshold_ref, lift, fine,
        intensity_ref, fields, *fold_refs,
        sems, codes_v, codes, spectrum, intensity_out,
    ) = refs
    codes_of(sent_refs, codes_v)
    (get_codes,) = copies(sems, (codes_v, codes))

    def gather(total, items):
        for ref, place in items:
            value = ref[:W].astype(f32)
            lane = lane_of(value.shape)
            rest = jnp.where((lane % M < W) | (lane == FACTS), 0.0, value)
            total = total + (value + pltpu.roll(rest, LANES - K, 1))
        return total

    spectrum[...] = over_owners(sent_refs, gather, jnp.zeros((W, LANES), f32))
    if len(sent_refs) == 1:
        get_codes.wait()
    lift_cols, lift_rows = book.read(lift, "lift_cols"), book.read(lift, "lift_rows")
    even = slot_lanes(K)
    turn_low = signs(K, -1.0, 1.0)

    def forward(total, items):
        waves = []
        parts = [pair_parts(ref, pair) for ref, place in items for pair in range(PAIRS)]
        if len(items) > 1:
            get_codes.wait()
        for ref, place in items:
            for pair in range(PAIRS):
                real, imag = parts.pop(0)
                row, col = window_of(codes, place, 2 * pair)
                left = pltpu.roll(spectrum[pl.ds(row, K), :], lax.rem(LANES - col, LANES), 1)
                row, col = window_of(codes, place, 2 * pair + 1)
                right = pltpu.roll(spectrum[pl.ds(row, K), :], lax.rem(LANES + K - col, LANES), 1)
                window = jnp.where(even, left, right)
                waves.append((real * window + imag * (turn_low * swap(window))).astype(bf16))
        wave = jnp.concatenate(waves, 0)
        wave = dot(jnp.concatenate([wave, wave], 1), lift_cols).astype(bf16)
        number = 0
        for ref, place in items:
            weights = weights_of(ref)
            for pair in range(PAIRS):
                here = slice(number * K, (number + 1) * K)
                number += 1
                own, turned = wave[here, : 2 * LANES], wave[here, 2 * LANES :]
                raw = dot(lift_rows, jnp.concatenate([own, own, turned, turned], 0))
                for slot in range(2):
                    field = raw[:, slot * LANES : (slot + 1) * LANES]
                    fields[place * MOST + 2 * pair + slot] = field
                    at = 2 * pair + slot
                    total = total + weights[at : at + 1] * (field * field)
        return total

    power = over_owners(sent_refs, forward, jnp.zeros((M, LANES), f32))
    high, low = split(power + swap(power))
    coarse = jnp.concatenate([high, high, low, low], 0)
    fine_cols, fold_cols = book.read(fine, "fine_cols"), book.read(fine, "fold_cols")
    threshold = threshold_ref[:1, :1]
    grid = jnp.zeros((M, LANES), f32)
    fine_rows = [book.read(rows_ref, "fine_rows") for rows_ref in rows_refs]
    high, low = split(dot(jnp.concatenate(fine_rows, 0), coarse))
    intensities = dot(jnp.concatenate([high, low], 1), fine_cols)
    span = intensity_out.shape[0]
    intensity_out[...] = intensities[:span]
    put = pltpu.make_async_copy(intensity_out, intensity_ref.at[0], sems.at[1])
    put.start()
    slopes = []
    for number, target in enumerate(targets):
        intensity = intensities[number * span : (number + 1) * span]
        resist = 1.0 / (1.0 + jnp.exp(-STEEP * (intensity - threshold)))
        slope = 2.0 * STEEP * (resist - target[...]) * resist * (1.0 - resist)
        slopes.append(slope.astype(bf16))
    folded = dot(jnp.concatenate(slopes, 0), fold_cols)
    high, low = split(folded + swap(folded))
    for number, rows_ref in enumerate(rows_refs):
        here = slice(number * span, (number + 1) * span)
        grid = grid + dot(
            book.read(rows_ref, "fold_rows"),
            jnp.concatenate([high[here], high[here], low[here]], 0),
        )
    lane = lane_of((M // 2, LANES))
    packed = jnp.where(lane < M, grid[: M // 2], grid[M // 2 :])
    for fold_ref in fold_refs:
        fold_ref[: M // 2] = packed.astype(fold_ref.dtype)

    def weigh(none, items):
        for ref, place in items:
            sums = []
            for slot in range(MOST):
                field = fields[place * MOST + slot]
                sums.append(jnp.sum(grid * (field * field), 0, keepdims=True))
            sums = jnp.concatenate(sums + [jnp.zeros((SUMS - MOST, LANES), f32)], 0)
            if place_is_static(place) and place > 0:
                high, low = split(sums)
                fold_refs[place][M // 2 :] = jnp.concatenate([high, low], 0)
            elif len(fold_refs) > 1:
                fold_refs[place][M // 2 :] = sums
            else:
                start = pl.multiple_of(M // 2 + place * SUMS, SUMS)
                fold_refs[0][pl.ds(start, SUMS), :] = sums
        return none

    over_owners(sent_refs, weigh, 0)
    put.wait()


def gradient_kernel(book, n_fold, n_sent, *refs):
    fold_refs, refs = refs[:n_fold], refs[n_fold:]
    sent_refs, refs = refs[:n_sent], refs[n_sent:]
    (
        fields, drop, grad_table, rows_table,
        mask_grad_ref,
        sems, codes_v, codes, sums, mask_grad_out,
    ) = refs
    codes_of(sent_refs, codes_v)
    (get_codes,) = copies(sems, (codes_v, codes))
    packed = fold_refs[0][: M // 2]
    for ref in fold_refs[1:]:
        packed = packed + ref[: M // 2].astype(f32)
    other = swap(packed)
    low_half = lane_of(packed.shape) < M
    grid = jnp.concatenate(
        [jnp.where(low_half, packed, other), jnp.where(low_half, other, packed)], 0
    )
    for number in range(2):
        sums[number] = jnp.zeros((W, LANES), f32)
    turn = signs(K, 1.0, -1.0)
    even = slot_lanes(K)
    real_or_imag = lane_of((K, LANES)) % M < K
    get_codes.wait()
    drop_rows, drop_cols = book.read(drop, "drop_rows"), book.read(drop, "drop_cols")

    def backward(none, items):
        waves = []
        for ref, place in items:
            for pair in range(PAIRS):
                scaled = [grid * fields[place * MOST + 2 * pair + slot] for slot in range(2)]
                pull = jnp.concatenate(scaled, 1).astype(bf16)
                raw = dot(drop_rows, jnp.concatenate([pull, pull], 0))
                wave = []
                for slot in range(2):
                    mine = raw[:, slot * LANES : (slot + 1) * LANES]
                    wave.append(mine[:K] + turn * swap(mine[K:]))
                waves.append(jnp.concatenate(wave, 1))
        wave = jnp.concatenate(waves, 0).astype(bf16)
        back = dot(jnp.concatenate([wave, wave], 1), drop_cols)
        number = 0
        for ref, place in items:
            weights = weights_of(ref) * (2.0 / K)
            for pair in range(PAIRS):
                mine = back[number * K : (number + 1) * K]
                number += 1
                real, imag = pair_parts(ref, pair)
                product = real * mine[:, :LANES] + imag * mine[:, LANES:]
                first, second = weights[2 * pair : 2 * pair + 1], weights[2 * pair + 1 : 2 * pair + 2]
                product = jnp.where(even[:1], first, second) * product
                for slot in range(2):
                    row, col = window_of(codes, place, 2 * pair + slot)
                    keep = even if slot == 0 else jnp.logical_not(even)
                    shift = lax.rem(col + LANES - slot * K, LANES)
                    moved = pltpu.roll(jnp.where(keep, product, 0.0), shift, 1)
                    sums[slot, pl.ds(row, K), :] += moved
        return none

    over_owners(sent_refs, backward, 0)
    grad_cols = book.read(grad_table, "grad_cols")
    grad = sums[0] + sums[1]
    turn = signs(W, 1.0, -1.0)
    high, low = split(jnp.concatenate([grad * turn, -swap(grad)], 0))
    half = dot(book.read(rows_table, "grad_rows"), jnp.concatenate([high, high, low], 0))
    half = half.astype(bf16)
    both = jnp.concatenate([half, half], 1)
    chunk = grad_cols.shape[1] // PIECES
    puts = []
    for piece in range(PIECES):
        here = slice(piece * chunk, (piece + 1) * chunk)
        mask_grad_out[:, here] = dot(both, grad_cols[:, here])
        place = mask_grad_ref.at[0, :, pl.ds(piece * chunk, chunk)]
        puts.append(
            pltpu.make_async_copy(mask_grad_out.at[:, pl.ds(piece * chunk, chunk)], place, sems.at[1 + piece])
        )
        puts[-1].start()
    for put in puts:
        put.wait()


VMEM = pl.BlockSpec(memory_space=pltpu.VMEM)
SMEM = pl.BlockSpec(memory_space=pltpu.SMEM)
HBM = pl.BlockSpec(memory_space=pltpu.HBM)


def room(kib):
    return pltpu.CompilerParams(vmem_limit_bytes=(64 * 1024 - kib) * 1024)


def in_hbm(value):
    return pltpu.with_memory_space_constraint(value, pltpu.HBM)


def exchange(value, axis, step):
    return lax.ppermute(value, axis, [(i, i ^ step) for i in range(lax.axis_size(axis))])


def others(value, axis):
    return [exchange(value, axis, step) for step in range(1, lax.axis_size(axis))]


def like(value):
    return pltpu.VMEM(value.shape, value.dtype)


def shards(
    mask, target, tile_class, thresholds, source_pupil, source_weight, source_cell, active_count
):
    span, period = mask.shape[1:]
    slots = source_pupil.shape[0]
    src_count = lax.axis_size("src")
    few = src_count in (2, 4)
    spec_cols, spec_rows, book = tables(period, span)
    pages = jnp.asarray(book.pages)
    src = lax.axis_index("src")
    sems = pltpu.SemaphoreType.DMA
    smem = pltpu.SMEM

    part, sent, threshold = pl.pallas_call(
        spectrum_kernel,
        in_specs=[HBM] * 5 + [SMEM] + [HBM] * 3,
        out_specs=[VMEM] * 3,
        out_shape=[
            jax.ShapeDtypeStruct((W, LANES), f32),
            jax.ShapeDtypeStruct((PAIRS * K + W, LANES), bf16),
            jax.ShapeDtypeStruct((8, LANES), f32),
        ],
        scratch_shapes=[
            like(mask[0]),
            like(source_pupil[:16]),
            like(source_weight),
            smem(source_cell.shape, jnp.int32),
            smem(active_count.shape, jnp.int32),
            smem(thresholds.shape, f32),
            like(spec_cols),
            like(spec_rows[0]),
            sems((8,)),
            pltpu.VMEM((LANES, LANES), f32),
            pltpu.VMEM((PAIRS * K, LANES), f32),
        ],
        compiler_params=room(24576),
        name="spectrum",
    )(
        *map(in_hbm, (mask, source_pupil, source_weight, source_cell, active_count)),
        tile_class,
        *map(in_hbm, (thresholds, jnp.asarray(spec_cols), jnp.asarray(spec_rows))),
    )
    from_pix = others(part, "pix")
    sent = pl.pallas_call(
        pack_kernel,
        in_specs=[VMEM] * (2 + len(from_pix)),
        out_specs=VMEM,
        out_shape=jax.ShapeDtypeStruct((ROWS, LANES), bf16),
        compiler_params=room(32768),
        name="pack",
    )(part, *from_pix, sent)
    if few:
        parcels = [sent] + others(sent, "src")
    else:
        parcels = [lax.all_gather(sent, "src")]

    late_target, late_pages, _ = lax.optimization_barrier((target, pages, sent))
    staged_shapes = [
        jax.ShapeDtypeStruct((span, period), f32),
        *book.shapes(LIFT, FINE, DROP, GRAD, IMAGE_ROWS + book.blocks),
        *book.shapes(IMAGE_ROWS) * lax.axis_size("pix"),
    ]
    staged = pl.pallas_call(
        functools.partial(stage_kernel, book),
        in_specs=[HBM] * 2,
        out_specs=[VMEM] * len(staged_shapes),
        out_shape=staged_shapes,
        scratch_shapes=[sems((len(staged_shapes),))],
        compiler_params=room(24576),
        name="stage",
    )(in_hbm(late_target), in_hbm(late_pages))
    near_target, lift, fine, *for_gradient = staged[:6]
    early_target, _ = lax.optimization_barrier((target, from_pix[0]))
    targets = [near_target] + others(early_target[0], "pix")
    image_rows = staged[6:]

    numbers = src_count * MOST
    owners_up = -(-src_count // 8) * 8
    fold_rows = M // 2 + (1 if few else src_count) * SUMS
    fold_count = src_count if few else 1
    codes = [pltpu.VMEM((owners_up, LANES), jnp.int32), smem((owners_up, LANES), jnp.int32)]
    intensity, fields, *folded = pl.pallas_call(
        functools.partial(image_kernel, book, len(parcels), len(targets)),
        in_specs=[VMEM] * (len(parcels) + 2 * len(targets) + 3),
        out_specs=[HBM, VMEM] + [VMEM] * fold_count,
        out_shape=[
            jax.ShapeDtypeStruct((1, span, period), f32),
            jax.ShapeDtypeStruct((numbers, M, LANES), f32),
            jax.ShapeDtypeStruct((fold_rows, LANES), f32),
            *[jax.ShapeDtypeStruct((M // 2 + 2 * SUMS, LANES), bf16)] * (fold_count - 1),
        ],
        scratch_shapes=[
            sems((2,)),
            *codes,
            pltpu.VMEM((W, LANES), f32),
            like(target[0]),
        ],
        compiler_params=room(24576),
        name="image",
    )(*parcels, *targets, *image_rows, threshold, lift, fine)

    if few:
        folds = [
            value if step == 0 else exchange(value, "src", step)
            for step, value in enumerate(folded)
        ]
        rows = folds[0][M // 2 :]
        for fold in folds[1:]:
            sums = fold[M // 2 :].astype(f32)
            rows = rows + (sums[:SUMS] + sums[SUMS:])
    else:
        folds = [lax.psum(folded[0], "src")]
        rows = lax.dynamic_slice_in_dim(folds[0], M // 2 + src * SUMS, SUMS, 0)
    for other in others(rows, "tile"):
        rows = rows + other
    mask_grad = pl.pallas_call(
        functools.partial(gradient_kernel, book, len(folds), len(parcels)),
        in_specs=[VMEM] * (len(folds) + len(parcels) + 1 + len(for_gradient)),
        out_specs=HBM,
        out_shape=jax.ShapeDtypeStruct((1, span, period), f32),
        scratch_shapes=[
            sems((1 + PIECES,)),
            *codes,
            pltpu.VMEM((2, W, LANES), f32),
            like(mask[0]),
        ],
        compiler_params=room(24576),
        name="gradient",
    )(*folds, *parcels, fields, *for_gradient)
    sums = jnp.sum(rows, 1) * (1.0 / (period * K))
    source_grad = jnp.zeros((slots,), f32).at[:SUMS].set(sums)
    return intensity, mask_grad, source_grad


def solution(mesh):
    in_specs = (
        P(("groups", "tile"), ("src", "pix"), None),
        P(("groups", "tile"), ("src", "pix"), None),
        P(("groups", "tile")),
        P(),
        P("src", None),
        P("src"),
        P("src"),
        P(),
    )
    out_specs = (
        P(("groups", "tile"), ("src", "pix"), None),
        P(("groups", "tile"), ("src", "pix"), None),
        P(("groups", "src")),
    )
    return jax.shard_map(shards, mesh=mesh, in_specs=in_specs, out_specs=out_specs, check_vma=False)
```

```python
import functools

import jax
import jax.numpy as jnp
import ml_dtypes
import numpy as np
from jax import lax
from jax.experimental import pallas as pl
from jax.experimental.pallas import tpu as pltpu
from jax.sharding import PartitionSpec as P

K = 32
SG = 17
W = 48
MOST = 6
CLASSES = 4
STEEP = 4.0

M = 64
LANES = 128
PAIRS = MOST // 2
AT_PUPILS = W
ROWS = AT_PUPILS + PAIRS * K
FACTS = M - 1
PIECES = 4
SUMS = 8

f32 = jnp.float32
bf16 = jnp.bfloat16


def split_np(table):
    table = np.asarray(table, np.float32)
    high = table.astype(ml_dtypes.bfloat16)
    low = (table - high.astype(np.float32)).astype(ml_dtypes.bfloat16)
    return high, low


def halves(left, right):
    out = np.zeros((left.shape[0], LANES))
    out[:, : left.shape[1]] = left
    out[:, M : M + right.shape[1]] = right
    return out


@functools.lru_cache(maxsize=None)
def tables(period, span):
    blocks = period // span
    freqs = np.arange(W) - W // 2
    pixels = np.arange(period)
    wide = 2.0 * np.pi / period * ((freqs[:, None] * pixels[None, :]) % period)
    wide_cos, wide_sin = np.cos(wide), np.sin(wide)
    narrow = np.arange(K) - K // 2
    coarse = 2.0 * np.pi / M * ((narrow[:, None] * np.arange(M)[None, :]) % M)
    coarse_cos, coarse_sin = np.cos(coarse), np.sin(coarse)
    near = 2.0 * np.pi / period * ((narrow[:, None] * pixels[None, :]) % period)
    gain = sum(
        (wave * wave.astype(np.float32).astype(ml_dtypes.bfloat16).astype(np.float64)).mean(1)
        for wave in (np.cos(near), np.sin(near))
    )
    rounded_cos, rounded_sin = gain[:, None] * coarse_cos, gain[:, None] * coarse_sin
    high, low = split_np(halves(wide_cos.T, -wide_sin.T))
    spec_cols = np.concatenate([high, low], 1)
    rows = np.concatenate(
        [wide_cos.reshape(W, blocks, span), wide_sin.reshape(W, blocks, span)], 2
    ).transpose(1, 0, 2)
    high, low = split_np(rows / period)
    spec_rows = np.concatenate([high, low], 1)
    def pair_table(cos, sin):
        out = np.zeros((4 * K, 4 * M))
        for slot in range(2):
            real, imag, at = slot * K, (2 + slot) * K, slot * 2 * M
            out[real : real + K, at : at + 2 * M] = np.concatenate([cos, sin], 1)
            out[imag : imag + K, at : at + 2 * M] = np.concatenate([-sin, cos], 1)
        return out

    lift = pair_table(rounded_cos, rounded_sin)
    turned = pair_table(-rounded_sin, rounded_cos)
    high, low = split_np(np.concatenate([lift, turned], 1))
    lift_cols = np.concatenate([high, low], 0)
    lift_rows = np.concatenate(split_np(rounded_cos.T / K) + split_np(rounded_sin.T / K), 1)
    orders = np.arange(-(M // 2 - 1), M // 2)
    places = pixels[:, None] * (M / period) - np.arange(M)[None, :]
    inter = np.cos(2.0 * np.pi / M * places[:, :, None] * orders).sum(-1) / M
    high, low = split_np(inter)
    fine_cols = np.concatenate([high.T, low.T, high.T, low.T], 0)
    fold_cols = np.concatenate([high, low], 1)
    fine_rows = np.concatenate([high, low, high, low], 1).reshape(blocks, span, 4 * M)
    high_t = high.reshape(blocks, span, M).transpose(0, 2, 1)
    low_t = low.reshape(blocks, span, M).transpose(0, 2, 1)
    fold_rows = np.concatenate([high_t, low_t, high_t], 2)
    high, low = split_np(np.concatenate([rounded_cos, rounded_sin], 0))
    drop_rows = np.concatenate([high, low], 1)
    drop = pair_table(coarse_cos, coarse_sin).T
    drop = np.concatenate([drop, drop[:, M:], -drop[:, :M]], 1)
    high, low = split_np(drop)
    drop_cols = np.concatenate([high, low], 0)
    rows = np.concatenate(
        [
            wide_cos.reshape(W, blocks, span).transpose(1, 2, 0),
            wide_sin.reshape(W, blocks, span).transpose(1, 2, 0),
        ],
        2,
    )
    high, low = split_np(rows / period)
    grad_rows = np.concatenate([high, low, high], 2)
    padded = [np.pad(part, ((0, M - W), (0, 0))) for part in (wide_cos, wide_sin)]
    high, low = split_np(np.concatenate(padded, 0))
    grad_cols = np.concatenate([high, low], 0)
    chapters = [
        dict(lift_cols=lift_cols, lift_rows=lift_rows),
        dict(fine_cols=fine_cols, fold_cols=fold_cols),
        dict(drop_rows=drop_rows, drop_cols=drop_cols),
        dict(grad_cols=grad_cols),
    ]
    for block in range(blocks):
        chapters.append(dict(fine_rows=fine_rows[block], fold_rows=fold_rows[block]))
    for block in range(blocks):
        chapters.append(dict(grad_rows=grad_rows[block]))
    pages, starts, places, at = [], [], {}, 0
    for chapter in chapters:
        starts.append(at)
        for name, value in chapter.items():
            places[name] = (at - starts[-1], value.shape)
            for lane in range(0, value.shape[1], LANES):
                page = value[:, lane : lane + LANES]
                pages.append(np.pad(page, ((0, 0), (0, LANES - page.shape[1]))))
                at += page.shape[0]
    starts.append(at)
    return spec_cols, spec_rows, Book(np.concatenate(pages, 0), starts, places, blocks)


class Book:
    def __init__(self, pages, starts, places, blocks):
        self.pages, self.starts, self.places, self.blocks = pages, starts, places, blocks

    def rows(self, chapter):
        return self.starts[chapter + 1] - self.starts[chapter]

    def shapes(self, *chapters):
        return [jax.ShapeDtypeStruct((self.rows(chapter), LANES), bf16) for chapter in chapters]

    def where(self, ref, chapter, block=0):
        return ref.at[pl.ds(self.starts[chapter] + block * self.rows(chapter), self.rows(chapter))]

    def read(self, ref, name):
        at, (rows, lanes) = self.places[name]
        pages = [
            ref[at + number * rows : at + (number + 1) * rows, : min(LANES, lanes - lane)]
            for number, lane in enumerate(range(0, lanes, LANES))
        ]
        return pages[0] if len(pages) == 1 else jnp.concatenate(pages, 1)


LIFT, FINE, DROP, GRAD, IMAGE_ROWS = range(5)


def dot(left, right):
    return jnp.dot(left, right, preferred_element_type=f32)


def split(value):
    high = value.astype(bf16)
    return high, (value - high.astype(f32)).astype(bf16)


def lane_of(shape):
    return lax.broadcasted_iota(jnp.int32, shape, len(shape) - 1)


def row_of(shape):
    return lax.broadcasted_iota(jnp.int32, shape, 0)


def swap(value):
    return pltpu.roll(value, M, 1)


def signs(rows, low, high):
    return jnp.where(lane_of((rows, LANES)) < M, f32(low), f32(high))


def place_is_static(place):
    return isinstance(place, int)


def my_block():
    return lax.axis_index("src") * lax.axis_size("pix") + lax.axis_index("pix")


def chip_blocks():
    pix, count = lax.axis_index("pix"), lax.axis_size("pix")
    base = lax.axis_index("src") * count
    return [base + jnp.bitwise_xor(pix, step) for step in range(count)]


def copies(sems, *pairs):
    out = [
        pltpu.make_async_copy(source, place, sems.at[number])
        for number, (source, place) in enumerate(pairs)
    ]
    for copy in out:
        copy.start()
    return out


def spectrum_kernel(
    mask_ref, pupil_ref, weight_ref, cell_ref, active_ref, class_ref, thresholds_ref,
    cols_ref, rows_ref,
    part_ref, sent_ref, threshold_ref,
    mask_in, pupil_in, weight_in, cell_in, active_in, thresholds, cols, rows,
    sems, lined, paired,
):
    (
        get_pupil, get_mask, get_cols, get_active, get_cell, get_weight, get_rows,
        get_thresholds,
    ) = copies(
        sems,
        (pupil_ref.at[pl.ds(0, 16)], pupil_in),
        (mask_ref.at[0], mask_in),
        (cols_ref, cols),
        (active_ref, active_in),
        (cell_ref, cell_in),
        (weight_ref, weight_in),
        (rows_ref.at[my_block()], rows),
        (thresholds_ref, thresholds),
    )
    get_active.wait()
    get_cell.wait()
    get_pupil.wait()
    get_weight.wait()
    active = active_in[lax.axis_index("src")]
    raw = pupil_in[...].astype(f32)[:8]
    raw = jnp.where(row_of(raw.shape) < active, raw, 0.0)
    for piece in range(16):
        lined[pl.ds(piece, 8, stride=16), :] = raw[:, piece * LANES : (piece + 1) * LANES]
    quarter = lane_of((8, LANES)) // K
    for pair in range(PAIRS):
        first, second = pair * 32, pair * 32 + 16
        quarters = [lined[pl.ds(start, 8), :] for start in (first, second, first + 8, second + 8)]
        for turn in range(4):
            moved = [
                value if number == turn else pltpu.roll(value, K * (number - turn) % LANES, 1)
                for number, value in enumerate(quarters)
            ]
            out = moved[3]
            for number in range(3):
                out = jnp.where(quarter == number, moved[number], out)
            paired[pl.ds(pair * K + turn, 8, stride=4), :] = out
    sent_ref[: PAIRS * K] = paired[...].astype(bf16)
    shape = (8, LANES)
    weights = jnp.broadcast_to(weight_in[...].astype(f32).reshape(1, -1)[:, :LANES], shape)
    column = jnp.sum(jnp.where(row_of(shape) == lane_of(shape), weights, 0.0), 1, keepdims=True)
    row_code, col_code = jnp.zeros(shape, f32), jnp.zeros(shape, f32)
    for slot in range(MOST):
        cell = cell_in[slot]
        row_code = jnp.where(row_of(shape) == slot, lax.div(cell, SG).astype(f32), row_code)
        col_code = jnp.where(row_of(shape) == slot, lax.rem(cell, SG).astype(f32), col_code)
    facts = [jnp.broadcast_to(column, shape), row_code, col_code, jnp.zeros((W - 24, LANES), f32)]
    sent_ref[PAIRS * K :] = jnp.concatenate(facts, 0).astype(bf16)
    get_mask.wait()
    get_cols.wait()
    get_rows.wait()
    high, low = split(mask_in[...])
    both = dot(high, cols[...])
    part = both[:, :LANES] + both[:, LANES:] + dot(low, cols[:, :LANES])
    turned = swap(part) * signs(part.shape[0], 1.0, -1.0)
    high, low = split(jnp.concatenate([part, turned], 0))
    product = dot(rows[...], jnp.concatenate([high, low], 1))
    part_ref[...] = product[:W, :LANES] + product[:W, LANES:] + product[W:, :LANES]
    get_thresholds.wait()
    kind = class_ref[0]
    threshold = thresholds[0]
    for number in range(1, CLASSES):
        threshold = jnp.where(kind == number, thresholds[number], threshold)
    threshold_ref[...] = jnp.full(threshold_ref.shape, threshold, f32)


def pack_kernel(part_ref, *refs):
    *other_refs, sent_ref, out_ref = refs
    part = part_ref[...]
    for ref in other_refs:
        part = part + ref[...]
    high, low = split(part)
    rest = pltpu.roll(low.astype(f32), K, 1)
    lane = lane_of(part.shape)
    mixed = jnp.where(lane % M < W, high.astype(f32), rest)
    facts = sent_ref[PAIRS * K :].astype(f32)
    out_ref[:W] = jnp.where(lane == FACTS, facts, mixed).astype(bf16)
    out_ref[AT_PUPILS:] = sent_ref[: PAIRS * K]


def stage_kernel(book, target_ref, book_ref, *refs):
    *out_refs, sems = refs
    target_out, lift_out, fine_out, drop_out, grad_out, grad_rows_out, *rows_out = out_refs
    gets = copies(
        sems,
        (book.where(book_ref, LIFT), lift_out),
        (book.where(book_ref, FINE), fine_out),
        (target_ref.at[0], target_out),
        *(
            (book.where(book_ref, IMAGE_ROWS, block), out)
            for block, out in zip(chip_blocks(), rows_out)
        ),
        (book.where(book_ref, DROP), drop_out),
        (book.where(book_ref, GRAD), grad_out),
        (book.where(book_ref, IMAGE_ROWS + book.blocks, my_block()), grad_rows_out),
    )
    for get in gets:
        get.wait()


def over_owners(refs, body, carry):
    if len(refs) > 1:
        return body(carry, [(ref, place) for place, ref in enumerate(refs)])
    (ref,) = refs
    return lax.fori_loop(
        0, ref.shape[0], lambda owner, carry: body(carry, [(ref.at[owner], owner)]), carry
    )


def codes_of(refs, codes_v):
    def body(none, items):
        for ref, place in items:
            facts = ref[:W].astype(f32)[:, FACTS : FACTS + 1]
            shape = (8, LANES)
            code = jnp.broadcast_to(facts[8:16] * 32.0 + facts[16:24], shape)
            code = jnp.sum(jnp.where(row_of(shape) == lane_of(shape), code, 0.0), 0, keepdims=True)
            codes_v[pl.ds(place, 1), :] = code.astype(jnp.int32)
        return none

    over_owners(refs, body, 0)


def weights_of(ref):
    return jnp.broadcast_to(ref[:16].astype(f32)[:8, FACTS : FACTS + 1], (8, LANES))


def window_of(codes, place, slot):
    code = codes[place, slot]
    return lax.div(code, 32), lax.rem(code, 32)


def pair_parts(ref, pair):
    value = ref[pl.ds(AT_PUPILS + pair * K, K), :].astype(f32)
    other = swap(value)
    low = lane_of(value.shape) < M
    return jnp.where(low, value, other), jnp.where(low, other, value)


def slot_lanes(rows):
    return lane_of((rows, LANES)) // K % 2 == 0


def image_kernel(book, n_sent, n_pix, *refs):
    sent_refs, refs = refs[:n_sent], refs[n_sent:]
    targets, refs = refs[:n_pix], refs[n_pix:]
    rows_refs, refs = refs[:n_pix], refs[n_pix:]
    (
        threshold_ref, lift, fine,
        intensity_ref, fields, *fold_refs,
        sems, codes_v, codes, spectrum, intensity_out,
    ) = refs
    codes_of(sent_refs, codes_v)
    (get_codes,) = copies(sems, (codes_v, codes))

    def gather(total, items):
        for ref, place in items:
            value = ref[:W].astype(f32)
            lane = lane_of(value.shape)
            rest = jnp.where((lane % M < W) | (lane == FACTS), 0.0, value)
            total = total + (value + pltpu.roll(rest, LANES - K, 1))
        return total

    spectrum[...] = over_owners(sent_refs, gather, jnp.zeros((W, LANES), f32))
    if len(sent_refs) == 1:
        get_codes.wait()
    lift_cols, lift_rows = book.read(lift, "lift_cols"), book.read(lift, "lift_rows")
    even = slot_lanes(K)
    turn_low = signs(K, -1.0, 1.0)

    def forward(total, items):
        waves = []
        parts = [pair_parts(ref, pair) for ref, place in items for pair in range(PAIRS)]
        if len(items) > 1:
            get_codes.wait()
        for ref, place in items:
            for pair in range(PAIRS):
                real, imag = parts.pop(0)
                row, col = window_of(codes, place, 2 * pair)
                left = pltpu.roll(spectrum[pl.ds(row, K), :], lax.rem(LANES - col, LANES), 1)
                row, col = window_of(codes, place, 2 * pair + 1)
                right = pltpu.roll(spectrum[pl.ds(row, K), :], lax.rem(LANES + K - col, LANES), 1)
                window = jnp.where(even, left, right)
                waves.append((real * window + imag * (turn_low * swap(window))).astype(bf16))
        wave = jnp.concatenate(waves, 0)
        wave = dot(jnp.concatenate([wave, wave], 1), lift_cols).astype(bf16)
        number = 0
        for ref, place in items:
            weights = weights_of(ref)
            for pair in range(PAIRS):
                here = slice(number * K, (number + 1) * K)
                number += 1
                own, turned = wave[here, : 2 * LANES], wave[here, 2 * LANES :]
                raw = dot(lift_rows, jnp.concatenate([own, own, turned, turned], 0))
                for slot in range(2):
                    field = raw[:, slot * LANES : (slot + 1) * LANES]
                    fields[place * MOST + 2 * pair + slot] = field
                    at = 2 * pair + slot
                    total = total + weights[at : at + 1] * (field * field)
        return total

    power = over_owners(sent_refs, forward, jnp.zeros((M, LANES), f32))
    high, low = split(power + swap(power))
    coarse = jnp.concatenate([high, high, low, low], 0)
    fine_cols, fold_cols = book.read(fine, "fine_cols"), book.read(fine, "fold_cols")
    threshold = threshold_ref[:1, :1]
    grid = jnp.zeros((M, LANES), f32)
    fine_rows = [book.read(rows_ref, "fine_rows") for rows_ref in rows_refs]
    high, low = split(dot(jnp.concatenate(fine_rows, 0), coarse))
    intensities = dot(jnp.concatenate([high, low], 1), fine_cols)
    span = intensity_out.shape[0]
    intensity_out[...] = intensities[:span]
    put = pltpu.make_async_copy(intensity_out, intensity_ref.at[0], sems.at[1])
    put.start()
    slopes = []
    for number, target in enumerate(targets):
        intensity = intensities[number * span : (number + 1) * span]
        bend = jnp.tanh((0.5 * STEEP) * (intensity - threshold))
        slope = (0.5 * STEEP) * (0.5 * bend + (0.5 - target[...])) * (1.0 - bend * bend)
        slopes.append(slope.astype(bf16))
    folded = dot(jnp.concatenate(slopes, 0), fold_cols)
    high, low = split(folded + swap(folded))
    for number, rows_ref in enumerate(rows_refs):
        here = slice(number * span, (number + 1) * span)
        grid = grid + dot(
            book.read(rows_ref, "fold_rows"),
            jnp.concatenate([high[here], high[here], low[here]], 0),
        )
    lane = lane_of((M // 2, LANES))
    packed = jnp.where(lane < M, grid[: M // 2], grid[M // 2 :])
    for fold_ref in fold_refs:
        fold_ref[: M // 2] = packed.astype(fold_ref.dtype)

    def weigh(none, items):
        for ref, place in items:
            sums = []
            for slot in range(MOST):
                field = fields[place * MOST + slot]
                sums.append(jnp.sum(grid * (field * field), 0, keepdims=True))
            sums = jnp.concatenate(sums + [jnp.zeros((SUMS - MOST, LANES), f32)], 0)
            if place_is_static(place) and place > 0:
                high, low = split(sums)
                fold_refs[place][M // 2 :] = jnp.concatenate([high, low], 0)
            elif len(fold_refs) > 1:
                fold_refs[place][M // 2 :] = sums
            else:
                start = pl.multiple_of(M // 2 + place * SUMS, SUMS)
                fold_refs[0][pl.ds(start, SUMS), :] = sums
        return none

    over_owners(sent_refs, weigh, 0)
    put.wait()


def gradient_kernel(book, n_fold, n_sent, *refs):
    fold_refs, refs = refs[:n_fold], refs[n_fold:]
    sent_refs, refs = refs[:n_sent], refs[n_sent:]
    (
        fields, drop, grad_table, rows_table,
        mask_grad_ref,
        sems, codes_v, codes, sums, mask_grad_out,
    ) = refs
    codes_of(sent_refs, codes_v)
    (get_codes,) = copies(sems, (codes_v, codes))
    packed = fold_refs[0][: M // 2]
    for ref in fold_refs[1:]:
        packed = packed + ref[: M // 2].astype(f32)
    other = swap(packed)
    low_half = lane_of(packed.shape) < M
    grid = jnp.concatenate(
        [jnp.where(low_half, packed, other), jnp.where(low_half, other, packed)], 0
    )
    for number in range(MOST):
        sums[number] = jnp.zeros((W, LANES), f32)
    turn = signs(K, 1.0, -1.0)
    even = slot_lanes(K)
    real_or_imag = lane_of((K, LANES)) % M < K
    get_codes.wait()
    drop_rows, drop_cols = book.read(drop, "drop_rows"), book.read(drop, "drop_cols")

    def backward(none, items):
        waves = []
        for ref, place in items:
            for pair in range(PAIRS):
                scaled = [grid * fields[place * MOST + 2 * pair + slot] for slot in range(2)]
                pull = jnp.concatenate(scaled, 1).astype(bf16)
                raw = dot(drop_rows, jnp.concatenate([pull, pull], 0))
                wave = []
                for slot in range(2):
                    mine = raw[:, slot * LANES : (slot + 1) * LANES]
                    wave.append(mine[:K] + turn * swap(mine[K:]))
                waves.append(jnp.concatenate(wave, 1))
        wave = jnp.concatenate(waves, 0).astype(bf16)
        back = dot(jnp.concatenate([wave, wave], 1), drop_cols)
        number = 0
        for ref, place in items:
            weights = weights_of(ref) * (2.0 / K)
            for pair in range(PAIRS):
                mine = back[number * K : (number + 1) * K]
                number += 1
                real, imag = pair_parts(ref, pair)
                product = real * mine[:, :LANES] + imag * mine[:, LANES:]
                first, second = weights[2 * pair : 2 * pair + 1], weights[2 * pair + 1 : 2 * pair + 2]
                product = jnp.where(even[:1], first, second) * product
                for slot in range(2):
                    row, col = window_of(codes, place, 2 * pair + slot)
                    keep = even if slot == 0 else jnp.logical_not(even)
                    shift = lax.rem(col + LANES - slot * K, LANES)
                    moved = pltpu.roll(jnp.where(keep, product, 0.0), shift, 1)
                    sums[2 * pair + slot, pl.ds(row, K), :] += moved
        return none

    over_owners(sent_refs, backward, 0)
    grad_cols = book.read(grad_table, "grad_cols")
    grad = sum(sums[number] for number in range(1, MOST)) + sums[0]
    turn = signs(W, 1.0, -1.0)
    high, low = split(jnp.concatenate([grad * turn, -swap(grad)], 0))
    half = dot(book.read(rows_table, "grad_rows"), jnp.concatenate([high, high, low], 0))
    half = half.astype(bf16)
    both = jnp.concatenate([half, half], 1)
    chunk = grad_cols.shape[1] // PIECES
    puts = []
    for piece in range(PIECES):
        here = slice(piece * chunk, (piece + 1) * chunk)
        mask_grad_out[:, here] = dot(both, grad_cols[:, here])
        place = mask_grad_ref.at[0, :, pl.ds(piece * chunk, chunk)]
        puts.append(
            pltpu.make_async_copy(mask_grad_out.at[:, pl.ds(piece * chunk, chunk)], place, sems.at[1 + piece])
        )
        puts[-1].start()
    for put in puts:
        put.wait()


VMEM = pl.BlockSpec(memory_space=pltpu.VMEM)
SMEM = pl.BlockSpec(memory_space=pltpu.SMEM)
HBM = pl.BlockSpec(memory_space=pltpu.HBM)


def room(kib):
    return pltpu.CompilerParams(vmem_limit_bytes=(64 * 1024 - kib) * 1024)


def in_hbm(value):
    return pltpu.with_memory_space_constraint(value, pltpu.HBM)


def exchange(value, axis, step):
    return lax.ppermute(value, axis, [(i, i ^ step) for i in range(lax.axis_size(axis))])


def others(value, axis):
    return [exchange(value, axis, step) for step in range(1, lax.axis_size(axis))]


def like(value):
    return pltpu.VMEM(value.shape, value.dtype)


def shards(
    mask, target, tile_class, thresholds, source_pupil, source_weight, source_cell, active_count
):
    span, period = mask.shape[1:]
    slots = source_pupil.shape[0]
    src_count = lax.axis_size("src")
    few = src_count in (2, 4)
    spec_cols, spec_rows, book = tables(period, span)
    pages = jnp.asarray(book.pages)
    src = lax.axis_index("src")
    sems = pltpu.SemaphoreType.DMA
    smem = pltpu.SMEM

    part, sent, threshold = pl.pallas_call(
        spectrum_kernel,
        in_specs=[HBM] * 5 + [SMEM] + [HBM] * 3,
        out_specs=[VMEM] * 3,
        out_shape=[
            jax.ShapeDtypeStruct((W, LANES), f32),
            jax.ShapeDtypeStruct((PAIRS * K + W, LANES), bf16),
            jax.ShapeDtypeStruct((8, LANES), f32),
        ],
        scratch_shapes=[
            like(mask[0]),
            like(source_pupil[:16]),
            like(source_weight),
            smem(source_cell.shape, jnp.int32),
            smem(active_count.shape, jnp.int32),
            smem(thresholds.shape, f32),
            like(spec_cols),
            like(spec_rows[0]),
            sems((8,)),
            pltpu.VMEM((LANES, LANES), f32),
            pltpu.VMEM((PAIRS * K, LANES), f32),
        ],
        compiler_params=room(24576),
        name="spectrum",
    )(
        *map(in_hbm, (mask, source_pupil, source_weight, source_cell, active_count)),
        tile_class,
        *map(in_hbm, (thresholds, jnp.asarray(spec_cols), jnp.asarray(spec_rows))),
    )
    from_pix = others(part, "pix")
    sent = pl.pallas_call(
        pack_kernel,
        in_specs=[VMEM] * (2 + len(from_pix)),
        out_specs=VMEM,
        out_shape=jax.ShapeDtypeStruct((ROWS, LANES), bf16),
        compiler_params=room(32768),
        name="pack",
    )(part, *from_pix, sent)
    if few:
        parcels = [sent] + others(sent, "src")
    else:
        parcels = [lax.all_gather(sent, "src")]

    late_target, late_pages, _ = lax.optimization_barrier((target, pages, sent))
    staged_shapes = [
        jax.ShapeDtypeStruct((span, period), f32),
        *book.shapes(LIFT, FINE, DROP, GRAD, IMAGE_ROWS + book.blocks),
        *book.shapes(IMAGE_ROWS) * lax.axis_size("pix"),
    ]
    staged = pl.pallas_call(
        functools.partial(stage_kernel, book),
        in_specs=[HBM] * 2,
        out_specs=[VMEM] * len(staged_shapes),
        out_shape=staged_shapes,
        scratch_shapes=[sems((len(staged_shapes),))],
        compiler_params=room(24576),
        name="stage",
    )(in_hbm(late_target), in_hbm(late_pages))
    near_target, lift, fine, *for_gradient = staged[:6]
    early_target, _ = lax.optimization_barrier((target, from_pix[0]))
    targets = [near_target] + others(early_target[0], "pix")
    image_rows = staged[6:]

    numbers = src_count * MOST
    owners_up = -(-src_count // 8) * 8
    fold_rows = M // 2 + (1 if few else src_count) * SUMS
    fold_count = src_count if few else 1
    codes = [pltpu.VMEM((owners_up, LANES), jnp.int32), smem((owners_up, LANES), jnp.int32)]
    intensity, fields, *folded = pl.pallas_call(
        functools.partial(image_kernel, book, len(parcels), len(targets)),
        in_specs=[VMEM] * (len(parcels) + 2 * len(targets) + 3),
        out_specs=[HBM, VMEM] + [VMEM] * fold_count,
        out_shape=[
            jax.ShapeDtypeStruct((1, span, period), f32),
            jax.ShapeDtypeStruct((numbers, M, LANES), f32),
            jax.ShapeDtypeStruct((fold_rows, LANES), f32),
            *[jax.ShapeDtypeStruct((M // 2 + 2 * SUMS, LANES), bf16)] * (fold_count - 1),
        ],
        scratch_shapes=[
            sems((2,)),
            *codes,
            pltpu.VMEM((W, LANES), f32),
            like(target[0]),
        ],
        compiler_params=room(24576),
        name="image",
    )(*parcels, *targets, *image_rows, threshold, lift, fine)

    if few:
        folds = [
            value if step == 0 else exchange(value, "src", step)
            for step, value in enumerate(folded)
        ]
        rows = folds[0][M // 2 :]
        for fold in folds[1:]:
            sums = fold[M // 2 :].astype(f32)
            rows = rows + (sums[:SUMS] + sums[SUMS:])
    else:
        folds = [lax.psum(folded[0], "src")]
        rows = lax.dynamic_slice_in_dim(folds[0], M // 2 + src * SUMS, SUMS, 0)
    for other in others(rows, "tile"):
        rows = rows + other
    mask_grad = pl.pallas_call(
        functools.partial(gradient_kernel, book, len(folds), len(parcels)),
        in_specs=[VMEM] * (len(folds) + len(parcels) + 1 + len(for_gradient)),
        out_specs=HBM,
        out_shape=jax.ShapeDtypeStruct((1, span, period), f32),
        scratch_shapes=[
            sems((1 + PIECES,)),
            *codes,
            pltpu.VMEM((MOST, W, LANES), f32),
            like(mask[0]),
        ],
        compiler_params=room(24576),
        name="gradient",
    )(*folds, *parcels, fields, *for_gradient)
    sums = jnp.sum(rows, 1) * (1.0 / (period * K))
    source_grad = jnp.zeros((slots,), f32).at[:SUMS].set(sums)
    return intensity, mask_grad, source_grad


def solution(mesh):
    in_specs = (
        P(("groups", "tile"), ("src", "pix"), None),
        P(("groups", "tile"), ("src", "pix"), None),
        P(("groups", "tile")),
        P(),
        P("src", None),
        P("src"),
        P("src"),
        P(),
    )
    out_specs = (
        P(("groups", "tile"), ("src", "pix"), None),
        P(("groups", "tile"), ("src", "pix"), None),
        P(("groups", "src")),
    )
    return jax.shard_map(shards, mesh=mesh, in_specs=in_specs, out_specs=out_specs, check_vma=False)
```
